32 devices in a mesh: group: 4 (over y, x), shard: 8 (over z, core).
Axes of the slice: x: 2, y: 2, z: 4, core: 2. Of those that a mesh axis runs over, the one named last changes fastest.
Arguments:
- step_count: int32 [1], replicated, may hold values from 2 to 8
- block_order: int32 [224], replicated, may hold values from 0 to 223, as said below
- saved_tiles: bfloat16 [32, 4, 18, 18, 256], P(('group', 'shard')), may hold values from -6 to 6
- pre_act: bfloat16 [16384, 256], P(('group', 'shard')), may hold values from -6 to 6
- grad_output: bfloat16 [16384, 256], P(('group', 'shard')), may hold values from -0.09375 to 0.09375
- pointwise_live: bfloat16 [256, 256], replicated, may hold values from -0.375 to 0.375
- master_rows: float32 [7168, 256], P('shard'), may hold values from -0.25 to 0.25, as said below
- row_moment: float32 [7168], P('shard'), may hold values from 0.5 to 30, as said below
- col_moment: float32 [2, 256], replicated, may hold values from 0.03 to 0.3
- next_tiles: bfloat16 [32, 4, 18, 18, 256], P(('group', 'shard')), may hold values from -6 to 6
Outputs:
- update_rows: float32 [7168, 256], P('shard')
- new_master: float32 [7168, 256], P('shard')
- new_row_moment: float32 [7168], P('shard')
- new_col_moment: float32 [2, 256], replicated
- next_output: bfloat16 [16384, 256], P(('group', 'shard'))
The draws below stay inside these ranges and needn't reach their ends.
Inputs may be any that keep to these rules, and one draw needn't show every extreme that they name: `block_order`: a permutation of 0 to 223. `master_rows`: rows of the 3x3x3 kernel are of order (6912) ** -0.5 and rows of the 1x1x1 kernel of order 256 ** -0.5. `row_moment`: positive row factors.
All inputs are finite; a program needn't handle non-finite values.
Results may differ from the reference program's by a relative error of at most 0.023.
Values may be sent and summed in bfloat16 or wider, within the bound.
No kernel may reach another device: no remote copies, remote signals or barrier semaphores. Data moves between devices by JAX's collectives and lax.ppermute only.
A program may use at most 64 MiB of HBM per device.

```python
import math
import jax
import jax.numpy as jnp
from jax import lax

CI = 256
CO = 256
BLK = 32
FR = 2
HW = 16
NB3 = 216
NB = 224
ROWS_DEV = 512
N_GROUP = 4
N_SHARD = 8


def block_permutation(key):
    return jax.random.permutation(jax.random.fold_in(key, 17), NB).astype(jnp.int32)


def draw_block_order(key, part):
    return block_permutation(key)


def draw_master_rows(key, part):
    order = block_permutation(key)
    is_small = jnp.repeat(order >= NB3, BLK, total_repeat_length=NB * BLK)
    scale = jnp.where(is_small, CO ** (-0.5), (27 * CI) ** (-0.5)).astype(jnp.float32)
    noise_key = jax.random.fold_in(key, 29)
    values = jax.random.truncated_normal(noise_key, -4.0, 4.0, (NB * BLK, CO), jnp.float32)
    return values * scale[:, None]


def draw_row_moment(key, part):
    position = jnp.arange(NB * BLK, dtype=jnp.float32) / (NB * BLK - 1)
    jitter = jax.random.uniform(jax.random.fold_in(key, 41), (NB * BLK,), jnp.float32, -0.7, 0.0)
    spread = 2.3
    return (30.0 * jnp.exp(jitter - spread * position)).astype(jnp.float32)


def steps_of(key, extent, shards, least, high):
    loudness, own = 1.0, jax.random.fold_in(key, 6)
    for axis_at, shards_of in shards:
        draws = jnp.exp(jax.random.uniform(jax.random.fold_in(own, axis_at), (shards_of,), jnp.float32, least / len(shards), high / len(shards)))
        loudness = loudness * jnp.repeat(draws, extent[axis_at] // shards_of).reshape([-1 if axis == axis_at else 1 for axis in range(len(extent))])
    return loudness


def noise(stream_key, shape, scale, limit, cuts=(), kind=jnp.bfloat16):
    drawn = jax.random.normal(stream_key, shape, jnp.float32) * scale
    if len(cuts) > 0:
        drawn = steps_of(stream_key, shape, cuts, -0.22, 0.18) * drawn
    return jnp.clip(drawn, min=-limit, max=limit).astype(kind)


def setup_inputs(seed: int = 0) -> dict:
    arg_keys = jax.random.split(jax.random.key(seed), 11)
    return {
        "step_count": jax.random.randint(arg_keys[0], (1,), 2, 9).astype(jnp.int32),
        "block_order": draw_block_order(jax.random.fold_in(arg_keys[10], 71), 0),
        "saved_tiles": noise(arg_keys[2], (N_GROUP * N_SHARD, FR + 2, HW + 2, HW + 2, CI), 1.0, 6.0, ((0, 32),)),
        "pre_act": noise(arg_keys[3], (N_GROUP * N_SHARD * ROWS_DEV, CO), 1.0, 6.0, ((0, 32),)),
        "grad_output": noise(arg_keys[4], (N_GROUP * N_SHARD * ROWS_DEV, CO), (2.0 * (N_GROUP * N_SHARD * ROWS_DEV) ** -0.5), 0.09375, ((0, 32),)),
        "pointwise_live": noise(arg_keys[5], (CO, CO), CO ** -0.5, 0.375),
        "master_rows": draw_master_rows(jax.random.fold_in(arg_keys[10], 71), 0),
        "row_moment": draw_row_moment(jax.random.fold_in(arg_keys[10], 71), 0),
        "col_moment": jnp.clip(jnp.exp(jax.random.uniform(arg_keys[8], (2, CO), jnp.float32, math.log(0.03), math.log(0.3))), 0.03, 0.3),
        "next_tiles": noise(arg_keys[9], (N_GROUP * N_SHARD, FR + 2, HW + 2, HW + 2, CI), 1.0, 6.0, ((0, 32),)),
    }


learn_rate = 0.002
decay_power = 0.8

def silu_slope(values):
    sigma = jax.nn.sigmoid(values)
    return sigma * (1.0 + values * (1.0 - sigma))

def tap_views(frames):
    views = []
    for frame_off in range(3):
        for row_off in range(3):
            for col_off in range(3):
                window = frames[frame_off:frame_off + FR, row_off:row_off + HW, col_off:col_off + HW, :]
                views.append(window.reshape(FR * HW * HW, CI))
    return views

def contract_rows(left, right):
    return lax.dot_general(left, right, (((0,), (0,)), ((), ())), preferred_element_type=jnp.float32)

def kernel_sums(values, is_small):
    large_part = lax.optimization_barrier(jnp.sum(jnp.where(is_small[:, None], 0.0, values), axis=0))
    small_part = lax.optimization_barrier(jnp.sum(jnp.where(is_small[:, None], values, 0.0), axis=0))
    return jnp.stack([large_part, small_part])

def device_term(frames, pre_rows, grad_rows, pointwise_live):
    pre_float = pre_rows.astype(jnp.float32)
    activation = jax.nn.silu(pre_float).astype(jnp.bfloat16)
    grad_act = lax.dot_general(grad_rows, pointwise_live, (((1,), (1,)), ((), ())), preferred_element_type=jnp.float32)
    grad_pre = (grad_act * silu_slope(pre_float)).astype(jnp.bfloat16)
    pieces = [contract_rows(view, grad_pre) for view in tap_views(frames)]
    pieces.append(contract_rows(activation, grad_rows))
    return jnp.concatenate(pieces, axis=0).astype(jnp.bfloat16)

def forward_tile(frames, spatial, pointwise):
    hidden_sum = jnp.zeros((FR * HW * HW, CO), jnp.float32)
    for index_tap, view in enumerate(tap_views(frames)):
        hidden_sum = hidden_sum + jnp.dot(view, spatial[index_tap], preferred_element_type=jnp.float32)
    hidden_act = jax.nn.silu(hidden_sum).astype(jnp.bfloat16)
    return jnp.dot(hidden_act, pointwise, preferred_element_type=jnp.float32).astype(jnp.bfloat16)

def reference(step_count, block_order, saved_tiles, pre_act, grad_output, pointwise_live, master_rows, row_moment, col_moment, next_tiles):
    device_count = N_GROUP * N_SHARD
    total_rows = NB * BLK
    pre_all = pre_act.reshape(device_count, FR * HW * HW, CO)
    grad_all = grad_output.reshape(device_count, FR * HW * HW, CO)

    def accumulate(total, inputs):
        frames, pre_rows, grad_rows = inputs
        term = device_term(frames, pre_rows, grad_rows, pointwise_live)
        return (total + term.astype(jnp.float32), None)
    natural_grad, unused = lax.scan(accumulate, jnp.zeros((total_rows, CO), jnp.float32), (saved_tiles, pre_all, grad_all))
    gradient = jnp.take(natural_grad.reshape(NB, BLK, CO), block_order, axis=0).reshape(total_rows, CO)
    is_small = jnp.repeat(block_order >= NB3, BLK, total_repeat_length=total_rows)
    decay_rate = 1.0 - step_count.astype(jnp.float32)[0] ** (-decay_power)
    counts = jnp.array([27 * CI, CO], jnp.float32)
    squares = gradient * gradient
    new_row = decay_rate * row_moment + (1.0 - decay_rate) * lax.optimization_barrier(jnp.mean(squares, axis=1))
    col_total = kernel_sums(squares, is_small)
    new_col = decay_rate * col_moment + (1.0 - decay_rate) * col_total / counts[:, None]
    row_mean = kernel_sums(new_row[:, None], is_small)[:, 0] / counts
    col_rows = jnp.where(is_small[:, None], new_col[1], new_col[0])
    mean_rows = jnp.where(is_small, row_mean[1], row_mean[0])
    scaled = gradient / jnp.sqrt(new_row[:, None] * col_rows / mean_rows[:, None])
    square_total = kernel_sums(lax.optimization_barrier(jnp.sum(scaled * scaled, axis=1))[:, None], is_small)[:, 0]
    clip_factor = jnp.maximum(1.0, jnp.sqrt(square_total / (counts * CO)))
    update_rows = scaled / jnp.where(is_small, clip_factor[1], clip_factor[0])[:, None]
    new_master = master_rows - learn_rate * update_rows
    weights_low = new_master.astype(jnp.bfloat16)
    inverse = jnp.zeros((NB,), jnp.int32).at[block_order].set(jnp.arange(NB, dtype=jnp.int32))
    natural = jnp.take(weights_low.reshape(NB, BLK, CO), inverse, axis=0).reshape(total_rows, CO)
    spatial = natural[:27 * CI].reshape(27, CI, CO)
    pointwise = natural[27 * CI:]

    def forward_one(frames):
        return forward_tile(frames, spatial, pointwise)
    next_output = lax.map(forward_one, next_tiles).reshape(device_count * FR * HW * HW, CO)
    return (update_rows, new_master, new_row, new_col, next_output)
```

```python
import functools
import jax
import jax.numpy as jnp
from jax import lax
from jax.experimental import pallas as pl
from jax.experimental.pallas import tpu as pltpu
from jax.sharding import PartitionSpec as P

CI = 256
CO = 256
BLK = 32
FR = 2
HW = 16
NB3 = 216
NB = 224


learn_rate = 0.002
decay_power = 0.8


def silu_slope(values):
    sigma = jax.nn.sigmoid(values)
    return sigma * (1.0 + values * (1.0 - sigma))


def tap_views(frames):
    views = []
    for frame_off in range(3):
        for row_off in range(3):
            for col_off in range(3):
                window = frames[
                    frame_off : frame_off + FR, row_off : row_off + HW, col_off : col_off + HW, :
                ]
                views.append(window.reshape(FR * HW * HW, CI))
    return views


def contract_rows(left, right):
    return lax.dot_general(
        left, right, (((0,), (0,)), ((), ())), preferred_element_type=jnp.float32
    )


def kernel_sums(values, is_small):
    large_part = jnp.sum(jnp.where(is_small[:, None], 0.0, values), axis=0)
    small_part = jnp.sum(jnp.where(is_small[:, None], values, 0.0), axis=0)
    return jnp.stack([large_part, small_part])


def general_shards(
    step_count,
    block_order,
    saved_tiles,
    pre_act,
    grad_output,
    pointwise_live,
    master_rows,
    row_moment,
    col_moment,
    next_tiles,
):
    pre_float = pre_act.astype(jnp.float32)
    activation = jax.nn.silu(pre_float).astype(jnp.bfloat16)
    grad_act = lax.dot_general(
        grad_output, pointwise_live, (((1,), (1,)), ((), ())), preferred_element_type=jnp.float32
    )
    grad_pre = (grad_act * silu_slope(pre_float)).astype(jnp.bfloat16)
    pieces = [contract_rows(view, grad_pre) for view in tap_views(saved_tiles[0])]
    pieces.append(contract_rows(activation, grad_output))
    own_term = jnp.concatenate(pieces, axis=0).astype(jnp.bfloat16)
    total_rows = NB * BLK
    stored = jnp.take(own_term.reshape(NB, BLK, CO), block_order, axis=0).reshape(total_rows, CO)
    own_rows = master_rows.shape[0]
    partial_value = lax.psum_scatter(stored, "shard", scatter_dimension=0, tiled=True).astype(
        jnp.float32
    )
    gradient = lax.psum(partial_value, "group")
    owner = lax.axis_index("shard")
    own_count = own_rows // BLK
    own_blocks = lax.dynamic_slice_in_dim(block_order, owner * own_count, own_count)
    is_small = jnp.repeat(own_blocks >= NB3, BLK, total_repeat_length=own_rows)
    decay_rate = 1.0 - step_count.astype(jnp.float32)[0] ** (-decay_power)
    counts = jnp.array([27 * CI, CO], jnp.float32)
    squares = gradient * gradient
    new_row = decay_rate * row_moment + (1.0 - decay_rate) * jnp.mean(squares, axis=1)
    col_part = kernel_sums(squares, is_small)
    row_part = kernel_sums(new_row[:, None], is_small)[:, 0]
    weighted = kernel_sums(squares / new_row[:, None], is_small)
    col_total, weight_total, row_total = lax.psum((col_part, weighted, row_part), "shard")
    new_col = decay_rate * col_moment + (1.0 - decay_rate) * col_total / counts[:, None]
    row_mean = row_total / counts
    col_rows = jnp.where(is_small[:, None], new_col[1], new_col[0])
    mean_rows = jnp.where(is_small, row_mean[1], row_mean[0])
    scaled = gradient / jnp.sqrt(new_row[:, None] * col_rows / mean_rows[:, None])
    square_total = row_mean * jnp.sum(weight_total / new_col, axis=1)
    clip_factor = jnp.maximum(1.0, jnp.sqrt(square_total / (counts * CO)))
    update_rows = scaled / jnp.where(is_small, clip_factor[1], clip_factor[0])[:, None]
    new_master = master_rows - learn_rate * update_rows
    weights_low = new_master.astype(jnp.bfloat16)
    gathered = lax.all_gather(weights_low, "shard", axis=0, tiled=True)
    inverse = jnp.zeros((NB,), jnp.int32).at[block_order].set(jnp.arange(NB, dtype=jnp.int32))
    natural = jnp.take(gathered.reshape(NB, BLK, CO), inverse, axis=0).reshape(total_rows, CO)
    spatial = natural[: 27 * CI].reshape(27, CI, CO)
    pointwise = natural[27 * CI :]
    hidden_sum = jnp.zeros((FR * HW * HW, CO), jnp.float32)
    for index_tap, view in enumerate(tap_views(next_tiles[0])):
        hidden_sum = hidden_sum + jnp.dot(
            view, spatial[index_tap], preferred_element_type=jnp.float32
        )
    hidden_act = jax.nn.silu(hidden_sum).astype(jnp.bfloat16)
    next_output = jnp.dot(hidden_act, pointwise, preferred_element_type=jnp.float32).astype(
        jnp.bfloat16
    )
    return (update_rows, new_master, new_row, new_col, next_output)


AXES = ("group", "shard")
SLOTS = 14
HALF = 7
PIX = FR * HW * HW
SHIFTED = (FR + 2) * (HW + 2) * HW
LOW = jnp.bfloat16
WIDE = jnp.float32
VMEM = pl.BlockSpec(memory_space=pltpu.VMEM)
SMEM = pl.BlockSpec(memory_space=pltpu.SMEM)
HBM = pl.BlockSpec(memory_space=pl.ANY)
MASK_CORE, MASK_X, MASK_Y = 1, 8, 16


def swap(value, mask):
    return lax.ppermute(value, AXES, [(at, at ^ mask) for at in range(32)])


def call(kernel, outs, in_specs, out_specs=None, scratch=(), flops=0, moved=0):
    return pl.pallas_call(
        kernel,
        out_shape=[jax.ShapeDtypeStruct(shape, dtype) for shape, dtype in outs],
        in_specs=in_specs,
        out_specs=[VMEM] * len(outs) if out_specs is None else out_specs,
        scratch_shapes=list(scratch),
        compiler_params=pltpu.CompilerParams(vmem_limit_bytes=44 << 20),
        cost_estimate=pl.CostEstimate(flops=flops, bytes_accessed=moved, transcendentals=0),
    )


def store_shifted(tile, out):
    for col_off in range(3):
        out[col_off] = tile[:, :, col_off : col_off + HW, :].reshape(SHIFTED, CI)


def shift_kernel(tile, out):
    store_shifted(tile, out)


def slope_of(pre, grad, pointwise):
    grad_act = lax.dot_general(
        grad, pointwise, (((1,), (1,)), ((), ())), preferred_element_type=WIDE
    )
    return (grad_act * silu_slope(pre.astype(WIDE))).astype(LOW)


def term_kernel(
    at, tile, tile_peer, pre, pre_peer, grad, grad_peer, pointwise,
    keep_a, send_a, keep_b, send_b, views, slopes, acts, grads, staged,
):
    axis_x, axis_y, core = at[0], at[1], at[3]
    store_shifted(tile, views.at[0])
    store_shifted(tile_peer, views.at[1])
    slopes[:PIX] = slope_of(pre[...], grad[...], pointwise[...])
    slopes[PIX:] = slope_of(pre_peer[...], grad_peer[...], pointwise[...])

    def put(slot, total):
        value = total.astype(LOW)
        if slot < HALF:
            for mine in range(2):

                @pl.when(axis_x == mine)
                def _():
                    keep_a[slot] = value[mine * 128 : mine * 128 + 128]
                    send_a[slot] = value[128 - mine * 128 : 256 - mine * 128]
        else:
            for mine in range(2):

                @pl.when(axis_y == mine)
                def _():
                    for half in range(2):
                        base, other = half * 128 + mine * 64, half * 128 + 64 - mine * 64
                        to = slice(half * 64, half * 64 + 64)
                        keep_b[slot - HALF, to] = value[base : base + 64]
                        send_b[slot - HALF, to] = value[other : other + 64]

    def tap_rows(tap):
        frame_off, row_off, col_off = tap // 9, lax.rem(tap // 3, 3), lax.rem(tap, 3)
        parts = []
        for peer in range(2):
            for frame in range(FR):
                start = pl.multiple_of(((frame + frame_off) * (HW + 2) + row_off) * HW, HW)
                parts.append(views[peer, col_off, pl.ds(start, HW * HW), :])
        return jnp.concatenate(parts, axis=0)

    for slot in range(SLOTS - 1):
        put(slot, contract_rows(tap_rows(core * SLOTS + slot), slopes[...]))

    @pl.when(core == 0)
    def _():
        staged[...] = contract_rows(tap_rows(SLOTS - 1), slopes[...])

    @pl.when(core == 1)
    def _():
        acts[:PIX] = jax.nn.silu(pre[...].astype(WIDE)).astype(LOW)
        acts[PIX:] = jax.nn.silu(pre_peer[...].astype(WIDE)).astype(LOW)
        grads[:PIX] = grad[...]
        grads[PIX:] = grad_peer[...]
        staged[...] = contract_rows(acts[...], grads[...])

    put(SLOTS - 1, staged[...])


def second_kernel(at, keep_a, got_a, keep_b, got_b, next_a, send_a, next_b, send_b):
    axis_x, axis_y = at[0], at[1]
    for keep, got, mine, stay, send in (
        (keep_a, got_a, axis_y, next_a, send_a),
        (keep_b, got_b, axis_x, next_b, send_b),
    ):
        for which, out in ((mine, stay), (1 - mine, send)):
            rows = pl.ds(pl.multiple_of(which * 64, 64), 64)
            out[...] = (keep[:, rows].astype(WIDE) + got[:, rows].astype(WIDE)).astype(LOW)


def third_kernel(at, keep_a, got_a, keep_b, got_b, own, *sends):
    for away, out in enumerate((own,) + sends):
        rows = pl.ds(pl.multiple_of((at[2] ^ away) * 16, 16), 16)
        out[:HALF] = (keep_a[:, rows].astype(WIDE) + got_a[:, rows].astype(WIDE)).astype(LOW)
        out[HALF:] = (keep_b[:, rows].astype(WIDE) + got_b[:, rows].astype(WIDE)).astype(LOW)


def moment_kernel(at, rate, own, one, two, three, row_moment, scaled, message):
    total = own[...].astype(WIDE) + one[...].astype(WIDE)
    total = total + (two[...].astype(WIDE) + three[...].astype(WIDE))
    total = total.reshape(SLOTS * 16, CO)
    squares = total * total
    decay = rate[0]
    mean = jnp.sum(squares, axis=1, keepdims=True) * (1.0 / CO)
    new_row = decay * row_moment[...] + (1.0 - decay) * mean
    scaled[...] = (total * lax.rsqrt(new_row)).astype(LOW).reshape(SLOTS, 16, CO)
    weighted = squares / new_row
    cut = (SLOTS - 1) * 16
    last_small = at[3] == 1
    rows = []
    for values in (squares, weighted, jnp.broadcast_to(new_row, (SLOTS * 16, CO))):
        large = jnp.sum(values[:cut], axis=0, keepdims=True)
        last = jnp.sum(values[cut:], axis=0, keepdims=True)
        rows.append(large + jnp.where(last_small, 0.0, last))
        rows.append(jnp.where(last_small, last, 0.0))
    spread = jnp.broadcast_to(new_row, (SLOTS * 16, 128))
    spread = jnp.concatenate([spread, jnp.zeros((32, 128), WIDE)], axis=0)
    rows.append(jnp.transpose(spread)[:1])
    rows.append(jnp.zeros((1, CO), WIDE))
    message[...] = jnp.concatenate(rows, axis=0)


def factor_kernel(rate, mine, peer, col_moment, new_col, factor):
    total = jnp.sum(mine[...], axis=0) + jnp.sum(peer[...], axis=0)
    decay = rate[0]
    for kernel in range(2):
        count = 27.0 * CI if kernel == 0 else float(CO)
        col = decay * col_moment[kernel : kernel + 1] + (1.0 - decay) * (
            total[kernel : kernel + 1] / count
        )
        row_mean = total[4 + kernel : 5 + kernel] / count
        square = row_mean * jnp.sum(
            total[2 + kernel : 3 + kernel] / col, axis=1, keepdims=True
        )
        clip = jnp.maximum(1.0, jnp.sqrt(square / (count * CO)))
        new_col[kernel : kernel + 1] = col
        factor[kernel : kernel + 1] = 1.0 / (jnp.sqrt(col / row_mean) * clip)


def order_kernel(at, block_order, *refs):
    pieces, out = refs[:-1], refs[-1]
    count = NB // 8
    for index, piece in enumerate(pieces):
        flip_core, away = divmod(index, 4)
        owner = (at[2] ^ away) * 2 + (at[3] ^ flip_core)

        def move(local, carry, piece=piece, owner=owner):
            block = block_order[owner * count + local]
            to = pl.ds(pl.multiple_of(block * BLK, BLK), BLK)
            out[to, :] = piece[pl.ds(pl.multiple_of(local * BLK, BLK), BLK), :]
            return carry

        lax.fori_loop(0, count, move, 0, unroll=4)


def join_kernel(at, own, one, two, three, out_a, out_b):
    for away, piece in enumerate((own, one, two, three)):
        rows = pl.ds(pl.multiple_of((at[2] ^ away) * 16, 16), 16)
        out_a[:, rows] = piece[:HALF]
        out_b[:, rows] = piece[HALF:]


def pair_kernel(at, mine_a, got_a, mine_b, got_b, out_a, out_b):
    for which, mine, got, out in ((at[1], mine_a, got_a, out_a), (at[0], mine_b, got_b, out_b)):
        out[:, pl.ds(pl.multiple_of(which * 64, 64), 64)] = mine[...]
        out[:, pl.ds(pl.multiple_of(64 - which * 64, 64), 64)] = got[...]


def finish_kernel(
    at, block_order, factor, views, natural, master,
    mine_a, got_a, mine_b, got_b, peer_a, peer_got_a, peer_b, peer_got_b,
    update_rows, new_master, next_output, scaled, hidden, pointwise,
):
    axis_x, axis_y, core = at[0], at[1], at[3]
    for index, (a_own, a_got, b_own, b_got) in enumerate(
        ((mine_a, got_a, mine_b, got_b), (peer_a, peer_got_a, peer_b, peer_got_b))
    ):
        base = (core ^ index) * SLOTS
        for which, piece in ((axis_x, a_own), (1 - axis_x, a_got)):
            rows = pl.ds(pl.multiple_of(which * 128, 128), 128)
            scaled[pl.ds(base, HALF), rows] = piece[...]
        for which, piece in ((axis_y, b_own), (1 - axis_y, b_got)):
            for half in range(2):
                rows = pl.ds(pl.multiple_of(half * 128 + which * 64, 64), 64)
                scaled[pl.ds(base + HALF, HALF), rows] = piece[:, half * 64 : half * 64 + 64]
    large = learn_rate * factor[0:1]
    total = jnp.zeros((PIX, CO), WIDE)
    for tap in range(27):
        frame_off, row_off, col_off = tap // 9, tap // 3 % 3, tap % 3
        weights = natural[tap * CI : tap * CI + CI].astype(WIDE) - scaled[tap].astype(WIDE) * large
        starts = [((frame + frame_off) * (HW + 2) + row_off) * HW for frame in range(FR)]
        window = jnp.concatenate(
            [views[col_off, start : start + HW * HW, :] for start in starts], axis=0
        )
        total = total + jnp.dot(window, weights.astype(LOW), preferred_element_type=WIDE)
    small = learn_rate * factor[1:2]
    weights = natural[27 * CI :].astype(WIDE) - scaled[27].astype(WIDE) * small
    next_act = jax.nn.silu(total).astype(LOW)
    next_output[...] = jnp.dot(
        next_act, weights.astype(LOW), preferred_element_type=WIDE
    ).astype(LOW)

    owner = at[2] * 2 + core

    def own_block(local, carry):
        block = block_order[owner * (NB // 8) + local]
        chosen = jnp.where(block >= NB3, factor[1:2], factor[0:1])
        rows = pl.ds(pl.multiple_of(local * BLK, BLK), BLK)
        start = pl.multiple_of(lax.rem(block, 8) * BLK, BLK)
        update = scaled[block // 8, pl.ds(start, BLK), :].astype(WIDE) * chosen
        update_rows[rows, :] = update
        new_master[rows, :] = master[rows, :] - learn_rate * update
        return carry

    lax.fori_loop(0, NB // 8, own_block, 0, unroll=4)


def shards(
    step_count,
    block_order,
    saved_tiles,
    pre_act,
    grad_output,
    pointwise_live,
    master_rows,
    row_moment,
    col_moment,
    next_tiles,
):
    group, shard = lax.axis_index("group"), lax.axis_index("shard")
    axis_y, axis_x, axis_z, core = group // 2, group % 2, shard // 2, shard % 2
    at = jnp.stack([axis_x, axis_y, axis_z, core]).astype(jnp.int32)
    decay_rate = 1.0 - step_count.astype(WIDE) ** (-decay_power)

    tile_peer = swap(saved_tiles, MASK_CORE)
    pre_peer = swap(pre_act, MASK_CORE)
    grad_peer = swap(grad_output, MASK_CORE)
    part_a, part_b = (HALF, 128, CO), (HALF, 128, CO)
    keep_a, send_a, keep_b, send_b = call(
        term_kernel,
        [(part_a, LOW), (part_a, LOW), (part_b, LOW), (part_b, LOW)],
        [SMEM] + [VMEM] * 7,
        scratch=[
            pltpu.VMEM((2, 3, SHIFTED, CI), LOW),
            pltpu.VMEM((2 * PIX, CO), LOW),
            pltpu.VMEM((2 * PIX, CO), LOW),
            pltpu.VMEM((2 * PIX, CO), LOW),
            pltpu.VMEM((CI, CO), WIDE),
        ],
        flops=2 * 14 * 1024 * 256 * 256,
        moved=6 << 20,
    )(
        at, saved_tiles[0], tile_peer[0], pre_act, pre_peer, grad_output, grad_peer, pointwise_live
    )

    master_low = master_rows.astype(LOW)
    master_line = [master_low] + [swap(master_low, away * 2) for away in (1, 2, 3)]
    master_all = master_line + [swap(piece, MASK_CORE) for piece in master_line]
    natural = call(
        order_kernel, [((NB * BLK, CO), LOW)], [SMEM] * 2 + [VMEM] * 8, moved=8 << 20
    )(at, block_order, *master_all)[0]
    moment_line = jnp.stack([row_moment] + [swap(row_moment, away * 2) for away in (1, 2, 3)])
    moment_all = jnp.stack([moment_line, swap(moment_line, MASK_CORE)])
    moment_stored = moment_all[jnp.arange(2) ^ core][:, jnp.arange(4) ^ axis_z]
    moment_stored = jnp.swapaxes(moment_stored, 0, 1).reshape(NB, BLK)
    inverse = jnp.zeros((NB,), jnp.int32).at[block_order].set(jnp.arange(NB, dtype=jnp.int32))
    moment_natural = jnp.take(moment_stored, inverse, axis=0).reshape(2, SLOTS, 16, 16)
    place = axis_x * 8 + axis_y * 4 + axis_z
    own_moment = lax.dynamic_index_in_dim(
        lax.dynamic_index_in_dim(moment_natural, core, 0, False), place, 1, False
    ).reshape(SLOTS * 16, 1)
    views = call(shift_kernel, [((3, SHIFTED, CI), LOW)], [VMEM], moved=3 << 20)(next_tiles[0])[0]

    got_a, got_b = swap(send_a, MASK_X), swap(send_b, MASK_Y)
    quarter = (HALF, 64, CO)
    keep_a, send_a, keep_b, send_b = call(
        second_kernel, [(quarter, LOW)] * 4, [SMEM] + [VMEM] * 4, moved=3 << 20
    )(at, keep_a, got_a, keep_b, got_b)
    got_a, got_b = swap(send_a, MASK_Y), swap(send_b, MASK_X)
    piece = (SLOTS, 16, CO)
    own, *sends = call(third_kernel, [(piece, LOW)] * 4, [SMEM] + [VMEM] * 4, moved=2 << 20)(
        at, keep_a, got_a, keep_b, got_b
    )
    gots = [swap(send, (away + 1) * 2) for away, send in enumerate(sends)]
    scaled, message = call(
        moment_kernel,
        [(piece, LOW), ((8, CO), WIDE)],
        [SMEM] * 2 + [VMEM] * 5,
        moved=1 << 20,
    )(at, decay_rate, own, *gots, own_moment)

    gots = [swap(scaled, away * 2) for away in (1, 2, 3)]
    mine_a, mine_b = call(join_kernel, [(quarter, LOW)] * 2, [SMEM] + [VMEM] * 4, moved=1 << 20)(
        at, scaled, *gots
    )
    got_a, got_b = swap(mine_a, MASK_Y), swap(mine_b, MASK_X)
    mine_a, mine_b = call(
        pair_kernel, [(part_a, LOW), (part_b, LOW)], [SMEM] + [VMEM] * 4, moved=2 << 20
    )(at, mine_a, got_a, mine_b, got_b)
    got_a, got_b = swap(mine_a, MASK_X), swap(mine_b, MASK_Y)
    halves = (mine_a, got_a, mine_b, got_b)
    peers = [swap(half, MASK_CORE) for half in halves]

    line = jnp.stack([message] + [swap(message, away * 2) for away in (1, 2, 3)])
    plane = jnp.stack([line] + [swap(line, mask) for mask in (MASK_Y, MASK_X, MASK_X + MASK_Y)])
    plane_peer = swap(plane, MASK_CORE)
    new_col, factor = call(
        factor_kernel, [((2, CO), WIDE)] * 2, [SMEM] + [VMEM] * 3, moved=1 << 18
    )(decay_rate, plane.reshape(16, 8, CO), plane_peer.reshape(16, 8, CO), col_moment)
    rows = jnp.stack([plane, plane_peer])[:, :, :, 6, : SLOTS * 16]
    rows = rows[jnp.arange(2) ^ core]
    rows = rows[:, jnp.arange(4) ^ (axis_x * 2 + axis_y)]
    rows = rows[:, :, jnp.arange(4) ^ axis_z].reshape(2, 4, 4, SLOTS, 16)
    rows = jnp.transpose(rows, (0, 3, 1, 2, 4)).reshape(NB, BLK)
    own_blocks = lax.dynamic_slice_in_dim(block_order, shard * (NB // 8), NB // 8)
    new_row = jnp.take(rows, own_blocks, axis=0).reshape(-1)

    update_rows, new_master, next_output = call(
        finish_kernel,
        [((NB // 8 * BLK, CO), WIDE), ((NB // 8 * BLK, CO), WIDE), ((PIX, CO), LOW)],
        [SMEM] * 2 + [VMEM] * 12,
        scratch=[
            pltpu.VMEM((28, CI, CO), LOW),
            pltpu.VMEM((PIX, CO), WIDE),
            pltpu.VMEM((CI, CO), LOW),
        ],
        flops=2 * 28 * 512 * 256 * 256,
        moved=16 << 20,
    )(at, block_order, factor, views, natural, master_rows, *halves, *peers)
    return (update_rows, new_master, new_row, new_col, next_output)


def solution(mesh):
    in_specs = (
        P(),
        P(),
        P(("group", "shard"), None, None, None, None),
        P(("group", "shard"), None),
        P(("group", "shard"), None),
        P(),
        P("shard", None),
        P("shard"),
        P(),
        P(("group", "shard"), None, None, None, None),
    )
    out_specs = (P("shard", None), P("shard", None), P("shard"), P(), P(("group", "shard"), None))
    body = shards if (mesh.shape["group"], mesh.shape["shard"]) == (4, 8) else general_shards
    return jax.shard_map(body, mesh=mesh, in_specs=in_specs, out_specs=out_specs, check_vma=False)
```

```python
import functools
import jax
import jax.numpy as jnp
from jax import lax
from jax.experimental import pallas as pl
from jax.experimental.pallas import tpu as pltpu
from jax.sharding import PartitionSpec as P

CI = 256
CO = 256
BLK = 32
FR = 2
HW = 16
NB3 = 216
NB = 224


learn_rate = 0.002
decay_power = 0.8


def silu_slope(values):
    sigma = jax.nn.sigmoid(values)
    return sigma * (1.0 + values * (1.0 - sigma))


def tap_views(frames):
    views = []
    for frame_off in range(3):
        for row_off in range(3):
            for col_off in range(3):
                window = frames[
                    frame_off : frame_off + FR, row_off : row_off + HW, col_off : col_off + HW, :
                ]
                views.append(window.reshape(FR * HW * HW, CI))
    return views


def contract_rows(left, right):
    return lax.dot_general(
        left, right, (((0,), (0,)), ((), ())), preferred_element_type=jnp.float32
    )


def kernel_sums(values, is_small):
    large_part = jnp.sum(jnp.where(is_small[:, None], 0.0, values), axis=0)
    small_part = jnp.sum(jnp.where(is_small[:, None], values, 0.0), axis=0)
    return jnp.stack([large_part, small_part])


def general_shards(
    step_count,
    block_order,
    saved_tiles,
    pre_act,
    grad_output,
    pointwise_live,
    master_rows,
    row_moment,
    col_moment,
    next_tiles,
):
    pre_float = pre_act.astype(jnp.float32)
    activation = jax.nn.silu(pre_float).astype(jnp.bfloat16)
    grad_act = lax.dot_general(
        grad_output, pointwise_live, (((1,), (1,)), ((), ())), preferred_element_type=jnp.float32
    )
    grad_pre = (grad_act * silu_slope(pre_float)).astype(jnp.bfloat16)
    pieces = [contract_rows(view, grad_pre) for view in tap_views(saved_tiles[0])]
    pieces.append(contract_rows(activation, grad_output))
    own_term = jnp.concatenate(pieces, axis=0).astype(jnp.bfloat16)
    total_rows = NB * BLK
    stored = jnp.take(own_term.reshape(NB, BLK, CO), block_order, axis=0).reshape(total_rows, CO)
    own_rows = master_rows.shape[0]
    partial_value = lax.psum_scatter(stored, "shard", scatter_dimension=0, tiled=True).astype(
        jnp.float32
    )
    gradient = lax.psum(partial_value, "group")
    owner = lax.axis_index("shard")
    own_count = own_rows // BLK
    own_blocks = lax.dynamic_slice_in_dim(block_order, owner * own_count, own_count)
    is_small = jnp.repeat(own_blocks >= NB3, BLK, total_repeat_length=own_rows)
    decay_rate = 1.0 - step_count.astype(jnp.float32)[0] ** (-decay_power)
    counts = jnp.array([27 * CI, CO], jnp.float32)
    squares = gradient * gradient
    new_row = decay_rate * row_moment + (1.0 - decay_rate) * jnp.mean(squares, axis=1)
    col_part = kernel_sums(squares, is_small)
    row_part = kernel_sums(new_row[:, None], is_small)[:, 0]
    weighted = kernel_sums(squares / new_row[:, None], is_small)
    col_total, weight_total, row_total = lax.psum((col_part, weighted, row_part), "shard")
    new_col = decay_rate * col_moment + (1.0 - decay_rate) * col_total / counts[:, None]
    row_mean = row_total / counts
    col_rows = jnp.where(is_small[:, None], new_col[1], new_col[0])
    mean_rows = jnp.where(is_small, row_mean[1], row_mean[0])
    scaled = gradient / jnp.sqrt(new_row[:, None] * col_rows / mean_rows[:, None])
    square_total = row_mean * jnp.sum(weight_total / new_col, axis=1)
    clip_factor = jnp.maximum(1.0, jnp.sqrt(square_total / (counts * CO)))
    update_rows = scaled / jnp.where(is_small, clip_factor[1], clip_factor[0])[:, None]
    new_master = master_rows - learn_rate * update_rows
    weights_low = new_master.astype(jnp.bfloat16)
    gathered = lax.all_gather(weights_low, "shard", axis=0, tiled=True)
    inverse = jnp.zeros((NB,), jnp.int32).at[block_order].set(jnp.arange(NB, dtype=jnp.int32))
    natural = jnp.take(gathered.reshape(NB, BLK, CO), inverse, axis=0).reshape(total_rows, CO)
    spatial = natural[: 27 * CI].reshape(27, CI, CO)
    pointwise = natural[27 * CI :]
    hidden_sum = jnp.zeros((FR * HW * HW, CO), jnp.float32)
    for index_tap, view in enumerate(tap_views(next_tiles[0])):
        hidden_sum = hidden_sum + jnp.dot(
            view, spatial[index_tap], preferred_element_type=jnp.float32
        )
    hidden_act = jax.nn.silu(hidden_sum).astype(jnp.bfloat16)
    next_output = jnp.dot(hidden_act, pointwise, preferred_element_type=jnp.float32).astype(
        jnp.bfloat16
    )
    return (update_rows, new_master, new_row, new_col, next_output)


AXES = ("group", "shard")
SLOTS = 14
HALF = 7
PIX = FR * HW * HW
SHIFTED = (FR + 2) * (HW + 2) * HW
LOW = jnp.bfloat16
WIDE = jnp.float32
VMEM = pl.BlockSpec(memory_space=pltpu.VMEM)
SMEM = pl.BlockSpec(memory_space=pltpu.SMEM)
HBM = pl.BlockSpec(memory_space=pl.ANY)
MASK_CORE, MASK_X, MASK_Y = 1, 8, 16


def swap(value, mask):
    return lax.ppermute(value, AXES, [(at, at ^ mask) for at in range(32)])


def call(kernel, outs, in_specs, scratch=(), flops=0, moved=0, room=8):
    return pl.pallas_call(
        kernel,
        out_shape=[jax.ShapeDtypeStruct(shape, dtype) for shape, dtype in outs],
        in_specs=in_specs,
        out_specs=[VMEM] * len(outs),
        scratch_shapes=list(scratch),
        compiler_params=pltpu.CompilerParams(vmem_limit_bytes=room << 20),
        cost_estimate=pl.CostEstimate(flops=flops, bytes_accessed=moved, transcendentals=0),
    )


def store_shifted(tile, out):
    for col_off in range(3):
        out[col_off] = tile[:, :, col_off : col_off + HW, :].reshape(SHIFTED, CI)


def shift_kernel(tile, out):
    store_shifted(tile, out)


def slope_of(pre, grad, pointwise):
    grad_act = lax.dot_general(
        grad, pointwise, (((1,), (1,)), ((), ())), preferred_element_type=WIDE
    )
    return (grad_act * silu_slope(pre.astype(WIDE))).astype(LOW)


def term_kernel(
    at, tile, tile_peer, pre, pre_peer, grad, grad_peer, pointwise,
    keep_a, send_a, keep_b, send_b, views, slopes, acts, grads, staged,
):
    axis_x, axis_y, core = at[0], at[1], at[3]
    store_shifted(tile, views.at[0])
    store_shifted(tile_peer, views.at[1])
    slopes[:PIX] = slope_of(pre[...], grad[...], pointwise[...])
    slopes[PIX:] = slope_of(pre_peer[...], grad_peer[...], pointwise[...])

    def put(slot, total):
        value = total.astype(LOW)
        if slot < HALF:
            for mine in range(2):

                @pl.when(axis_x == mine)
                def _():
                    keep_a[slot] = value[mine * 128 : mine * 128 + 128]
                    send_a[slot] = value[128 - mine * 128 : 256 - mine * 128]
        else:
            for mine in range(2):

                @pl.when(axis_y == mine)
                def _():
                    for half in range(2):
                        base, other = half * 128 + mine * 64, half * 128 + 64 - mine * 64
                        to = slice(half * 64, half * 64 + 64)
                        keep_b[slot - HALF, to] = value[base : base + 64]
                        send_b[slot - HALF, to] = value[other : other + 64]

    def tap_rows(tap):
        frame_off, row_off, col_off = tap // 9, lax.rem(tap // 3, 3), lax.rem(tap, 3)
        parts = []
        for peer in range(2):
            for frame in range(FR):
                start = pl.multiple_of(((frame + frame_off) * (HW + 2) + row_off) * HW, HW)
                parts.append(views[peer, col_off, pl.ds(start, HW * HW), :])
        return jnp.concatenate(parts, axis=0)

    for slot in range(SLOTS - 1):
        put(slot, contract_rows(tap_rows(core * SLOTS + slot), slopes[...]))

    @pl.when(core == 0)
    def _():
        staged[...] = contract_rows(tap_rows(SLOTS - 1), slopes[...])

    @pl.when(core == 1)
    def _():
        acts[:PIX] = jax.nn.silu(pre[...].astype(WIDE)).astype(LOW)
        acts[PIX:] = jax.nn.silu(pre_peer[...].astype(WIDE)).astype(LOW)
        grads[:PIX] = grad[...]
        grads[PIX:] = grad_peer[...]
        staged[...] = contract_rows(acts[...], grads[...])

    put(SLOTS - 1, staged[...])


def second_kernel(at, keep_a, got_a, keep_b, got_b, next_a, send_a, next_b, send_b):
    axis_x, axis_y = at[0], at[1]
    for keep, got, mine, stay, send in (
        (keep_a, got_a, axis_y, next_a, send_a),
        (keep_b, got_b, axis_x, next_b, send_b),
    ):
        for which, out in ((mine, stay), (1 - mine, send)):
            rows = pl.ds(pl.multiple_of(which * 64, 64), 64)
            out[...] = (keep[:, rows].astype(WIDE) + got[:, rows].astype(WIDE)).astype(LOW)


def third_kernel(at, keep_a, got_a, keep_b, got_b, own, *sends):
    for away, out in enumerate((own,) + sends):
        rows = pl.ds(pl.multiple_of((at[2] ^ away) * 16, 16), 16)
        out[:HALF] = (keep_a[:, rows].astype(WIDE) + got_a[:, rows].astype(WIDE)).astype(LOW)
        out[HALF:] = (keep_b[:, rows].astype(WIDE) + got_b[:, rows].astype(WIDE)).astype(LOW)


def moment_kernel(at, rate, own, one, two, three, row_moment, scaled):
    total = own[...].astype(WIDE) + one[...].astype(WIDE)
    total = total + (two[...].astype(WIDE) + three[...].astype(WIDE))
    total = total.reshape(SLOTS * 16, CO)
    squares = total * total
    decay = rate[0]
    mean = jnp.sum(squares, axis=1, keepdims=True) * (1.0 / CO)
    new_row = decay * row_moment[...] + (1.0 - decay) * mean
    scaled[:SLOTS] = (total * lax.rsqrt(new_row)).astype(LOW).reshape(SLOTS, 16, CO)
    weighted = squares / new_row
    cut = (SLOTS - 1) * 16
    last_small = at[3] == 1
    rows = []
    for values in (squares, weighted, jnp.broadcast_to(new_row, (SLOTS * 16, CO))):
        large = jnp.sum(values[:cut], axis=0, keepdims=True)
        last = jnp.sum(values[cut:], axis=0, keepdims=True)
        rows.append(large + jnp.where(last_small, 0.0, last))
        rows.append(jnp.where(last_small, last, 0.0))
    spread = jnp.broadcast_to(new_row, (SLOTS * 16, 128))
    spread = jnp.concatenate([spread, jnp.zeros((32, 128), WIDE)], axis=0)
    rows.append(jnp.transpose(spread)[:1])
    rows.append(jnp.zeros((1, CO), WIDE))
    message = jnp.concatenate(rows, axis=0)
    high = message.astype(LOW).astype(WIDE)
    scaled[SLOTS] = jnp.concatenate([high, message - high], axis=0).astype(LOW)


def store_factors(total, decay, col_moment, new_col, factor):
    for kernel in range(2):
        count = 27.0 * CI if kernel == 0 else float(CO)
        col = decay * col_moment[kernel : kernel + 1] + (1.0 - decay) * (
            total[kernel : kernel + 1] / count
        )
        row_mean = total[4 + kernel : 5 + kernel] / count
        square = row_mean * jnp.sum(
            total[2 + kernel : 3 + kernel] / col, axis=1, keepdims=True
        )
        clip = jnp.maximum(1.0, jnp.sqrt(square / (count * CO)))
        new_col[kernel : kernel + 1] = col
        factor[kernel : kernel + 1] = 1.0 / (jnp.sqrt(col / row_mean) * clip)


def pack_kernel(at, master, row_moment, packed, rows, arrived):
    quarter = (at[1] * 2 + at[0]) * (SLOTS * 16)
    copy = pltpu.make_async_copy(
        master.at[pl.ds(pl.multiple_of(quarter, SLOTS * 16), SLOTS * 16), :], rows, arrived
    )
    copy.start()
    copy.wait()
    packed[:SLOTS] = rows[...].astype(LOW).reshape(SLOTS, 16, CO)
    values = jnp.concatenate([row_moment[...], jnp.zeros((9, 128), WIDE)], axis=0)
    high = values.astype(LOW).astype(WIDE)
    packed[SLOTS] = jnp.concatenate([high, values - high], axis=1).astype(LOW)


def line_kernel(at, after, own, one, two, three, out):
    for away, piece in enumerate((own, one, two, three)):
        out[at[2] ^ away] = piece[:SLOTS].reshape(SLOTS * 16, CO)


def order_kernel(at, block_order, *refs):
    pieces, out = refs[:-1], refs[-1]
    count = NB // 8
    blocks = count // 4
    for index, piece in enumerate(pieces):
        flip_core, away = divmod(index, 4)
        core, quarter = at[3] ^ flip_core, (at[1] * 2 + at[0]) ^ away
        for line in range(4):
            for local in range(blocks):
                block = block_order[(line * 2 + core) * count + quarter * blocks + local]
                to = pl.ds(pl.multiple_of(block * BLK, BLK), BLK)
                out[to, :] = piece[line, local * BLK : local * BLK + BLK]


def join_kernel(at, after, own, one, two, three, out_a, out_b):
    for away, piece in enumerate((own, one, two, three)):
        rows = pl.ds(pl.multiple_of((at[2] ^ away) * 16, 16), 16)
        out_a[:, rows] = piece[:HALF]
        out_b[:, rows] = piece[HALF:]


def pair_kernel(at, after, mine_a, got_a, mine_b, got_b, out_a, out_b):
    for which, mine, got, out in ((at[1], mine_a, got_a, out_a), (at[0], mine_b, got_b, out_b)):
        out[:, pl.ds(pl.multiple_of(which * 64, 64), 64)] = mine[...]
        out[:, pl.ds(pl.multiple_of(64 - which * 64, 64), 64)] = got[...]


def finish_kernel(
    at, block_order, rate, col_moment, views, natural, master,
    mine_a, got_a, mine_b, got_b, peer_a, peer_got_a, peer_b, peer_got_b,
    update_rows, new_master, new_row, new_col, next_output, scaled, factor, row_table,
):
    axis_x, axis_y, core = at[0], at[1], at[3]
    for index, (a_own, a_got, b_own, b_got) in enumerate(
        ((mine_a, got_a, mine_b, got_b), (peer_a, peer_got_a, peer_b, peer_got_b))
    ):
        side = core ^ index
        for which, piece in ((axis_x, a_own), (1 - axis_x, a_got)):
            rows = pl.ds(pl.multiple_of(which * 128, 128), 128)
            scaled[side, :HALF, rows] = piece[...]
        for which, piece in ((axis_y, b_own), (1 - axis_y, b_got)):
            for half in range(2):
                rows = pl.ds(pl.multiple_of(half * 128 + which * 64, 64), 64)
                scaled[side, HALF:, rows] = piece[:, half * 64 : half * 64 + 64]
    message = scaled[:, SLOTS].astype(WIDE).reshape(32, 2, 8, CO)
    message = message[:, 0] + message[:, 1]
    store_factors(jnp.sum(message, axis=0), rate[0], col_moment, new_col, factor)
    for index in range(32):
        for half in range(2):
            row_table[index * 2 + half : index * 2 + half + 1] = message[
                index, 6:7, half * 128 : half * 128 + 128
            ]
    large = learn_rate * factor[0:1]
    total = jnp.zeros((PIX, CO), WIDE)
    for tap in range(27):
        frame_off, row_off, col_off = tap // 9, tap // 3 % 3, tap % 3
        step = scaled[tap // SLOTS, tap % SLOTS].astype(WIDE) * large
        weights = natural[tap * CI : tap * CI + CI].astype(WIDE) - step
        starts = [((frame + frame_off) * (HW + 2) + row_off) * HW for frame in range(FR)]
        window = jnp.concatenate(
            [views[col_off, start : start + HW * HW, :] for start in starts], axis=0
        )
        total = total + jnp.dot(window, weights.astype(LOW), preferred_element_type=WIDE)
    small = learn_rate * factor[1:2]
    weights = natural[27 * CI :].astype(WIDE) - scaled[1, SLOTS - 1].astype(WIDE) * small
    next_act = jax.nn.silu(total).astype(LOW)
    next_output[...] = jnp.dot(
        next_act, weights.astype(LOW), preferred_element_type=WIDE
    ).astype(LOW)

    owner = at[2] * 2 + core
    lane = lax.broadcasted_iota(jnp.int32, (1, 128), 1)
    for line in range(7):
        values = jnp.zeros((1, 128), WIDE)
        for part in range(4):
            local = line * 4 + part
            block = block_order[owner * (NB // 8) + local]
            side, slot, place = block // (8 * SLOTS), lax.rem(block // 8, SLOTS), lax.rem(block, 8)
            chosen = jnp.where(block >= NB3, factor[1:2], factor[0:1])
            rows = slice(local * BLK, local * BLK + BLK)
            start = pl.multiple_of(place * BLK, BLK)
            update = scaled[side, slot, pl.ds(start, BLK), :].astype(WIDE) * chosen
            update_rows[rows, :] = update
            new_master[rows, :] = master[rows, :] - learn_rate * update
            for half in range(2):
                at_row = (side * 16 + place * 2 + half) * 2 + slot // 8
                to = part * 32 + half * 16
                turn = lax.rem(128 + to - lax.rem(slot, 8) * 16, 128)
                turned = pltpu.roll(row_table[pl.ds(at_row, 1), :], turn, 1)
                values = jnp.where((lane >= to) & (lane < to + 16), turned, values)
        new_row[line : line + 1] = values


def shards(
    step_count,
    block_order,
    saved_tiles,
    pre_act,
    grad_output,
    pointwise_live,
    master_rows,
    row_moment,
    col_moment,
    next_tiles,
):
    group, shard = lax.axis_index("group"), lax.axis_index("shard")
    axis_y, axis_x, axis_z, core = group // 2, group % 2, shard // 2, shard % 2
    at = jnp.stack([axis_x, axis_y, axis_z, core]).astype(jnp.int32)
    decay_rate = 1.0 - step_count.astype(WIDE) ** (-decay_power)

    tile_peer = swap(saved_tiles, MASK_CORE)
    pre_peer = swap(pre_act, MASK_CORE)
    grad_peer = swap(grad_output, MASK_CORE)
    part_a, part_b = (HALF, 128, CO), (HALF, 128, CO)
    keep_a, send_a, keep_b, send_b = call(
        term_kernel,
        [(part_a, LOW), (part_a, LOW), (part_b, LOW), (part_b, LOW)],
        [SMEM] + [VMEM] * 7,
        scratch=[
            pltpu.VMEM((2, 3, SHIFTED, CI), LOW),
            pltpu.VMEM((2 * PIX, CO), LOW),
            pltpu.VMEM((2 * PIX, CO), LOW),
            pltpu.VMEM((2 * PIX, CO), LOW),
            pltpu.VMEM((CI, CO), WIDE),
        ],
        flops=2 * 14 * 1024 * 256 * 256,
        moved=6 << 20,
        room=16,
    )(
        at, saved_tiles[0], tile_peer[0], pre_act, pre_peer, grad_output, grad_peer, pointwise_live
    )

    packed = call(
        pack_kernel,
        [((SLOTS + 1, 16, CO), LOW)],
        [SMEM, HBM, VMEM],
        scratch=[pltpu.VMEM((SLOTS * 16, CO), WIDE), pltpu.SemaphoreType.DMA],
    )(at, master_rows, row_moment.reshape(7, 128))[0]
    packs = [packed] + [swap(packed, away * 2) for away in (1, 2, 3)]
    moment_line = jnp.stack([pack[SLOTS] for pack in packs])
    moment_all = jnp.stack([moment_line, swap(moment_line, MASK_CORE)])[:, :, :7].astype(WIDE)
    moment_all = (moment_all[..., :128] + moment_all[..., 128:]).reshape(2, 4, 896)
    moment_stored = moment_all[jnp.arange(2) ^ core][:, jnp.arange(4) ^ axis_z]
    moment_stored = jnp.swapaxes(moment_stored, 0, 1).reshape(NB, BLK)
    inverse = jnp.zeros((NB,), jnp.int32).at[block_order].set(jnp.arange(NB, dtype=jnp.int32))
    moment_natural = jnp.take(moment_stored, inverse, axis=0).reshape(2, SLOTS, 16, 16)
    place = axis_x * 8 + axis_y * 4 + axis_z
    own_moment = lax.dynamic_index_in_dim(
        lax.dynamic_index_in_dim(moment_natural, core, 0, False), place, 1, False
    ).reshape(SLOTS * 16, 1)
    views = call(shift_kernel, [((3, SHIFTED, CI), LOW)], [VMEM], moved=3 << 20)(next_tiles[0])[0]

    got_a, got_b = swap(send_a, MASK_X), swap(send_b, MASK_Y)
    quarter = (HALF, 64, CO)
    keep_a, send_a, keep_b, send_b = call(
        second_kernel, [(quarter, LOW)] * 4, [SMEM] + [VMEM] * 4, moved=3 << 20
    )(at, keep_a, got_a, keep_b, got_b)
    got_a, got_b = swap(send_a, MASK_Y), swap(send_b, MASK_X)
    piece = (SLOTS, 16, CO)
    own, *sends = call(third_kernel, [(piece, LOW)] * 4, [SMEM] + [VMEM] * 4, moved=2 << 20)(
        at, keep_a, got_a, keep_b, got_b
    )
    gots = [swap(send, (away + 1) * 2) for away, send in enumerate(sends)]
    wide_piece = (SLOTS + 1, 16, CO)
    scaled = call(moment_kernel, [(wide_piece, LOW)], [SMEM] * 2 + [VMEM] * 5, moved=1 << 20)(
        at, decay_rate, own, *gots, own_moment
    )[0]

    line = call(
        line_kernel, [((4, SLOTS * 16, CO), LOW)], [SMEM, HBM] + [VMEM] * 4, moved=1 << 20
    )(at, own, *packs)[0]
    plane = [line] + [swap(line, mask) for mask in (MASK_X, MASK_Y, MASK_X + MASK_Y)]
    plane_peer = [swap(piece, MASK_CORE) for piece in plane]
    natural = call(
        order_kernel, [((NB * BLK, CO), LOW)], [SMEM] * 2 + [VMEM] * 8, moved=8 << 20
    )(at, block_order, *plane, *plane_peer)[0]

    gots = [swap(scaled, away * 2) for away in (1, 2, 3)]
    mine_a, mine_b = call(
        join_kernel,
        [((HALF, 64, CO), LOW), ((HALF + 1, 64, CO), LOW)],
        [SMEM, HBM] + [VMEM] * 4,
        moved=1 << 20,
    )(at, views, scaled, *gots)
    got_a, got_b = swap(mine_a, MASK_Y), swap(mine_b, MASK_X)
    mine_a, mine_b = call(
        pair_kernel,
        [((HALF, 128, CO), LOW), ((HALF + 1, 128, CO), LOW)],
        [SMEM, HBM] + [VMEM] * 4,
        moved=2 << 20,
    )(at, natural, mine_a, got_a, mine_b, got_b)
    got_a, got_b = swap(mine_a, MASK_X), swap(mine_b, MASK_Y)
    halves = (mine_a, got_a, mine_b, got_b)
    peers = [swap(half, MASK_CORE) for half in halves]

    update_rows, new_master, new_row, new_col, next_output = call(
        finish_kernel,
        [
            ((NB // 8 * BLK, CO), WIDE),
            ((NB // 8 * BLK, CO), WIDE),
            ((7, 128), WIDE),
            ((2, CO), WIDE),
            ((PIX, CO), LOW),
        ],
        [SMEM] * 3 + [VMEM] * 12,
        scratch=[
            pltpu.VMEM((2, SLOTS + 1, CI, CO), LOW),
            pltpu.VMEM((2, CO), WIDE),
            pltpu.VMEM((64, 128), WIDE),
        ],
        flops=2 * 28 * 512 * 256 * 256,
        moved=16 << 20,
        room=16,
    )(at, block_order, decay_rate, col_moment, views, natural, master_rows, *halves, *peers)
    return (update_rows, new_master, new_row.reshape(-1), new_col, next_output)


def solution(mesh):
    in_specs = (
        P(),
        P(),
        P(("group", "shard"), None, None, None, None),
        P(("group", "shard"), None),
        P(("group", "shard"), None),
        P(),
        P("shard", None),
        P("shard"),
        P(),
        P(("group", "shard"), None, None, None, None),
    )
    out_specs = (P("shard", None), P("shard", None), P("shard"), P(), P(("group", "shard"), None))
    body = shards if (mesh.shape["group"], mesh.shape["shard"]) == (4, 8) else general_shards
    return jax.shard_map(body, mesh=mesh, in_specs=in_specs, out_specs=out_specs, check_vma=False)
```

```python
import functools
import jax
import jax.numpy as jnp
from jax import lax
from jax.experimental import pallas as pl
from jax.experimental.pallas import tpu as pltpu
from jax.sharding import PartitionSpec as P

CI = 256
CO = 256
BLK = 32
FR = 2
HW = 16
NB3 = 216
NB = 224


learn_rate = 0.002
decay_power = 0.8


def silu_slope(values):
    sigma = jax.nn.sigmoid(values)
    return sigma * (1.0 + values * (1.0 - sigma))


def tap_views(frames):
    views = []
    for frame_off in range(3):
        for row_off in range(3):
            for col_off in range(3):
                window = frames[
                    frame_off : frame_off + FR, row_off : row_off + HW, col_off : col_off + HW, :
                ]
                views.append(window.reshape(FR * HW * HW, CI))
    return views


def contract_rows(left, right):
    return lax.dot_general(
        left, right, (((0,), (0,)), ((), ())), preferred_element_type=jnp.float32
    )


def kernel_sums(values, is_small):
    large_part = jnp.sum(jnp.where(is_small[:, None], 0.0, values), axis=0)
    small_part = jnp.sum(jnp.where(is_small[:, None], values, 0.0), axis=0)
    return jnp.stack([large_part, small_part])


def general_shards(
    step_count,
    block_order,
    saved_tiles,
    pre_act,
    grad_output,
    pointwise_live,
    master_rows,
    row_moment,
    col_moment,
    next_tiles,
):
    pre_float = pre_act.astype(jnp.float32)
    activation = jax.nn.silu(pre_float).astype(jnp.bfloat16)
    grad_act = lax.dot_general(
        grad_output, pointwise_live, (((1,), (1,)), ((), ())), preferred_element_type=jnp.float32
    )
    grad_pre = (grad_act * silu_slope(pre_float)).astype(jnp.bfloat16)
    pieces = [contract_rows(view, grad_pre) for view in tap_views(saved_tiles[0])]
    pieces.append(contract_rows(activation, grad_output))
    own_term = jnp.concatenate(pieces, axis=0).astype(jnp.bfloat16)
    total_rows = NB * BLK
    stored = jnp.take(own_term.reshape(NB, BLK, CO), block_order, axis=0).reshape(total_rows, CO)
    own_rows = master_rows.shape[0]
    partial_value = lax.psum_scatter(stored, "shard", scatter_dimension=0, tiled=True).astype(
        jnp.float32
    )
    gradient = lax.psum(partial_value, "group")
    owner = lax.axis_index("shard")
    own_count = own_rows // BLK
    own_blocks = lax.dynamic_slice_in_dim(block_order, owner * own_count, own_count)
    is_small = jnp.repeat(own_blocks >= NB3, BLK, total_repeat_length=own_rows)
    decay_rate = 1.0 - step_count.astype(jnp.float32)[0] ** (-decay_power)
    counts = jnp.array([27 * CI, CO], jnp.float32)
    squares = gradient * gradient
    new_row = decay_rate * row_moment + (1.0 - decay_rate) * jnp.mean(squares, axis=1)
    col_part = kernel_sums(squares, is_small)
    row_part = kernel_sums(new_row[:, None], is_small)[:, 0]
    weighted = kernel_sums(squares / new_row[:, None], is_small)
    col_total, weight_total, row_total = lax.psum((col_part, weighted, row_part), "shard")
    new_col = decay_rate * col_moment + (1.0 - decay_rate) * col_total / counts[:, None]
    row_mean = row_total / counts
    col_rows = jnp.where(is_small[:, None], new_col[1], new_col[0])
    mean_rows = jnp.where(is_small, row_mean[1], row_mean[0])
    scaled = gradient / jnp.sqrt(new_row[:, None] * col_rows / mean_rows[:, None])
    square_total = row_mean * jnp.sum(weight_total / new_col, axis=1)
    clip_factor = jnp.maximum(1.0, jnp.sqrt(square_total / (counts * CO)))
    update_rows = scaled / jnp.where(is_small, clip_factor[1], clip_factor[0])[:, None]
    new_master = master_rows - learn_rate * update_rows
    weights_low = new_master.astype(jnp.bfloat16)
    gathered = lax.all_gather(weights_low, "shard", axis=0, tiled=True)
    inverse = jnp.zeros((NB,), jnp.int32).at[block_order].set(jnp.arange(NB, dtype=jnp.int32))
    natural = jnp.take(gathered.reshape(NB, BLK, CO), inverse, axis=0).reshape(total_rows, CO)
    spatial = natural[: 27 * CI].reshape(27, CI, CO)
    pointwise = natural[27 * CI :]
    hidden_sum = jnp.zeros((FR * HW * HW, CO), jnp.float32)
    for index_tap, view in enumerate(tap_views(next_tiles[0])):
        hidden_sum = hidden_sum + jnp.dot(
            view, spatial[index_tap], preferred_element_type=jnp.float32
        )
    hidden_act = jax.nn.silu(hidden_sum).astype(jnp.bfloat16)
    next_output = jnp.dot(hidden_act, pointwise, preferred_element_type=jnp.float32).astype(
        jnp.bfloat16
    )
    return (update_rows, new_master, new_row, new_col, next_output)


AXES = ("group", "shard")
SLOTS = 14
PIX = FR * HW * HW
SHIFTED = (FR + 2) * (HW + 2) * HW
LOW = jnp.bfloat16
WIDE = jnp.float32
VMEM = pl.BlockSpec(memory_space=pltpu.VMEM)
SMEM = pl.BlockSpec(memory_space=pltpu.SMEM)
HBM = pl.BlockSpec(memory_space=pl.ANY)
MASK_CORE, MASK_NEAR, MASK_FAR, MASK_X, MASK_Y = 1, 2, 4, 8, 16
PARTS = ((0, 5, (0, 1, 2)), (5, 5, (1, 2, 0)), (10, 4, (2, 0, 1)))
MASKS = (MASK_X, MASK_Y, MASK_NEAR)


def swap(value, mask):
    return lax.ppermute(value, AXES, [(at, at ^ mask) for at in range(32)])


def call(kernel, outs, in_specs, scratch=(), flops=0, moved=0, room=8):
    return pl.pallas_call(
        kernel,
        out_shape=[jax.ShapeDtypeStruct(shape, dtype) for shape, dtype in outs],
        in_specs=in_specs,
        out_specs=[VMEM] * len(outs),
        scratch_shapes=list(scratch),
        compiler_params=pltpu.CompilerParams(vmem_limit_bytes=room << 20),
        cost_estimate=pl.CostEstimate(flops=flops, bytes_accessed=moved, transcendentals=0),
    )


def store_shifted(tile, out):
    for col_off in range(3):
        out[col_off] = tile[:, :, col_off : col_off + HW, :].reshape(SHIFTED, CI)


def shift_kernel(tile, out):
    store_shifted(tile, out)


def slope_of(pre, grad, pointwise):
    grad_act = lax.dot_general(
        grad, pointwise, (((1,), (1,)), ((), ())), preferred_element_type=WIDE
    )
    return (grad_act * silu_slope(pre.astype(WIDE))).astype(LOW)


def own_kernel(tile, pre, grad, pointwise, views, slopes, acts):
    store_shifted(tile, views)
    slopes[...] = slope_of(pre[...], grad[...], pointwise[...])
    acts[...] = jax.nn.silu(pre[...].astype(WIDE)).astype(LOW)


def term_kernel(
    at, views, slopes, acts, grad, tile_peer, pre_peer, grad_peer, pointwise,
    keep_one, send_one, keep_two, send_two, keep_three, send_three,
    views_peer, both_slopes, both_acts, both_grads, staged,
):
    core = at[4]
    store_shifted(tile_peer, views_peer)
    both_slopes[:PIX] = slopes[...]
    both_slopes[PIX:] = slope_of(pre_peer[...], grad_peer[...], pointwise[...])
    outs = ((keep_one, send_one), (keep_two, send_two), (keep_three, send_three))

    def put(slot, total):
        value = total.astype(LOW)
        for (first, count, order), (keep, send) in zip(PARTS, outs):
            if first <= slot < first + count:
                for mine in range(2):

                    @pl.when(at[order[0]] == mine)
                    def _():
                        keep[slot - first] = value[mine * 128 : mine * 128 + 128]
                        send[slot - first] = value[128 - mine * 128 : 256 - mine * 128]

    def tap_rows(tap):
        frame_off, row_off, col_off = tap // 9, lax.rem(tap // 3, 3), lax.rem(tap, 3)
        parts = []
        for ref in (views, views_peer):
            for frame in range(FR):
                start = pl.multiple_of(((frame + frame_off) * (HW + 2) + row_off) * HW, HW)
                parts.append(ref[col_off, pl.ds(start, HW * HW), :])
        return jnp.concatenate(parts, axis=0)

    for slot in range(SLOTS - 1):
        put(slot, contract_rows(tap_rows(core * SLOTS + slot), both_slopes[...]))

    @pl.when(core == 0)
    def _():
        staged[...] = contract_rows(tap_rows(SLOTS - 1), both_slopes[...])

    @pl.when(core == 1)
    def _():
        both_acts[:PIX] = acts[...]
        both_acts[PIX:] = jax.nn.silu(pre_peer[...].astype(WIDE)).astype(LOW)
        both_grads[:PIX] = grad[...]
        both_grads[PIX:] = grad_peer[...]
        staged[...] = contract_rows(both_acts[...], both_grads[...])

    put(SLOTS - 1, staged[...])


def fold_kernel(step, at, after, *refs):
    size = 256 >> (step + 1)
    ins, outs = refs[:6], refs[6:]
    for part, (first, count, order) in enumerate(PARTS):
        keep, got = ins[2 * part], ins[2 * part + 1]
        mine = at[order[step] if step < 3 else 3]
        for which, out in ((mine, 0), (1 - mine, 1)):
            rows = pl.ds(pl.multiple_of(which * size, size), size)
            value = (keep[:, rows].astype(WIDE) + got[:, rows].astype(WIDE)).astype(LOW)
            if step < 3:
                outs[2 * part + out][...] = value
            else:
                outs[out][first : first + count] = value


def moment_kernel(at, rate, own, got, row_moment, scaled):
    total = (own[...].astype(WIDE) + got[...].astype(WIDE)).reshape(SLOTS * 16, CO)
    squares = total * total
    decay = rate[0]
    mean = jnp.sum(squares, axis=1, keepdims=True) * (1.0 / CO)
    new_row = decay * row_moment[...] + (1.0 - decay) * mean
    scaled[:SLOTS] = (total * lax.rsqrt(new_row)).astype(LOW).reshape(SLOTS, 16, CO)
    weighted = squares / new_row
    cut = (SLOTS - 1) * 16
    last_small = at[4] == 1
    rows = []
    for values in (squares, weighted, jnp.broadcast_to(new_row, (SLOTS * 16, CO))):
        large = jnp.sum(values[:cut], axis=0, keepdims=True)
        last = jnp.sum(values[cut:], axis=0, keepdims=True)
        rows.append(large + jnp.where(last_small, 0.0, last))
        rows.append(jnp.where(last_small, last, 0.0))
    spread = jnp.broadcast_to(new_row, (SLOTS * 16, 128))
    spread = jnp.concatenate([spread, jnp.zeros((32, 128), WIDE)], axis=0)
    rows.append(jnp.transpose(spread)[:1])
    rows.append(jnp.zeros((1, CO), WIDE))
    message = jnp.concatenate(rows, axis=0)
    high = message.astype(LOW).astype(WIDE)
    scaled[SLOTS] = jnp.concatenate([high, message - high], axis=0).astype(LOW)


def store_factors(total, decay, col_moment, new_col, factor):
    for kernel in range(2):
        count = 27.0 * CI if kernel == 0 else float(CO)
        col = decay * col_moment[kernel : kernel + 1] + (1.0 - decay) * (
            total[kernel : kernel + 1] / count
        )
        row_mean = total[4 + kernel : 5 + kernel] / count
        square = row_mean * jnp.sum(
            total[2 + kernel : 3 + kernel] / col, axis=1, keepdims=True
        )
        clip = jnp.maximum(1.0, jnp.sqrt(square / (count * CO)))
        new_col[kernel : kernel + 1] = col
        factor[kernel : kernel + 1] = 1.0 / (jnp.sqrt(col / row_mean) * clip)


def stack_kernel(at, own, got, out):
    out[at[2]] = own[...]
    out[1 - at[2]] = got[...]


def line_kernel(at, after, own, got, out_a, out_b):
    for which, piece in ((at[3], own), (1 - at[3], got)):
        for near in range(2):
            rows = piece[near, :SLOTS].reshape(SLOTS * 16, CO)
            out_a[which * 2 + near] = rows[: 3 * BLK]
            out_b[which * 2 + near] = rows[3 * BLK :]


def double_kernel(after, own_a, got_a, own_b, got_b, out_a, out_b):
    out_a[0], out_a[1] = own_a[...], got_a[...]
    out_b[0], out_b[1] = own_b[...], got_b[...]


def order_kernel(at, block_order, *refs):
    pieces, out = refs[:-1], refs[-1]
    count = NB // 8
    quarters = count // 4
    for index, piece in enumerate(pieces):
        flip_core, kind = divmod(index, 4)
        core = at[4] ^ flip_core
        first, blocks = ((0, 3), (0, 3), (3, 4), (3, 4))[kind]
        for away in range(2):
            flip_x = away if kind < 2 else kind - 2
            flip_y = kind if kind < 2 else away
            quarter = (at[1] ^ flip_y) * 2 + (at[0] ^ flip_x)
            for line in range(4):
                for local in range(blocks):
                    block = block_order[
                        (line * 2 + core) * count + quarter * quarters + first + local
                    ]
                    to = pl.ds(pl.multiple_of(block * BLK, BLK), BLK)
                    out[to, :] = piece[away, line, local * BLK : local * BLK + BLK]


def widen_kernel(step, at, after, *refs):
    size = 256 >> (step + 1)
    if step == 3:
        (own, got), outs = refs[:2], refs[2:]
    else:
        ins, outs = refs[:6], refs[6:]
    for part, (first, _, order) in enumerate(PARTS):
        mine = at[order[step] if step < 3 else 3]
        for index, which in enumerate((mine, 1 - mine)):
            rows = pl.ds(pl.multiple_of(which * size, size), size)
            if step == 3:
                value = (own, got)[index][first : first + 5]
            else:
                value = ins[2 * part + index][...]
            outs[part][:, rows] = value
            if step == 1:
                outs[3][first : first + 5, rows] = value


def finish_kernel(
    at, block_order, rate, col_moment, views, natural, master,
    mine, got_one, got_two, got_three, peer, peer_one, peer_two, peer_three,
    update_rows, new_master, new_row, new_col, next_output, scaled, factor, row_table,
):
    core = at[4]
    gots = ((got_one, got_two, got_three), (peer_one, peer_two, peer_three))
    for index, own in enumerate((mine, peer)):
        side = core ^ index
        for (first, _, order), got in zip(PARTS, gots[index]):
            which = at[order[0]]
            rows = pl.ds(pl.multiple_of(which * 128, 128), 128)
            scaled[side, first : first + 5, rows] = own[first : first + 5]
            rows = pl.ds(pl.multiple_of(128 - which * 128, 128), 128)
            scaled[side, first : first + 5, rows] = got[...]
    message = scaled[:, SLOTS].astype(WIDE).reshape(32, 2, 8, CO)
    message = message[:, 0] + message[:, 1]
    store_factors(jnp.sum(message, axis=0), rate[0], col_moment, new_col, factor)
    for index in range(32):
        for half in range(2):
            row_table[index * 2 + half : index * 2 + half + 1] = message[
                index, 6:7, half * 128 : half * 128 + 128
            ]
    large = learn_rate * factor[0:1]
    total = jnp.zeros((PIX, CO), WIDE)
    for tap in range(27):
        frame_off, row_off, col_off = tap // 9, tap // 3 % 3, tap % 3
        step = scaled[tap // SLOTS, tap % SLOTS].astype(WIDE) * large
        weights = natural[tap * CI : tap * CI + CI].astype(WIDE) - step
        starts = [((frame + frame_off) * (HW + 2) + row_off) * HW for frame in range(FR)]
        window = jnp.concatenate(
            [views[col_off, start : start + HW * HW, :] for start in starts], axis=0
        )
        total = total + jnp.dot(window, weights.astype(LOW), preferred_element_type=WIDE)
    small = learn_rate * factor[1:2]
    weights = natural[27 * CI :].astype(WIDE) - scaled[1, SLOTS - 1].astype(WIDE) * small
    next_act = jax.nn.silu(total).astype(LOW)
    next_output[...] = jnp.dot(
        next_act, weights.astype(LOW), preferred_element_type=WIDE
    ).astype(LOW)

    owner = at[3] * 4 + at[2] * 2 + core
    lane = lax.broadcasted_iota(jnp.int32, (1, 128), 1)
    for line in range(7):
        values = jnp.zeros((1, 128), WIDE)
        for part in range(4):
            local = line * 4 + part
            block = block_order[owner * (NB // 8) + local]
            side, slot, place = block // (8 * SLOTS), lax.rem(block // 8, SLOTS), lax.rem(block, 8)
            one, two, three = place // 4, lax.rem(place // 2, 2), lax.rem(place, 2)
            sender = jnp.where(
                slot < 5,
                three * 8 + one * 4 + two * 2,
                jnp.where(slot < 10, two * 8 + three * 4 + one * 2, place * 2),
            )
            chosen = jnp.where(block >= NB3, factor[1:2], factor[0:1])
            rows = slice(local * BLK, local * BLK + BLK)
            start = pl.multiple_of(place * BLK, BLK)
            update = scaled[side, slot, pl.ds(start, BLK), :].astype(WIDE) * chosen
            update_rows[rows, :] = update
            new_master[rows, :] = master[rows, :] - learn_rate * update
            for half in range(2):
                at_row = (side * 16 + sender + half) * 2 + slot // 8
                to = part * 32 + half * 16
                turn = lax.rem(128 + to - lax.rem(slot, 8) * 16, 128)
                turned = pltpu.roll(row_table[pl.ds(at_row, 1), :], turn, 1)
                values = jnp.where((lane >= to) & (lane < to + 16), turned, values)
        new_row[line : line + 1] = values


def shards(
    step_count,
    block_order,
    saved_tiles,
    pre_act,
    grad_output,
    pointwise_live,
    master_rows,
    row_moment,
    col_moment,
    next_tiles,
):
    group, shard = lax.axis_index("group"), lax.axis_index("shard")
    axis_y, axis_x = group // 2, group % 2
    far, near, core = shard // 4, shard // 2 % 2, shard % 2
    at = jnp.stack([axis_x, axis_y, near, far, core]).astype(jnp.int32)
    decay_rate = 1.0 - step_count.astype(WIDE) ** (-decay_power)

    tile_peer = swap(saved_tiles, MASK_CORE)
    pre_peer = swap(pre_act, MASK_CORE)
    grad_peer = swap(grad_output, MASK_CORE)
    own_views, slopes, acts = call(
        own_kernel,
        [((3, SHIFTED, CI), LOW), ((PIX, CO), LOW), ((PIX, CO), LOW)],
        [VMEM] * 4,
        moved=4 << 20,
    )(saved_tiles[0], pre_act, grad_output, pointwise_live)

    quarter = lax.dynamic_slice_in_dim(master_rows, group * (SLOTS * 16), SLOTS * 16)
    values = jnp.pad(row_moment.reshape(7, 128), ((0, 9), (0, 0)))
    high = lax.reduce_precision(values, 8, 7)
    values = jnp.concatenate([high, values - high], axis=1)
    packed = jnp.concatenate([quarter, values], axis=0).astype(LOW).reshape(SLOTS + 1, 16, CO)
    pair = call(stack_kernel, [((2, SLOTS + 1, 16, CO), LOW)], [SMEM] + [VMEM] * 2)(
        at, packed, swap(packed, MASK_NEAR)
    )[0]
    pair_far = swap(pair, MASK_FAR)
    moment_line = jnp.stack([pair[:, SLOTS], pair_far[:, SLOTS]])
    moment_all = jnp.stack([moment_line, swap(moment_line, MASK_CORE)])[:, :, :, :7].astype(WIDE)
    moment_all = (moment_all[..., :128] + moment_all[..., 128:]).reshape(2, 2, 2, 896)
    moment_stored = moment_all[jnp.arange(2) ^ core][:, jnp.arange(2) ^ far]
    moment_stored = jnp.transpose(moment_stored, (1, 2, 0, 3)).reshape(NB, BLK)
    inverse = jnp.zeros((NB,), jnp.int32).at[block_order].set(jnp.arange(NB, dtype=jnp.int32))
    moment_natural = jnp.take(moment_stored, inverse, axis=0).reshape(2, SLOTS, 16, 16)
    moment_natural = lax.dynamic_index_in_dim(moment_natural, core, 0, False)
    place = (axis_x, axis_y, near)
    own_moment = [
        lax.dynamic_index_in_dim(
            moment_natural[first : first + count],
            place[order[0]] * 8 + place[order[1]] * 4 + place[order[2]] * 2 + far,
            1,
            False,
        )
        for first, count, order in PARTS
    ]
    own_moment = jnp.concatenate(own_moment, axis=0).reshape(SLOTS * 16, 1)
    views = call(shift_kernel, [((3, SHIFTED, CI), LOW)], [VMEM], moved=3 << 20)(next_tiles[0])[0]

    sums = call(
        term_kernel,
        [((count, 128, CO), LOW) for _, count, _ in PARTS for _ in range(2)],
        [SMEM] + [VMEM] * 8,
        scratch=[
            pltpu.VMEM((3, SHIFTED, CI), LOW),
            pltpu.VMEM((2 * PIX, CO), LOW),
            pltpu.VMEM((2 * PIX, CO), LOW),
            pltpu.VMEM((2 * PIX, CO), LOW),
            pltpu.VMEM((CI, CO), WIDE),
        ],
        flops=2 * 14 * 1024 * 256 * 256,
        moved=6 << 20,
        room=12,
    )(at, own_views, slopes, acts, grad_output, tile_peer[0], pre_peer, grad_peer, pointwise_live)
    for step in range(1, 4):
        arrived = []
        for part, (_, _, order) in enumerate(PARTS):
            arrived += [sums[2 * part], swap(sums[2 * part + 1], MASKS[order[step - 1]])]
        size = 256 >> (step + 1)
        outs = [((count, size, CO), LOW) for _, count, _ in PARTS for _ in range(2)]
        if step == 3:
            outs = [((SLOTS, size, CO), LOW)] * 2
        after = (pair_far, pair_far, views)[step - 1]
        sums = call(
            functools.partial(fold_kernel, step), outs, [SMEM, HBM] + [VMEM] * 6, moved=1 << 20
        )(at, after, *arrived)

    line_a, line_b = call(
        line_kernel,
        [((4, 3 * BLK, CO), LOW), ((4, 4 * BLK, CO), LOW)],
        [SMEM, HBM] + [VMEM] * 2,
        moved=1 << 20,
    )(at, sums[0], pair, pair_far)
    line_got_a, line_got_b = swap(line_a, MASK_X), swap(line_b, MASK_Y)
    scaled = call(moment_kernel, [((SLOTS + 1, 16, CO), LOW)], [SMEM] * 2 + [VMEM] * 3)(
        at, decay_rate, sums[0], swap(sums[1], MASK_FAR), own_moment
    )[0]
    plane_a, plane_b = call(
        double_kernel,
        [((2, 4, 3 * BLK, CO), LOW), ((2, 4, 4 * BLK, CO), LOW)],
        [HBM] + [VMEM] * 4,
        moved=2 << 20,
    )(scaled, line_a, line_got_a, line_b, line_got_b)
    planes = [plane_a, swap(plane_a, MASK_Y), plane_b, swap(plane_b, MASK_X)]
    planes = planes + [swap(plane, MASK_CORE) for plane in planes]
    natural = call(
        order_kernel, [((NB * BLK, CO), LOW)], [SMEM] * 2 + [VMEM] * 8, moved=8 << 20
    )(at, block_order, *planes)[0]

    pieces = [scaled, swap(scaled, MASK_FAR)]
    for step in range(3, 0, -1):
        size = 256 >> step
        outs = [((5, size, CO), LOW)] * 3
        if step == 1:
            outs = outs + [((SLOTS + 1, size, CO), LOW)]
        after = (natural, at, at)[step - 1]
        joined = call(
            functools.partial(widen_kernel, step), outs, [SMEM, HBM] + [VMEM] * len(pieces)
        )(at, after, *pieces)
        pieces = []
        for part, (_, _, order) in enumerate(PARTS):
            pieces += [joined[part], swap(joined[part], MASKS[order[step - 1]])]
    halves = [joined[3], pieces[1], pieces[3], pieces[5]]
    peers = [swap(half, MASK_CORE) for half in halves]

    update_rows, new_master, new_row, new_col, next_output = call(
        finish_kernel,
        [
            ((NB // 8 * BLK, CO), WIDE),
            ((NB // 8 * BLK, CO), WIDE),
            ((7, 128), WIDE),
            ((2, CO), WIDE),
            ((PIX, CO), LOW),
        ],
        [SMEM] * 3 + [VMEM] * 12,
        scratch=[
            pltpu.VMEM((2, SLOTS + 1, CI, CO), LOW),
            pltpu.VMEM((2, CO), WIDE),
            pltpu.VMEM((64, 128), WIDE),
        ],
        flops=2 * 28 * 512 * 256 * 256,
        moved=16 << 20,
        room=16,
    )(at, block_order, decay_rate, col_moment, views, natural, master_rows, *halves, *peers)
    return (update_rows, new_master, new_row.reshape(-1), new_col, next_output)


def solution(mesh):
    in_specs = (
        P(),
        P(),
        P(("group", "shard"), None, None, None, None),
        P(("group", "shard"), None),
        P(("group", "shard"), None),
        P(),
        P("shard", None),
        P("shard"),
        P(),
        P(("group", "shard"), None, None, None, None),
    )
    out_specs = (P("shard", None), P("shard", None), P("shard"), P(), P(("group", "shard"), None))
    body = shards if (mesh.shape["group"], mesh.shape["shard"]) == (4, 8) else general_shards
    return jax.shard_map(body, mesh=mesh, in_specs=in_specs, out_specs=out_specs, check_vma=False)
```

```python
import functools
import jax
import jax.numpy as jnp
from jax import lax
from jax.experimental import pallas as pl
from jax.experimental.pallas import tpu as pltpu
from jax.sharding import PartitionSpec as P

CI = 256
CO = 256
BLK = 32
FR = 2
HW = 16
NB3 = 216
NB = 224


learn_rate = 0.002
decay_power = 0.8


def silu_slope(values):
    sigma = jax.nn.sigmoid(values)
    return sigma * (1.0 + values * (1.0 - sigma))


def tap_views(frames):
    views = []
    for frame_off in range(3):
        for row_off in range(3):
            for col_off in range(3):
                window = frames[
                    frame_off : frame_off + FR, row_off : row_off + HW, col_off : col_off + HW, :
                ]
                views.append(window.reshape(FR * HW * HW, CI))
    return views


def contract_rows(left, right):
    return lax.dot_general(
        left, right, (((0,), (0,)), ((), ())), preferred_element_type=jnp.float32
    )


def kernel_sums(values, is_small):
    large_part = jnp.sum(jnp.where(is_small[:, None], 0.0, values), axis=0)
    small_part = jnp.sum(jnp.where(is_small[:, None], values, 0.0), axis=0)
    return jnp.stack([large_part, small_part])


def general_shards(
    step_count,
    block_order,
    saved_tiles,
    pre_act,
    grad_output,
    pointwise_live,
    master_rows,
    row_moment,
    col_moment,
    next_tiles,
):
    pre_float = pre_act.astype(jnp.float32)
    activation = jax.nn.silu(pre_float).astype(jnp.bfloat16)
    grad_act = lax.dot_general(
        grad_output, pointwise_live, (((1,), (1,)), ((), ())), preferred_element_type=jnp.float32
    )
    grad_pre = (grad_act * silu_slope(pre_float)).astype(jnp.bfloat16)
    pieces = [contract_rows(view, grad_pre) for view in tap_views(saved_tiles[0])]
    pieces.append(contract_rows(activation, grad_output))
    own_term = jnp.concatenate(pieces, axis=0).astype(jnp.bfloat16)
    total_rows = NB * BLK
    stored = jnp.take(own_term.reshape(NB, BLK, CO), block_order, axis=0).reshape(total_rows, CO)
    own_rows = master_rows.shape[0]
    partial_value = lax.psum_scatter(stored, "shard", scatter_dimension=0, tiled=True).astype(
        jnp.float32
    )
    gradient = lax.psum(partial_value, "group")
    owner = lax.axis_index("shard")
    own_count = own_rows // BLK
    own_blocks = lax.dynamic_slice_in_dim(block_order, owner * own_count, own_count)
    is_small = jnp.repeat(own_blocks >= NB3, BLK, total_repeat_length=own_rows)
    decay_rate = 1.0 - step_count.astype(jnp.float32)[0] ** (-decay_power)
    counts = jnp.array([27 * CI, CO], jnp.float32)
    squares = gradient * gradient
    new_row = decay_rate * row_moment + (1.0 - decay_rate) * jnp.mean(squares, axis=1)
    col_part = kernel_sums(squares, is_small)
    row_part = kernel_sums(new_row[:, None], is_small)[:, 0]
    weighted = kernel_sums(squares / new_row[:, None], is_small)
    col_total, weight_total, row_total = lax.psum((col_part, weighted, row_part), "shard")
    new_col = decay_rate * col_moment + (1.0 - decay_rate) * col_total / counts[:, None]
    row_mean = row_total / counts
    col_rows = jnp.where(is_small[:, None], new_col[1], new_col[0])
    mean_rows = jnp.where(is_small, row_mean[1], row_mean[0])
    scaled = gradient / jnp.sqrt(new_row[:, None] * col_rows / mean_rows[:, None])
    square_total = row_mean * jnp.sum(weight_total / new_col, axis=1)
    clip_factor = jnp.maximum(1.0, jnp.sqrt(square_total / (counts * CO)))
    update_rows = scaled / jnp.where(is_small, clip_factor[1], clip_factor[0])[:, None]
    new_master = master_rows - learn_rate * update_rows
    weights_low = new_master.astype(jnp.bfloat16)
    gathered = lax.all_gather(weights_low, "shard", axis=0, tiled=True)
    inverse = jnp.zeros((NB,), jnp.int32).at[block_order].set(jnp.arange(NB, dtype=jnp.int32))
    natural = jnp.take(gathered.reshape(NB, BLK, CO), inverse, axis=0).reshape(total_rows, CO)
    spatial = natural[: 27 * CI].reshape(27, CI, CO)
    pointwise = natural[27 * CI :]
    hidden_sum = jnp.zeros((FR * HW * HW, CO), jnp.float32)
    for index_tap, view in enumerate(tap_views(next_tiles[0])):
        hidden_sum = hidden_sum + jnp.dot(
            view, spatial[index_tap], preferred_element_type=jnp.float32
        )
    hidden_act = jax.nn.silu(hidden_sum).astype(jnp.bfloat16)
    next_output = jnp.dot(hidden_act, pointwise, preferred_element_type=jnp.float32).astype(
        jnp.bfloat16
    )
    return (update_rows, new_master, new_row, new_col, next_output)


AXES = ("group", "shard")
SLOTS = 14
PIX = FR * HW * HW
SHIFTED = (FR + 2) * (HW + 2) * HW
SLOPES = 3 * SHIFTED
ACTS = SLOPES + PIX
BROUGHT = ACTS + PIX
LOW = jnp.bfloat16
WIDE = jnp.float32
VMEM = pl.BlockSpec(memory_space=pltpu.VMEM)
SMEM = pl.BlockSpec(memory_space=pltpu.SMEM)
HBM = pl.BlockSpec(memory_space=pl.ANY)
MASK_CORE, MASK_NEAR, MASK_FAR, MASK_X, MASK_Y = 1, 2, 4, 8, 16
PARTS = ((0, 5, (0, 1, 2)), (5, 5, (1, 2, 0)), (10, 4, (2, 0, 1)))
MASKS = (MASK_X, MASK_Y, MASK_NEAR)


def swap(value, mask):
    return lax.ppermute(value, AXES, [(at, at ^ mask) for at in range(32)])


def call(kernel, outs, in_specs, scratch=(), flops=0, moved=0, room=8, pin=True):
    return pl.pallas_call(
        kernel,
        out_shape=[(pltpu.VMEM if pin else jax.ShapeDtypeStruct)(*out) for out in outs],
        in_specs=in_specs,
        out_specs=[VMEM] * len(outs),
        scratch_shapes=list(scratch),
        compiler_params=pltpu.CompilerParams(vmem_limit_bytes=room << 20),
        cost_estimate=pl.CostEstimate(flops=flops, bytes_accessed=moved, transcendentals=0),
    )


def far_away(array):
    return pltpu.with_memory_space_constraint(array, pltpu.HBM)


def store_shifted(tile, out):
    for col_off in range(3):
        out[col_off * SHIFTED : (col_off + 1) * SHIFTED] = tile[
            :, :, col_off : col_off + HW, :
        ].reshape(SHIFTED, CI)


def shift_kernel(tile, out):
    store_shifted(tile, out)


def slope_of(pre, grad, pointwise):
    grad_act = lax.dot_general(
        grad, pointwise, (((1,), (1,)), ((), ())), preferred_element_type=WIDE
    )
    return (grad_act * silu_slope(pre.astype(WIDE))).astype(LOW)


def fetch(pairs, arrived):
    copies = [
        pltpu.make_async_copy(source, target, arrived.at[index])
        for index, (source, target) in enumerate(pairs)
    ]
    for copy in copies:
        copy.start()
    return copies


def own_kernel(at, tile, pre_far, grad_far, pointwise_far, brought, pre, grad, pointwise, arrived):
    copies = fetch(((pre_far, pre), (grad_far, grad), (pointwise_far, pointwise)), arrived)
    store_shifted(tile, brought)
    for copy in copies:
        copy.wait()
    brought[SLOPES:ACTS] = slope_of(pre[...], grad[...], pointwise[...])
    brought[ACTS:] = jax.nn.silu(pre[...].astype(WIDE)).astype(LOW)


def pack_kernel(at, after, master_far, row_moment_far, packed, master, row_moment, arrived):
    quarter = pl.multiple_of((at[1] * 2 + at[0]) * (SLOTS * 16), SLOTS * 16)
    row_moment[...] = jnp.zeros((16, 128), WIDE)
    copies = fetch(
        (
            (master_far.at[pl.ds(quarter, SLOTS * 16), :], master),
            (row_moment_far, row_moment.at[pl.ds(0, 7), :]),
        ),
        arrived,
    )
    for copy in copies:
        copy.wait()
    packed[:SLOTS] = master[...].astype(LOW).reshape(SLOTS, 16, CO)
    high = row_moment[...].astype(LOW).astype(WIDE)
    packed[SLOTS] = jnp.concatenate([high, row_moment[...] - high], axis=1).astype(LOW)


def term_kernel(
    at, own, tile_peer, pre_peer, grad_peer, grad_far, pointwise_far,
    keep, send_one, send_two, send_three, peer, rights, pointwise, arrived,
):
    core = at[4]
    copies = fetch(((grad_far, rights.at[1, pl.ds(0, PIX), :]), (pointwise_far, pointwise)), arrived)
    store_shifted(tile_peer, peer)
    peer[ACTS:] = jax.nn.silu(pre_peer[...].astype(WIDE)).astype(LOW)
    for copy in copies:
        copy.wait()
    peer[SLOPES:ACTS] = slope_of(pre_peer[...], grad_peer[...], pointwise[...])
    rights[0, :PIX] = own[SLOPES:ACTS]
    rights[0, PIX:] = peer[SLOPES:ACTS]
    rights[1, PIX:] = grad_peer[...]
    for slot in range(SLOTS):
        tap = core * SLOTS + slot
        frame_off, row_off, col_off = tap // 9, lax.rem(tap // 3, 3), lax.rem(tap, 3)
        pieces = []
        for ref in (own, peer):
            for frame in range(FR):
                start = col_off * SHIFTED + ((frame + frame_off) * (HW + 2) + row_off) * HW
                if slot == SLOTS - 1:
                    start = jnp.where(core == 0, start, ACTS + frame * HW * HW)
                pieces.append(ref[pl.ds(pl.multiple_of(start, HW), HW * HW), :])
        right = rights[core] if slot == SLOTS - 1 else rights[0]
        total = contract_rows(jnp.concatenate(pieces, axis=0), right)
        for (first, count, order), send in zip(PARTS, (send_one, send_two, send_three)):
            if first <= slot < first + count:
                low, high, at_low = total[:128], total[128:], at[order[0]] == 0
                keep[slot] = jnp.where(at_low, low, high).astype(LOW)
                send[slot - first] = jnp.where(at_low, high, low).astype(LOW)


def fold_kernel(step, skip, at, *refs):
    size = 256 >> (step + 1)
    refs = refs[skip:]
    keep, gots, stay, sends = refs[0], refs[1:4], refs[4], refs[5:]
    for part, (first, count, order) in enumerate(PARTS):
        mine = at[order[step] if step < 3 else 3]
        here = slice(first, first + count)
        for which, out in ((mine, 0), (1 - mine, 1)):
            rows = pl.ds(pl.multiple_of(which * size, size), size)
            value = keep[here, rows] + gots[part][:, rows]
            if out == 0:
                stay[here] = value
            elif step < 3:
                sends[part][...] = value
            else:
                sends[0][here] = value


def moment_kernel(at, rate, own, got, moments, scaled):
    total = (own[...].astype(WIDE) + got[...].astype(WIDE)).reshape(SLOTS * 16, CO)
    squares = total * total
    decay = rate[0]
    mean = jnp.sum(squares, axis=1, keepdims=True) * (1.0 / CO)
    row_moment = jnp.concatenate([moments[:, slot : slot + 1] for slot in range(SLOTS)], axis=0)
    new_row = decay * row_moment + (1.0 - decay) * mean
    scaled[:SLOTS] = (total * lax.rsqrt(new_row)).astype(LOW).reshape(SLOTS, 16, CO)
    weighted = squares / new_row
    cut = (SLOTS - 1) * 16
    last_small = at[4] == 1
    rows = []
    for values in (squares, weighted, jnp.broadcast_to(new_row, (SLOTS * 16, CO))):
        large = jnp.sum(values[:cut], axis=0, keepdims=True)
        last = jnp.sum(values[cut:], axis=0, keepdims=True)
        rows.append(large + jnp.where(last_small, 0.0, last))
        rows.append(jnp.where(last_small, last, 0.0))
    spread = jnp.broadcast_to(new_row, (SLOTS * 16, 128))
    spread = jnp.concatenate([spread, jnp.zeros((32, 128), WIDE)], axis=0)
    rows.append(jnp.transpose(spread)[:1])
    rows.append(jnp.zeros((1, CO), WIDE))
    message = jnp.concatenate(rows, axis=0)
    high = message.astype(LOW).astype(WIDE)
    scaled[SLOTS] = jnp.concatenate([high, message - high], axis=0).astype(LOW)


def store_factors(total, decay, col_moment, new_col, factor):
    for kernel in range(2):
        count = 27.0 * CI if kernel == 0 else float(CO)
        col = decay * col_moment[kernel : kernel + 1] + (1.0 - decay) * (
            total[kernel : kernel + 1] / count
        )
        row_mean = total[4 + kernel : 5 + kernel] / count
        square = row_mean * jnp.sum(
            total[2 + kernel : 3 + kernel] / col, axis=1, keepdims=True
        )
        clip = jnp.maximum(1.0, jnp.sqrt(square / (count * CO)))
        new_col[kernel : kernel + 1] = col
        factor[kernel : kernel + 1] = 1.0 / (jnp.sqrt(col / row_mean) * clip)


def stack_kernel(at, after, own, got, out):
    out[at[2]] = own[...]
    out[1 - at[2]] = got[...]


def line_kernel(at, after, own, got, out_a, out_b):
    for which, piece in ((at[3], own), (1 - at[3], got)):
        for near in range(2):
            rows = piece[near, :SLOTS].reshape(SLOTS * 16, CO)
            out_a[which * 2 + near] = rows[: 3 * BLK]
            out_b[which * 2 + near] = rows[3 * BLK :]


def gather_moments_kernel(at, own, got, out):
    for which, piece in ((at[3], own), (1 - at[3], got)):
        for near in range(2):
            out[which * 2 + near] = piece[near, SLOTS]


def moments_kernel(at, block_order, mine, peer, out, table, rows, inverse):
    core = at[4]
    for side, ref in enumerate((mine, peer)):
        for line in range(4):
            values = ref[line].astype(WIDE)
            values = values[:, :128] + values[:, 128:]
            table[pl.ds(pl.multiple_of((line * 2 + (core ^ side)) * 8, 8), 8), :] = values[:8]

    def invert(stored, carry):
        inverse[block_order[stored]] = stored
        return carry

    lax.fori_loop(0, NB, invert, 0, unroll=8)
    rows[...] = jnp.zeros((128, 128), WIDE)
    for first, count, order in PARTS:
        place = at[order[0]] * 4 + at[order[1]] * 2 + at[order[2]]
        for slot in range(first, first + count):
            stored = inverse[(core * SLOTS + slot) * 8 + place]
            owner, local = stored // (NB // 8), lax.rem(stored, NB // 8)
            row = table[pl.ds(owner * 8 + local // 4, 1), :]
            turn = lax.rem(128 - lax.rem(local, 4) * BLK - at[3] * 16, 128)
            rows[slot : slot + 1] = pltpu.roll(row, turn, 1)
    out[...] = jnp.transpose(rows[...])[:16]


def double_kernel(after, own_a, got_a, own_b, got_b, out_a, out_b):
    out_a[0], out_a[1] = own_a[...], got_a[...]
    out_b[0], out_b[1] = own_b[...], got_b[...]


def merge_kernel(after, *refs):
    pieces, out = refs[:-1], refs[-1]
    first = 0
    for kind, piece in enumerate(pieces):
        count = piece.shape[2]
        out[kind % 2, :, :, first : first + count] = piece[...]
        first += count * (kind % 2)


def order_kernel(at, block_order, mine, peer, out):
    count = NB // 8
    quarters = count // 4
    for flip_core, piece in enumerate((mine, peer)):
        core = at[4] ^ flip_core
        for kind in range(2):
            for away in range(2):
                for local in range(quarters):
                    in_a = local < 3
                    flip_x, flip_y = (away, kind) if in_a else (kind, away)
                    quarter = (at[1] ^ flip_y) * 2 + (at[0] ^ flip_x)
                    for line in range(4):
                        block = block_order[(line * 2 + core) * count + quarter * quarters + local]
                        to = pl.ds(pl.multiple_of(block * BLK, BLK), BLK)
                        out[to, :] = piece[kind, away, line, local * BLK : local * BLK + BLK]


def widen_kernel(step, at, after, *refs):
    size = 256 >> (step + 1)
    if step == 3:
        (own, got), outs = refs[:2], refs[2:]
    else:
        ins, outs = refs[:6], refs[6:]
    for part, (first, _, order) in enumerate(PARTS):
        mine = at[order[step] if step < 3 else 3]
        for index, which in enumerate((mine, 1 - mine)):
            rows = pl.ds(pl.multiple_of(which * size, size), size)
            if step == 3:
                value = (own, got)[index][first : first + 5]
            else:
                value = ins[2 * part + index][...]
            if step == 0:
                outs[0][first : first + 5, rows] = value
            else:
                outs[part][:, rows] = value


def window(views, tap):
    frame_off, row_off, col_off = tap // 9, lax.rem(tap // 3, 3), lax.rem(tap, 3)
    parts = []
    for frame in range(FR):
        start = col_off * SHIFTED + ((frame + frame_off) * (HW + 2) + row_off) * HW
        parts.append(views[pl.ds(pl.multiple_of(start, HW), HW * HW), :])
    return jnp.concatenate(parts, axis=0)


def old_hidden_kernel(views, natural, hidden):
    total = jnp.zeros((PIX, CO), WIDE)
    for tap in range(27):
        weights = natural[tap * CI : tap * CI + CI]
        total = total + jnp.dot(window(views, tap), weights, preferred_element_type=WIDE)
    hidden[...] = total


def add_taps(views, scaled, core):
    total = jnp.zeros((PIX, CO), WIDE)
    for slot in range(SLOTS):
        tap = jnp.minimum(core * SLOTS + slot, 26)
        weights = scaled[slot]
        if slot == SLOTS - 1:
            weights = jnp.where(core == 0, weights.astype(WIDE), 0.0).astype(LOW)
        total = total + jnp.dot(window(views, tap), weights, preferred_element_type=WIDE)
    return total


def half_hidden_kernel(at, views, scaled, hidden):
    hidden[...] = add_taps(views, scaled, at[4])


def finish_kernel(
    at, block_order, rate, col_moment, views, natural, master, mine, peer, old, own_part,
    update_rows, new_master, new_row, new_col, next_output, factor, row_table,
):
    core = at[4]
    total = jnp.zeros((8, CO), WIDE)
    for side, piece in enumerate((mine, peer)):
        message = piece[SLOTS].astype(WIDE).reshape(16, 2, 8, CO)
        message = message[:, 0] + message[:, 1]
        total = total + jnp.sum(message, axis=0)
        for index in range(16):
            for half in range(2):
                to = (side * 16 + index) * 2 + half
                row_table[to : to + 1] = message[index, 6:7, half * 128 : half * 128 + 128]
    store_factors(total, rate[0], col_moment, new_col, factor)
    change = own_part[...] + add_taps(views, peer, 1 - core)
    hidden = old[...] - (learn_rate * factor[0:1]) * change
    small = jnp.where(core == 1, mine[SLOTS - 1].astype(WIDE), peer[SLOTS - 1].astype(WIDE))
    weights = natural[27 * CI :].astype(WIDE) - small * (learn_rate * factor[1:2])
    next_output[...] = jnp.dot(
        jax.nn.silu(hidden).astype(LOW), weights.astype(LOW), preferred_element_type=WIDE
    ).astype(LOW)

    owner = at[3] * 4 + at[2] * 2 + core
    lane = lax.broadcasted_iota(jnp.int32, (1, 128), 1)
    for line in range(7):
        values = jnp.zeros((1, 128), WIDE)
        for part in range(4):
            local = line * 4 + part
            block = block_order[owner * (NB // 8) + local]
            side = (block // (8 * SLOTS)) ^ core
            slot, place = lax.rem(block // 8, SLOTS), lax.rem(block, 8)
            one, two, three = place // 4, lax.rem(place // 2, 2), lax.rem(place, 2)
            sender = jnp.where(
                slot < 5,
                three * 8 + one * 4 + two * 2,
                jnp.where(slot < 10, two * 8 + three * 4 + one * 2, place * 2),
            )
            chosen = jnp.where(block >= NB3, factor[1:2], factor[0:1])
            rows = slice(local * BLK, local * BLK + BLK)
            there = pl.ds(pl.multiple_of(place * BLK, BLK), BLK)
            value = jnp.where(
                side == 0, mine[slot, there, :].astype(WIDE), peer[slot, there, :].astype(WIDE)
            )
            update = value * chosen
            update_rows[rows, :] = update
            new_master[rows, :] = master[rows, :] - learn_rate * update
            for half in range(2):
                at_row = (side * 16 + sender + half) * 2 + slot // 8
                to = part * 32 + half * 16
                turn = lax.rem(128 + to - lax.rem(slot, 8) * 16, 128)
                turned = pltpu.roll(row_table[pl.ds(at_row, 1), :], turn, 1)
                values = jnp.where((lane >= to) & (lane < to + 16), turned, values)
        new_row[line : line + 1] = values


def shards(
    step_count,
    block_order,
    saved_tiles,
    pre_act,
    grad_output,
    pointwise_live,
    master_rows,
    row_moment,
    col_moment,
    next_tiles,
):
    group, shard = lax.axis_index("group"), lax.axis_index("shard")
    axis_y, axis_x = group // 2, group % 2
    far, near, core = shard // 4, shard // 2 % 2, shard % 2
    at = jnp.stack([axis_x, axis_y, near, far, core]).astype(jnp.int32)
    decay_rate = 1.0 - step_count.astype(WIDE) ** (-decay_power)

    tile_peer = swap(saved_tiles, MASK_CORE)
    pre_peer = swap(pre_act, MASK_CORE)
    grad_peer = swap(grad_output, MASK_CORE)
    rows_far = [far_away(array) for array in (pre_act, grad_output, pointwise_live)]
    brought = call(
        own_kernel,
        [((BROUGHT, CI), LOW)],
        [SMEM, VMEM] + [HBM] * 3,
        scratch=[
            pltpu.VMEM((PIX, CO), LOW),
            pltpu.VMEM((PIX, CO), LOW),
            pltpu.VMEM((CO, CO), LOW),
            pltpu.SemaphoreType.DMA((3,)),
        ],
        moved=4 << 20,
    )(at, saved_tiles[0], *rows_far)[0]

    keep, *sends = call(
        term_kernel,
        [((SLOTS, 128, CO), LOW)] + [((count, 128, CO), LOW) for _, count, _ in PARTS],
        [SMEM] + [VMEM] * 4 + [HBM] * 2,
        scratch=[
            pltpu.VMEM((BROUGHT, CI), LOW),
            pltpu.VMEM((2, 2 * PIX, CO), LOW),
            pltpu.VMEM((CO, CO), LOW),
            pltpu.SemaphoreType.DMA((2,)),
        ],
        flops=2 * 14 * 1024 * 256 * 256,
        moved=6 << 20,
        room=12,
    )(at, brought, tile_peer[0], pre_peer, grad_peer, *rows_far[1:])

    packed = call(
        pack_kernel,
        [((SLOTS + 1, 16, CO), LOW)],
        [SMEM] + [HBM] * 3,
        scratch=[
            pltpu.VMEM((SLOTS * 16, CO), WIDE),
            pltpu.VMEM((16, 128), WIDE),
            pltpu.SemaphoreType.DMA((2,)),
        ],
    )(at, keep, far_away(master_rows), far_away(row_moment.reshape(7, 128)))[0]
    packed_near = swap(packed, MASK_NEAR)
    views = call(shift_kernel, [((3 * SHIFTED, CI), LOW)], [VMEM], moved=3 << 20)(next_tiles[0])[0]

    for step in range(1, 4):
        gots = [
            swap(send, MASKS[order[step - 1]]) for send, (_, _, order) in zip(sends, PARTS)
        ]
        if step == 1:
            pair = call(
                stack_kernel,
                [((2, SLOTS + 1, 16, CO), LOW)],
                [SMEM, HBM] + [VMEM] * 2,
                moved=1 << 20,
            )(at, gots[2], packed, packed_near)[0]
            pair_far = swap(pair, MASK_FAR)
        size = 256 >> (step + 1)
        outs = [((SLOTS, size, CO), LOW)] + [((count, size, CO), LOW) for _, count, _ in PARTS]
        if step == 3:
            outs = outs[:1] * 2
        after = ([], [pair_far], [line_a, line_b, views] if step == 3 else [])[step - 1]
        keep, *sends = call(
            functools.partial(fold_kernel, step, len(after)),
            outs,
            [SMEM] + [HBM] * len(after) + [VMEM] * 4,
            moved=1 << 20,
        )(at, *after, keep, *gots)
        if step == 2:
            line_a, line_b = call(
                line_kernel,
                [((4, 3 * BLK, CO), LOW), ((4, 4 * BLK, CO), LOW)],
                [SMEM, HBM] + [VMEM] * 2,
                moved=1 << 20,
            )(at, keep, pair, pair_far)
    line_got_a, line_got_b = swap(line_a, MASK_X), swap(line_b, MASK_Y)
    moments = call(gather_moments_kernel, [((4, 16, CO), LOW)], [SMEM] + [VMEM] * 2)(
        at, pair, pair_far
    )[0]
    own_moment = call(
        moments_kernel,
        [((16, 128), WIDE)],
        [SMEM] * 2 + [VMEM] * 2,
        scratch=[
            pltpu.VMEM((64, 128), WIDE),
            pltpu.VMEM((128, 128), WIDE),
            pltpu.SMEM((NB,), jnp.int32),
        ],
    )(at, block_order, moments, swap(moments, MASK_CORE))[0]
    scaled = call(moment_kernel, [((SLOTS + 1, 16, CO), LOW)], [SMEM] * 2 + [VMEM] * 3)(
        at, decay_rate, keep, swap(sends[0], MASK_FAR), own_moment
    )[0]
    plane_a, plane_b = call(
        double_kernel,
        [((2, 4, 3 * BLK, CO), LOW), ((2, 4, 4 * BLK, CO), LOW)],
        [HBM] + [VMEM] * 4,
        moved=2 << 20,
    )(keep, line_a, line_got_a, line_b, line_got_b)
    planes = [plane_a, swap(plane_a, MASK_Y), plane_b, swap(plane_b, MASK_X)]

    pieces = [scaled, swap(scaled, MASK_FAR)]
    after = at
    for step in range(3, -1, -1):
        size = 256 >> step
        outs = [((5, size, CO), LOW)] * 3 if step > 0 else [((SLOTS + 1, size, CO), LOW)]
        joined = call(
            functools.partial(widen_kernel, step), outs, [SMEM, HBM] + [VMEM] * len(pieces)
        )(at, after, *pieces)
        if step == 2:
            merged = call(
                merge_kernel, [((2, 2, 4, 7 * BLK, CO), LOW)], [HBM] + [VMEM] * 4, moved=4 << 20
            )(joined[0], *planes)[0]
            natural = call(
                order_kernel, [((NB * BLK, CO), LOW)], [SMEM] * 2 + [VMEM] * 2, moved=8 << 20
            )(at, block_order, merged, swap(merged, MASK_CORE))[0]
        after = natural if step == 1 else at
        if step > 0:
            pieces = []
            for part, (_, _, order) in enumerate(PARTS):
                pieces += [joined[part], swap(joined[part], MASKS[order[step - 1]])]
    mine = joined[0]
    peer = swap(mine, MASK_CORE)
    old = call(
        old_hidden_kernel,
        [((PIX, CO), WIDE)],
        [VMEM] * 2,
        flops=2 * 27 * 512 * 256 * 256,
        moved=6 << 20,
    )(views, natural)[0]
    half = call(
        half_hidden_kernel,
        [((PIX, CO), WIDE)],
        [SMEM] + [VMEM] * 2,
        flops=2 * 14 * 512 * 256 * 256,
        moved=4 << 20,
    )(at, views, mine)[0]

    update_rows, new_master, new_row, new_col, next_output = call(
        finish_kernel,
        [
            ((NB // 8 * BLK, CO), WIDE),
            ((NB // 8 * BLK, CO), WIDE),
            ((7, 128), WIDE),
            ((2, CO), WIDE),
            ((PIX, CO), LOW),
        ],
        [SMEM] * 3 + [VMEM] * 8,
        scratch=[
            pltpu.VMEM((2, CO), WIDE),
            pltpu.VMEM((64, 128), WIDE),
        ],
        pin=False,
        flops=2 * 16 * 512 * 256 * 256,
        moved=16 << 20,
        room=16,
    )(at, block_order, decay_rate, col_moment, views, natural, master_rows, mine, peer, old, half)
    return (update_rows, new_master, new_row.reshape(-1), new_col, next_output)


def solution(mesh):
    in_specs = (
        P(),
        P(),
        P(("group", "shard"), None, None, None, None),
        P(("group", "shard"), None),
        P(("group", "shard"), None),
        P(),
        P("shard", None),
        P("shard"),
        P(),
        P(("group", "shard"), None, None, None, None),
    )
    out_specs = (P("shard", None), P("shard", None), P("shard"), P(), P(("group", "shard"), None))
    body = shards if (mesh.shape["group"], mesh.shape["shard"]) == (4, 8) else general_shards
    return jax.shard_map(body, mesh=mesh, in_specs=in_specs, out_specs=out_specs, check_vma=False)
```

```python
import functools
import jax
import jax.numpy as jnp
from jax import lax
from jax.experimental import pallas as pl
from jax.experimental.pallas import tpu as pltpu
from jax.sharding import PartitionSpec as P

CI = 256
CO = 256
BLK = 32
FR = 2
HW = 16
NB3 = 216
NB = 224


learn_rate = 0.002
decay_power = 0.8


def silu_slope(values):
    sigma = jax.nn.sigmoid(values)
    return sigma * (1.0 + values * (1.0 - sigma))


def tap_views(frames):
    views = []
    for frame_off in range(3):
        for row_off in range(3):
            for col_off in range(3):
                window = frames[
                    frame_off : frame_off + FR, row_off : row_off + HW, col_off : col_off + HW, :
                ]
                views.append(window.reshape(FR * HW * HW, CI))
    return views


def contract_rows(left, right):
    return lax.dot_general(
        left, right, (((0,), (0,)), ((), ())), preferred_element_type=jnp.float32
    )


def kernel_sums(values, is_small):
    large_part = jnp.sum(jnp.where(is_small[:, None], 0.0, values), axis=0)
    small_part = jnp.sum(jnp.where(is_small[:, None], values, 0.0), axis=0)
    return jnp.stack([large_part, small_part])


def general_shards(
    step_count,
    block_order,
    saved_tiles,
    pre_act,
    grad_output,
    pointwise_live,
    master_rows,
    row_moment,
    col_moment,
    next_tiles,
):
    pre_float = pre_act.astype(jnp.float32)
    activation = jax.nn.silu(pre_float).astype(jnp.bfloat16)
    grad_act = lax.dot_general(
        grad_output, pointwise_live, (((1,), (1,)), ((), ())), preferred_element_type=jnp.float32
    )
    grad_pre = (grad_act * silu_slope(pre_float)).astype(jnp.bfloat16)
    pieces = [contract_rows(view, grad_pre) for view in tap_views(saved_tiles[0])]
    pieces.append(contract_rows(activation, grad_output))
    own_term = jnp.concatenate(pieces, axis=0).astype(jnp.bfloat16)
    total_rows = NB * BLK
    stored = jnp.take(own_term.reshape(NB, BLK, CO), block_order, axis=0).reshape(total_rows, CO)
    own_rows = master_rows.shape[0]
    partial_value = lax.psum_scatter(stored, "shard", scatter_dimension=0, tiled=True).astype(
        jnp.float32
    )
    gradient = lax.psum(partial_value, "group")
    owner = lax.axis_index("shard")
    own_count = own_rows // BLK
    own_blocks = lax.dynamic_slice_in_dim(block_order, owner * own_count, own_count)
    is_small = jnp.repeat(own_blocks >= NB3, BLK, total_repeat_length=own_rows)
    decay_rate = 1.0 - step_count.astype(jnp.float32)[0] ** (-decay_power)
    counts = jnp.array([27 * CI, CO], jnp.float32)
    squares = gradient * gradient
    new_row = decay_rate * row_moment + (1.0 - decay_rate) * jnp.mean(squares, axis=1)
    col_part = kernel_sums(squares, is_small)
    row_part = kernel_sums(new_row[:, None], is_small)[:, 0]
    weighted = kernel_sums(squares / new_row[:, None], is_small)
    col_total, weight_total, row_total = lax.psum((col_part, weighted, row_part), "shard")
    new_col = decay_rate * col_moment + (1.0 - decay_rate) * col_total / counts[:, None]
    row_mean = row_total / counts
    col_rows = jnp.where(is_small[:, None], new_col[1], new_col[0])
    mean_rows = jnp.where(is_small, row_mean[1], row_mean[0])
    scaled = gradient / jnp.sqrt(new_row[:, None] * col_rows / mean_rows[:, None])
    square_total = row_mean * jnp.sum(weight_total / new_col, axis=1)
    clip_factor = jnp.maximum(1.0, jnp.sqrt(square_total / (counts * CO)))
    update_rows = scaled / jnp.where(is_small, clip_factor[1], clip_factor[0])[:, None]
    new_master = master_rows - learn_rate * update_rows
    weights_low = new_master.astype(jnp.bfloat16)
    gathered = lax.all_gather(weights_low, "shard", axis=0, tiled=True)
    inverse = jnp.zeros((NB,), jnp.int32).at[block_order].set(jnp.arange(NB, dtype=jnp.int32))
    natural = jnp.take(gathered.reshape(NB, BLK, CO), inverse, axis=0).reshape(total_rows, CO)
    spatial = natural[: 27 * CI].reshape(27, CI, CO)
    pointwise = natural[27 * CI :]
    hidden_sum = jnp.zeros((FR * HW * HW, CO), jnp.float32)
    for index_tap, view in enumerate(tap_views(next_tiles[0])):
        hidden_sum = hidden_sum + jnp.dot(
            view, spatial[index_tap], preferred_element_type=jnp.float32
        )
    hidden_act = jax.nn.silu(hidden_sum).astype(jnp.bfloat16)
    next_output = jnp.dot(hidden_act, pointwise, preferred_element_type=jnp.float32).astype(
        jnp.bfloat16
    )
    return (update_rows, new_master, new_row, new_col, next_output)


AXES = ("group", "shard")
SLOTS = 14
PIX = FR * HW * HW
SHIFTED = (FR + 2) * (HW + 2) * HW
SLOPES = 3 * SHIFTED
ACTS = SLOPES + PIX
BROUGHT = ACTS + PIX
LOW = jnp.bfloat16
WIDE = jnp.float32
VMEM = pl.BlockSpec(memory_space=pltpu.VMEM)
SMEM = pl.BlockSpec(memory_space=pltpu.SMEM)
HBM = pl.BlockSpec(memory_space=pl.ANY)
MASK_CORE, MASK_NEAR, MASK_FAR, MASK_X, MASK_Y = 1, 2, 4, 8, 16
PARTS = ((0, 9), (9, 5))
ORDERS = (((0, 1, 2), (1, 2, 0)), ((2, 0, 1), (2, 0, 1)))
MESSAGE = 9
GATHERED = ((0, 10), (10, 5))
MASKS = (MASK_X, MASK_Y, MASK_NEAR)


def swap(value, mask):
    return lax.ppermute(value, AXES, [(at, at ^ mask) for at in range(32)])


def swap_mixed(value, masks):
    return lax.ppermute(value, AXES, [(at, at ^ masks[at & 1]) for at in range(32)])


def swap_part(value, part, step):
    return swap_mixed(value, [MASKS[ORDERS[part][core][step]] for core in range(2)])


def place_of(at, part, step):
    if step == 3:
        return at[3]
    zero, one = (ORDERS[part][core][step] for core in range(2))
    return at[zero] if zero == one else jnp.where(at[4] == 0, at[zero], at[one])


def gathered_at(slot):
    return slot + (slot >= MESSAGE) * 1


def call(kernel, outs, in_specs, scratch=(), flops=0, moved=0, room=8, pin=True):
    return pl.pallas_call(
        kernel,
        out_shape=[(pltpu.VMEM if pin else jax.ShapeDtypeStruct)(*out) for out in outs],
        in_specs=in_specs,
        out_specs=[VMEM] * len(outs),
        scratch_shapes=list(scratch),
        compiler_params=pltpu.CompilerParams(vmem_limit_bytes=room << 20),
        cost_estimate=pl.CostEstimate(flops=flops, bytes_accessed=moved, transcendentals=0),
    )


def far_away(array):
    return pltpu.with_memory_space_constraint(array, pltpu.HBM)


def store_shifted(tile, out):
    for col_off in range(3):
        out[col_off * SHIFTED : (col_off + 1) * SHIFTED] = tile[
            :, :, col_off : col_off + HW, :
        ].reshape(SHIFTED, CI)


def shift_kernel(tile, out):
    store_shifted(tile, out)


def slope_of(pre, grad, pointwise):
    grad_act = lax.dot_general(
        grad, pointwise, (((1,), (1,)), ((), ())), preferred_element_type=WIDE
    )
    return (grad_act * silu_slope(pre.astype(WIDE))).astype(LOW)


def fetch(pairs, arrived):
    copies = [
        pltpu.make_async_copy(source, target, arrived.at[index])
        for index, (source, target) in enumerate(pairs)
    ]
    for copy in copies:
        copy.start()
    return copies


def own_kernel(at, tile, pre_far, grad_far, pointwise_far, brought, pre, grad, pointwise, arrived):
    copies = fetch(((pre_far, pre), (grad_far, grad), (pointwise_far, pointwise)), arrived)
    store_shifted(tile, brought)
    for copy in copies:
        copy.wait()
    brought[SLOPES:ACTS] = slope_of(pre[...], grad[...], pointwise[...])
    brought[ACTS:] = jax.nn.silu(pre[...].astype(WIDE)).astype(LOW)


def pack_kernel(at, after, master_far, row_moment_far, packed, master, row_moment, arrived):
    quarter = pl.multiple_of((at[1] * 2 + at[0]) * (SLOTS * 16), SLOTS * 16)
    row_moment[...] = jnp.zeros((16, 128), WIDE)
    copies = fetch(
        (
            (master_far.at[pl.ds(quarter, SLOTS * 16), :], master),
            (row_moment_far, row_moment.at[pl.ds(0, 7), :]),
        ),
        arrived,
    )
    for copy in copies:
        copy.wait()
    packed[:SLOTS] = master[...].astype(LOW).reshape(SLOTS, 16, CO)
    high = row_moment[...].astype(LOW).astype(WIDE)
    packed[SLOTS] = jnp.concatenate([high, row_moment[...] - high], axis=1).astype(LOW)


def term_kernel(
    at, own, tile_peer, pre_peer, grad_peer, grad_far, pointwise_far,
    keep, send_one, send_two, peer, rights, pointwise, arrived,
):
    core = at[4]
    copies = fetch(((grad_far, rights.at[1, pl.ds(0, PIX), :]), (pointwise_far, pointwise)), arrived)
    store_shifted(tile_peer, peer)
    peer[ACTS:] = jax.nn.silu(pre_peer[...].astype(WIDE)).astype(LOW)
    for copy in copies:
        copy.wait()
    peer[SLOPES:ACTS] = slope_of(pre_peer[...], grad_peer[...], pointwise[...])
    rights[0, :PIX] = own[SLOPES:ACTS]
    rights[0, PIX:] = peer[SLOPES:ACTS]
    rights[1, PIX:] = grad_peer[...]
    for slot in range(SLOTS):
        tap = core * SLOTS + slot
        frame_off, row_off, col_off = tap // 9, lax.rem(tap // 3, 3), lax.rem(tap, 3)
        pieces = []
        for ref in (own, peer):
            for frame in range(FR):
                start = col_off * SHIFTED + ((frame + frame_off) * (HW + 2) + row_off) * HW
                if slot == SLOTS - 1:
                    start = jnp.where(core == 0, start, ACTS + frame * HW * HW)
                pieces.append(ref[pl.ds(pl.multiple_of(start, HW), HW * HW), :])
        right = rights[core] if slot == SLOTS - 1 else rights[0]
        total = contract_rows(jnp.concatenate(pieces, axis=0), right)
        for part, ((first, count), send) in enumerate(zip(PARTS, (send_one, send_two))):
            if first <= slot < first + count:
                low, high, at_low = total[:128], total[128:], place_of(at, part, 0) == 0
                keep[slot] = jnp.where(at_low, low, high).astype(LOW)
                send[slot - first] = jnp.where(at_low, high, low).astype(LOW)


def fold_kernel(step, at, *refs):
    size = 256 >> (step + 1)
    extra = 0 if step == 2 else 2
    own, got = refs[:extra] or (None, None)
    refs = refs[extra:]
    keep, gots, stay, sends = refs[0], refs[1:3], refs[3], refs[4:]
    for part, (first, count) in enumerate(PARTS):
        mine = place_of(at, part, step)
        here = slice(first, first + count)
        for which, out in ((mine, 0), (1 - mine, 1)):
            rows = pl.ds(pl.multiple_of(which * size, size), size)
            value = keep[here, rows] + gots[part][:, rows]
            if out == 0:
                stay[here] = value
            elif step < 3:
                sends[part][...] = value
            else:
                sends[0][here] = value
    if step == 1:
        pair = sends[2]
        pair[at[2]] = own[...]
        pair[1 - at[2]] = got[...]
    if step == 3:
        line, moments = sends[1:]
        for which, piece in ((at[3], own), (1 - at[3], got)):
            for near in range(2):
                line[which * 2 + near] = piece[near, :SLOTS].reshape(SLOTS * 16, CO)
                moments[which * 2 + near] = piece[near, SLOTS]


def moment_kernel(at, rate, own, got, moments, line, line_got, scaled, plane):
    plane[0], plane[1] = line[...], line_got[...]
    total = (own[...].astype(WIDE) + got[...].astype(WIDE)).reshape(SLOTS * 16, CO)
    squares = total * total
    decay = rate[0]
    mean = jnp.sum(squares, axis=1, keepdims=True) * (1.0 / CO)
    row_moment = jnp.concatenate([moments[:, slot : slot + 1] for slot in range(SLOTS)], axis=0)
    new_row = decay * row_moment + (1.0 - decay) * mean
    value = (total * lax.rsqrt(new_row)).astype(LOW).reshape(SLOTS, 16, CO)
    scaled[:MESSAGE] = value[:MESSAGE]
    scaled[MESSAGE + 1 :] = value[MESSAGE:]
    weighted = squares / new_row
    cut = (SLOTS - 1) * 16
    last_small = at[4] == 1
    rows = []
    for values in (squares, weighted, jnp.broadcast_to(new_row, (SLOTS * 16, CO))):
        large = jnp.sum(values[:cut], axis=0, keepdims=True)
        last = jnp.sum(values[cut:], axis=0, keepdims=True)
        rows.append(large + jnp.where(last_small, 0.0, last))
        rows.append(jnp.where(last_small, last, 0.0))
    spread = jnp.broadcast_to(new_row, (SLOTS * 16, 128))
    spread = jnp.concatenate([spread, jnp.zeros((32, 128), WIDE)], axis=0)
    rows.append(jnp.transpose(spread)[:1])
    rows.append(jnp.zeros((1, CO), WIDE))
    message = jnp.concatenate(rows, axis=0)
    high = message.astype(LOW).astype(WIDE)
    scaled[MESSAGE] = jnp.concatenate([high, message - high], axis=0).astype(LOW)


def store_factors(total, decay, col_moment, new_col, factor):
    for kernel in range(2):
        count = 27.0 * CI if kernel == 0 else float(CO)
        col = decay * col_moment[kernel : kernel + 1] + (1.0 - decay) * (
            total[kernel : kernel + 1] / count
        )
        row_mean = total[4 + kernel : 5 + kernel] / count
        square = row_mean * jnp.sum(
            total[2 + kernel : 3 + kernel] / col, axis=1, keepdims=True
        )
        clip = jnp.maximum(1.0, jnp.sqrt(square / (count * CO)))
        new_col[kernel : kernel + 1] = col
        factor[kernel : kernel + 1] = 1.0 / (jnp.sqrt(col / row_mean) * clip)


def moments_kernel(at, block_order, mine, peer, out, table, rows, inverse):
    core = at[4]
    for side, ref in enumerate((mine, peer)):
        for line in range(4):
            values = ref[line].astype(WIDE)
            values = values[:, :128] + values[:, 128:]
            table[pl.ds(pl.multiple_of((line * 2 + (core ^ side)) * 8, 8), 8), :] = values[:8]

    def invert(stored, carry):
        inverse[block_order[stored]] = stored
        return carry

    lax.fori_loop(0, NB, invert, 0, unroll=8)
    rows[...] = jnp.zeros((128, 128), WIDE)
    for part, (first, count) in enumerate(PARTS):
        place = place_of(at, part, 0) * 4 + place_of(at, part, 1) * 2 + place_of(at, part, 2)
        for slot in range(first, first + count):
            stored = inverse[(core * SLOTS + slot) * 8 + place]
            owner, local = stored // (NB // 8), lax.rem(stored, NB // 8)
            row = table[pl.ds(owner * 8 + local // 4, 1), :]
            turn = lax.rem(128 - lax.rem(local, 4) * BLK - at[3] * 16, 128)
            rows[slot : slot + 1] = pltpu.roll(row, turn, 1)
    out[...] = jnp.transpose(rows[...])[:16]


def order_kernel(at, block_order, mine, mine_got, peer, peer_got, out):
    count = NB // 8
    quarters = count // 4
    for flip_core, pieces in enumerate(((mine, mine_got), (peer, peer_got))):
        core = at[4] ^ flip_core
        for second, piece in enumerate(pieces):
            for first in range(2):
                flip_x = jnp.where(core == 0, first, second)
                quarter = (at[1] ^ first ^ second ^ flip_x) * 2 + (at[0] ^ flip_x)
                for local in range(quarters):
                    for line in range(4):
                        block = block_order[(line * 2 + core) * count + quarter * quarters + local]
                        to = pl.ds(pl.multiple_of(block * BLK, BLK), BLK)
                        out[to, :] = piece[first, line, local * BLK : local * BLK + BLK]


def widen_kernel(step, at, after, *refs):
    size = 256 >> (step + 1)
    ins, outs = (refs[:2], refs[2:]) if step == 3 else (refs[:4], refs[4:])
    for part, (first, count) in enumerate(GATHERED):
        mine = place_of(at, part, step)
        here = slice(first, first + count)
        for index, which in enumerate((mine, 1 - mine)):
            rows = pl.ds(pl.multiple_of(which * size, size), size)
            value = ins[index][here] if step == 3 else ins[2 * part + index][...]
            if step == 0:
                outs[0][here, rows] = value
            else:
                outs[part][:, rows] = value


def window(views, tap):
    frame_off, row_off, col_off = tap // 9, lax.rem(tap // 3, 3), lax.rem(tap, 3)
    parts = []
    for frame in range(FR):
        start = col_off * SHIFTED + ((frame + frame_off) * (HW + 2) + row_off) * HW
        parts.append(views[pl.ds(pl.multiple_of(start, HW), HW * HW), :])
    return jnp.concatenate(parts, axis=0)


def old_hidden_kernel(views, natural, hidden):
    total = jnp.zeros((PIX, CO), WIDE)
    for tap in range(27):
        weights = natural[tap * CI : tap * CI + CI]
        total = total + jnp.dot(window(views, tap), weights, preferred_element_type=WIDE)
    hidden[...] = total


def add_taps(views, scaled, core):
    total = jnp.zeros((PIX, CO), WIDE)
    for slot in range(SLOTS):
        tap = jnp.minimum(core * SLOTS + slot, 26)
        weights = scaled[gathered_at(slot)]
        if slot == SLOTS - 1:
            weights = jnp.where(core == 0, weights.astype(WIDE), 0.0).astype(LOW)
        total = total + jnp.dot(window(views, tap), weights, preferred_element_type=WIDE)
    return total


def half_hidden_kernel(at, views, scaled, hidden):
    hidden[...] = add_taps(views, scaled, at[4])


def finish_kernel(
    at, block_order, rate, col_moment, views, natural, master, mine, peer, old, own_part,
    update_rows, new_master, new_row, new_col, next_output, factor, row_table,
):
    core = at[4]
    total = jnp.zeros((8, CO), WIDE)
    for side, piece in enumerate((mine, peer)):
        message = piece[MESSAGE].astype(WIDE).reshape(16, 2, 8, CO)
        message = message[:, 0] + message[:, 1]
        total = total + jnp.sum(message, axis=0)
        for index in range(16):
            for half in range(2):
                to = (side * 16 + index) * 2 + half
                row_table[to : to + 1] = message[index, 6:7, half * 128 : half * 128 + 128]
    store_factors(total, rate[0], col_moment, new_col, factor)
    change = own_part[...] + add_taps(views, peer, 1 - core)
    hidden = old[...] - (learn_rate * factor[0:1]) * change
    small = jnp.where(core == 1, mine[SLOTS].astype(WIDE), peer[SLOTS].astype(WIDE))
    weights = natural[27 * CI :].astype(WIDE) - small * (learn_rate * factor[1:2])
    next_output[...] = jnp.dot(
        jax.nn.silu(hidden).astype(LOW), weights.astype(LOW), preferred_element_type=WIDE
    ).astype(LOW)

    owner = at[3] * 4 + at[2] * 2 + core
    lane = lax.broadcasted_iota(jnp.int32, (1, 128), 1)
    for line in range(7):
        values = jnp.zeros((1, 128), WIDE)
        for part in range(4):
            local = line * 4 + part
            block = block_order[owner * (NB // 8) + local]
            side = (block // (8 * SLOTS)) ^ core
            slot, place = lax.rem(block // 8, SLOTS), lax.rem(block, 8)
            near, x, y = place // 4, lax.rem(place // 2, 2), lax.rem(place, 2)
            other = jnp.where(side == core, x * 8 + y * 4 + near * 2, y * 8 + near * 4 + x * 2)
            sender = jnp.where(slot < MESSAGE, place * 2, other)
            index = gathered_at(slot)
            chosen = jnp.where(block >= NB3, factor[1:2], factor[0:1])
            rows = slice(local * BLK, local * BLK + BLK)
            there = pl.ds(pl.multiple_of(place * BLK, BLK), BLK)
            value = jnp.where(
                side == 0, mine[index, there, :].astype(WIDE), peer[index, there, :].astype(WIDE)
            )
            update = value * chosen
            update_rows[rows, :] = update
            new_master[rows, :] = master[rows, :] - learn_rate * update
            for half in range(2):
                at_row = (side * 16 + sender + half) * 2 + slot // 8
                to = part * 32 + half * 16
                turn = lax.rem(128 + to - lax.rem(slot, 8) * 16, 128)
                turned = pltpu.roll(row_table[pl.ds(at_row, 1), :], turn, 1)
                values = jnp.where((lane >= to) & (lane < to + 16), turned, values)
        new_row[line : line + 1] = values


def shards(
    step_count,
    block_order,
    saved_tiles,
    pre_act,
    grad_output,
    pointwise_live,
    master_rows,
    row_moment,
    col_moment,
    next_tiles,
):
    group, shard = lax.axis_index("group"), lax.axis_index("shard")
    axis_y, axis_x = group // 2, group % 2
    far, near, core = shard // 4, shard // 2 % 2, shard % 2
    at = jnp.stack([axis_x, axis_y, near, far, core]).astype(jnp.int32)
    decay_rate = 1.0 - step_count.astype(WIDE) ** (-decay_power)

    tile_peer = swap(saved_tiles, MASK_CORE)
    pre_peer = swap(pre_act, MASK_CORE)
    grad_peer = swap(grad_output, MASK_CORE)
    rows_far = [far_away(array) for array in (pre_act, grad_output, pointwise_live)]
    brought = call(
        own_kernel,
        [((BROUGHT, CI), LOW)],
        [SMEM, VMEM] + [HBM] * 3,
        scratch=[
            pltpu.VMEM((PIX, CO), LOW),
            pltpu.VMEM((PIX, CO), LOW),
            pltpu.VMEM((CO, CO), LOW),
            pltpu.SemaphoreType.DMA((3,)),
        ],
        moved=4 << 20,
    )(at, saved_tiles[0], *rows_far)[0]

    keep, *sends = call(
        term_kernel,
        [((SLOTS, 128, CO), LOW)] + [((count, 128, CO), LOW) for _, count in PARTS],
        [SMEM] + [VMEM] * 4 + [HBM] * 2,
        scratch=[
            pltpu.VMEM((BROUGHT, CI), LOW),
            pltpu.VMEM((2, 2 * PIX, CO), LOW),
            pltpu.VMEM((CO, CO), LOW),
            pltpu.SemaphoreType.DMA((2,)),
        ],
        flops=2 * 14 * 1024 * 256 * 256,
        moved=6 << 20,
        room=12,
    )(at, brought, tile_peer[0], pre_peer, grad_peer, *rows_far[1:])

    packed = call(
        pack_kernel,
        [((SLOTS + 1, 16, CO), LOW)],
        [SMEM] + [HBM] * 3,
        scratch=[
            pltpu.VMEM((SLOTS * 16, CO), WIDE),
            pltpu.VMEM((16, 128), WIDE),
            pltpu.SemaphoreType.DMA((2,)),
        ],
    )(at, keep, far_away(master_rows), far_away(row_moment.reshape(7, 128)))[0]
    packed_near = swap(packed, MASK_NEAR)
    views = call(shift_kernel, [((3 * SHIFTED, CI), LOW)], [VMEM], moved=3 << 20)(next_tiles[0])[0]

    for step in range(1, 4):
        gots = [swap_part(send, part, step - 1) for part, send in enumerate(sends)]
        size = 256 >> (step + 1)
        outs = [((SLOTS, size, CO), LOW)] + [((count, size, CO), LOW) for _, count in PARTS]
        if step == 1:
            extra = [packed, packed_near]
            outs = outs + [((2, SLOTS + 1, 16, CO), LOW)]
        elif step == 2:
            extra = []
        else:
            extra = [pair, pair_far]
            outs = outs[:1] * 2 + [((4, SLOTS * 16, CO), LOW), ((4, 16, CO), LOW)]
        keep, *sends = call(
            functools.partial(fold_kernel, step),
            outs,
            [SMEM] + [VMEM] * (len(extra) + 3),
            moved=1 << 20,
        )(at, *extra, keep, *gots)
        if step == 1:
            pair = sends.pop()
            pair_far = swap(pair, MASK_FAR)
    _, line, moments = sends
    line_got = swap_mixed(line, (MASK_X, MASK_Y))
    own_moment = call(
        moments_kernel,
        [((16, 128), WIDE)],
        [SMEM] * 2 + [VMEM] * 2,
        scratch=[
            pltpu.VMEM((64, 128), WIDE),
            pltpu.VMEM((128, 128), WIDE),
            pltpu.SMEM((NB,), jnp.int32),
        ],
    )(at, block_order, moments, swap(moments, MASK_CORE))[0]
    scaled, plane = call(
        moment_kernel,
        [((SLOTS + 1, 16, CO), LOW), ((2, 4, SLOTS * 16, CO), LOW)],
        [SMEM] * 2 + [VMEM] * 5,
        moved=2 << 20,
    )(at, decay_rate, keep, swap(sends[0], MASK_FAR), own_moment, line, line_got)
    plane_got = swap_mixed(plane, (MASK_Y, MASK_X))
    natural = call(
        order_kernel, [((NB * BLK, CO), LOW)], [SMEM] * 2 + [VMEM] * 4, moved=8 << 20
    )(at, block_order, plane, plane_got, swap(plane, MASK_CORE), swap(plane_got, MASK_CORE))[0]

    pieces = [scaled, swap(scaled, MASK_FAR)]
    for step in range(3, -1, -1):
        after = (natural, at, plane_got, views)[step]
        size = 256 >> step
        outs = [((count, size, CO), LOW) for _, count in GATHERED]
        if step == 0:
            outs = [((SLOTS + 1, size, CO), LOW)]
        joined = call(
            functools.partial(widen_kernel, step), outs, [SMEM, HBM] + [VMEM] * len(pieces)
        )(at, after, *pieces)
        if step > 0:
            pieces = []
            for part, value in enumerate(joined):
                pieces += [value, swap_part(value, part, step - 1)]
    mine = joined[0]
    peer = swap(mine, MASK_CORE)
    old = call(
        old_hidden_kernel,
        [((PIX, CO), WIDE)],
        [VMEM] * 2,
        flops=2 * 27 * 512 * 256 * 256,
        moved=6 << 20,
    )(views, natural)[0]
    half = call(
        half_hidden_kernel,
        [((PIX, CO), WIDE)],
        [SMEM] + [VMEM] * 2,
        flops=2 * 14 * 512 * 256 * 256,
        moved=4 << 20,
    )(at, views, mine)[0]

    update_rows, new_master, new_row, new_col, next_output = call(
        finish_kernel,
        [
            ((NB // 8 * BLK, CO), WIDE),
            ((NB // 8 * BLK, CO), WIDE),
            ((7, 128), WIDE),
            ((2, CO), WIDE),
            ((PIX, CO), LOW),
        ],
        [SMEM] * 3 + [VMEM] * 8,
        scratch=[
            pltpu.VMEM((2, CO), WIDE),
            pltpu.VMEM((64, 128), WIDE),
        ],
        pin=False,
        flops=2 * 16 * 512 * 256 * 256,
        moved=16 << 20,
        room=16,
    )(at, block_order, decay_rate, col_moment, views, natural, master_rows, mine, peer, old, half)
    return (update_rows, new_master, new_row.reshape(-1), new_col, next_output)


def solution(mesh):
    in_specs = (
        P(),
        P(),
        P(("group", "shard"), None, None, None, None),
        P(("group", "shard"), None),
        P(("group", "shard"), None),
        P(),
        P("shard", None),
        P("shard"),
        P(),
        P(("group", "shard"), None, None, None, None),
    )
    out_specs = (P("shard", None), P("shard", None), P("shard"), P(), P(("group", "shard"), None))
    body = shards if (mesh.shape["group"], mesh.shape["shard"]) == (4, 8) else general_shards
    return jax.shard_map(body, mesh=mesh, in_specs=in_specs, out_specs=out_specs, check_vma=False)
```

```python
import functools
import jax
import jax.numpy as jnp
from jax import lax
from jax.experimental import pallas as pl
from jax.experimental.pallas import tpu as pltpu
from jax.sharding import PartitionSpec as P

CI = 256
CO = 256
BLK = 32
FR = 2
HW = 16
NB3 = 216
NB = 224


learn_rate = 0.002
decay_power = 0.8


def silu_slope(values):
    sigma = jax.nn.sigmoid(values)
    return sigma * (1.0 + values * (1.0 - sigma))


def tap_views(frames):
    views = []
    for frame_off in range(3):
        for row_off in range(3):
            for col_off in range(3):
                window = frames[
                    frame_off : frame_off + FR, row_off : row_off + HW, col_off : col_off + HW, :
                ]
                views.append(window.reshape(FR * HW * HW, CI))
    return views


def contract_rows(left, right):
    return lax.dot_general(
        left, right, (((0,), (0,)), ((), ())), preferred_element_type=jnp.float32
    )


def kernel_sums(values, is_small):
    large_part = jnp.sum(jnp.where(is_small[:, None], 0.0, values), axis=0)
    small_part = jnp.sum(jnp.where(is_small[:, None], values, 0.0), axis=0)
    return jnp.stack([large_part, small_part])


def general_shards(
    step_count,
    block_order,
    saved_tiles,
    pre_act,
    grad_output,
    pointwise_live,
    master_rows,
    row_moment,
    col_moment,
    next_tiles,
):
    pre_float = pre_act.astype(jnp.float32)
    activation = jax.nn.silu(pre_float).astype(jnp.bfloat16)
    grad_act = lax.dot_general(
        grad_output, pointwise_live, (((1,), (1,)), ((), ())), preferred_element_type=jnp.float32
    )
    grad_pre = (grad_act * silu_slope(pre_float)).astype(jnp.bfloat16)
    pieces = [contract_rows(view, grad_pre) for view in tap_views(saved_tiles[0])]
    pieces.append(contract_rows(activation, grad_output))
    own_term = jnp.concatenate(pieces, axis=0).astype(jnp.bfloat16)
    total_rows = NB * BLK
    stored = jnp.take(own_term.reshape(NB, BLK, CO), block_order, axis=0).reshape(total_rows, CO)
    own_rows = master_rows.shape[0]
    partial_value = lax.psum_scatter(stored, "shard", scatter_dimension=0, tiled=True).astype(
        jnp.float32
    )
    gradient = lax.psum(partial_value, "group")
    owner = lax.axis_index("shard")
    own_count = own_rows // BLK
    own_blocks = lax.dynamic_slice_in_dim(block_order, owner * own_count, own_count)
    is_small = jnp.repeat(own_blocks >= NB3, BLK, total_repeat_length=own_rows)
    decay_rate = 1.0 - step_count.astype(jnp.float32)[0] ** (-decay_power)
    counts = jnp.array([27 * CI, CO], jnp.float32)
    squares = gradient * gradient
    new_row = decay_rate * row_moment + (1.0 - decay_rate) * jnp.mean(squares, axis=1)
    col_part = kernel_sums(squares, is_small)
    row_part = kernel_sums(new_row[:, None], is_small)[:, 0]
    weighted = kernel_sums(squares / new_row[:, None], is_small)
    col_total, weight_total, row_total = lax.psum((col_part, weighted, row_part), "shard")
    new_col = decay_rate * col_moment + (1.0 - decay_rate) * col_total / counts[:, None]
    row_mean = row_total / counts
    col_rows = jnp.where(is_small[:, None], new_col[1], new_col[0])
    mean_rows = jnp.where(is_small, row_mean[1], row_mean[0])
    scaled = gradient / jnp.sqrt(new_row[:, None] * col_rows / mean_rows[:, None])
    square_total = row_mean * jnp.sum(weight_total / new_col, axis=1)
    clip_factor = jnp.maximum(1.0, jnp.sqrt(square_total / (counts * CO)))
    update_rows = scaled / jnp.where(is_small, clip_factor[1], clip_factor[0])[:, None]
    new_master = master_rows - learn_rate * update_rows
    weights_low = new_master.astype(jnp.bfloat16)
    gathered = lax.all_gather(weights_low, "shard", axis=0, tiled=True)
    inverse = jnp.zeros((NB,), jnp.int32).at[block_order].set(jnp.arange(NB, dtype=jnp.int32))
    natural = jnp.take(gathered.reshape(NB, BLK, CO), inverse, axis=0).reshape(total_rows, CO)
    spatial = natural[: 27 * CI].reshape(27, CI, CO)
    pointwise = natural[27 * CI :]
    hidden_sum = jnp.zeros((FR * HW * HW, CO), jnp.float32)
    for index_tap, view in enumerate(tap_views(next_tiles[0])):
        hidden_sum = hidden_sum + jnp.dot(
            view, spatial[index_tap], preferred_element_type=jnp.float32
        )
    hidden_act = jax.nn.silu(hidden_sum).astype(jnp.bfloat16)
    next_output = jnp.dot(hidden_act, pointwise, preferred_element_type=jnp.float32).astype(
        jnp.bfloat16
    )
    return (update_rows, new_master, new_row, new_col, next_output)


AXES = ("group", "shard")
SLOTS = 14
PIX = FR * HW * HW
SHIFTED = (FR + 2) * (HW + 2) * HW
SLOPES = 3 * SHIFTED
ACTS = SLOPES + PIX
BROUGHT = ACTS + PIX
LOW = jnp.bfloat16
WIDE = jnp.float32
VMEM = pl.BlockSpec(memory_space=pltpu.VMEM)
SMEM = pl.BlockSpec(memory_space=pltpu.SMEM)
HBM = pl.BlockSpec(memory_space=pl.ANY)
MASK_CORE, MASK_NEAR, MASK_FAR, MASK_X, MASK_Y = 1, 2, 4, 8, 16
PARTS = ((0, 10), (10, 4))
ORDERS = (((0, 1, 2), (1, 2, 0)), ((2, 0, 1), (2, 0, 1)))
MESSAGE = SLOTS
GATHERED = ((0, 10), (10, 5))
MASKS = (MASK_X, MASK_Y, MASK_NEAR)


def swap(value, mask):
    return lax.ppermute(value, AXES, [(at, at ^ mask) for at in range(32)])


def swap_mixed(value, masks):
    return lax.ppermute(value, AXES, [(at, at ^ masks[at & 1]) for at in range(32)])


def swap_part(value, part, step):
    return swap_mixed(value, [MASKS[ORDERS[part][core][step]] for core in range(2)])


def place_of(at, part, step):
    zero, one = (ORDERS[part][core][step] for core in range(2))
    return at[zero] if zero == one else jnp.where(at[4] == 0, at[zero], at[one])


def call(kernel, outs, in_specs, out_specs=None, scratch=(), flops=0, moved=0, room=8, pin=True):
    return pl.pallas_call(
        kernel,
        out_shape=[(pltpu.VMEM if pin else jax.ShapeDtypeStruct)(*out) for out in outs],
        in_specs=in_specs,
        out_specs=out_specs or [VMEM] * len(outs),
        scratch_shapes=list(scratch),
        compiler_params=pltpu.CompilerParams(vmem_limit_bytes=room << 20),
        cost_estimate=pl.CostEstimate(flops=flops, bytes_accessed=moved, transcendentals=0),
    )


def far_away(array):
    return pltpu.with_memory_space_constraint(array, pltpu.HBM)


def store_shifted(tile, out):
    for col_off in range(3):
        out[col_off * SHIFTED : (col_off + 1) * SHIFTED] = tile[
            :, :, col_off : col_off + HW, :
        ].reshape(SHIFTED, CI)


def shift_kernel(tile, out):
    store_shifted(tile, out)


def slope_of(pre, grad, pointwise):
    grad_act = lax.dot_general(
        grad, pointwise, (((1,), (1,)), ((), ())), preferred_element_type=WIDE
    )
    return (grad_act * silu_slope(pre.astype(WIDE))).astype(LOW)


def view_start(tap, frame):
    frame_off, row_off, col_off = tap // 9, tap // 3 % 3, tap % 3
    return col_off * SHIFTED + ((frame + frame_off) * (HW + 2) + row_off) * HW


def core_start(core, slot, frame):
    return pl.multiple_of(
        jnp.where(core == 0, view_start(slot, frame), view_start(min(SLOTS + slot, 26), frame)), HW
    )


def fetch(pairs, arrived):
    copies = [
        pltpu.make_async_copy(source, target, arrived.at[index])
        for index, (source, target) in enumerate(pairs)
    ]
    for copy in copies:
        copy.start()
    return copies


def own_kernel(at, tile, pre_far, grad_far, pointwise_far, brought, pre, grad, pointwise, arrived):
    copies = fetch(((pre_far, pre), (grad_far, grad), (pointwise_far, pointwise)), arrived)
    store_shifted(tile, brought)
    for copy in copies:
        copy.wait()
    brought[SLOPES:ACTS] = slope_of(pre[...], grad[...], pointwise[...])
    brought[ACTS:] = jax.nn.silu(pre[...].astype(WIDE)).astype(LOW)


def pack_kernel(at, after, master_far, row_moment_far, packed, master, row_moment, arrived):
    quarter = pl.multiple_of((at[1] * 2 + at[0]) * (SLOTS * 16), SLOTS * 16)
    row_moment[...] = jnp.zeros((16, 128), WIDE)
    copies = fetch(
        (
            (master_far.at[pl.ds(quarter, SLOTS * 16), :], master),
            (row_moment_far, row_moment.at[pl.ds(0, 7), :]),
        ),
        arrived,
    )
    for copy in copies:
        copy.wait()
    packed[:SLOTS] = master[...].astype(LOW).reshape(SLOTS, 16, CO)
    high = row_moment[...].astype(LOW).astype(WIDE)
    packed[SLOTS] = jnp.concatenate([high, row_moment[...] - high], axis=1).astype(LOW)


def term_kernel(
    at, own, tile_peer, pre_peer, grad_peer, grad_far, pointwise_far,
    keep, send_one, send_two, peer, rights, pointwise, arrived,
):
    core = at[4]
    copies = fetch(((grad_far, rights.at[1, pl.ds(0, PIX), :]), (pointwise_far, pointwise)), arrived)
    store_shifted(tile_peer, peer)
    peer[ACTS:] = jax.nn.silu(pre_peer[...].astype(WIDE)).astype(LOW)
    for copy in copies:
        copy.wait()
    peer[SLOPES:ACTS] = slope_of(pre_peer[...], grad_peer[...], pointwise[...])
    rights[0, :PIX] = own[SLOPES:ACTS]
    rights[0, PIX:] = peer[SLOPES:ACTS]
    rights[1, PIX:] = grad_peer[...]
    for slot in range(SLOTS):
        pieces = []
        for ref in (own, peer):
            for frame in range(FR):
                start = core_start(core, slot, frame)
                if slot == SLOTS - 1:
                    start = jnp.where(core == 0, start, ACTS + frame * HW * HW)
                pieces.append(ref[pl.ds(pl.multiple_of(start, HW), HW * HW), :])
        right = rights[core] if slot == SLOTS - 1 else rights[0]
        total = contract_rows(jnp.concatenate(pieces, axis=0), right)
        for part, ((first, count), send) in enumerate(zip(PARTS, (send_one, send_two))):
            if first <= slot < first + count:
                low, high, at_low = total[:128], total[128:], place_of(at, part, 0) == 0
                keep[slot] = jnp.where(at_low, low, high).astype(LOW)
                send[slot - first] = jnp.where(at_low, high, low).astype(LOW)


def fold_kernel(step, at, *refs):
    size = 256 >> (step + 1)
    extra = 0 if step == 2 else 2
    own, got = refs[:extra] or (None, None)
    refs = refs[extra:]
    keep, gots, stay, sends = refs[0], refs[1:3], refs[3], refs[4:]
    for part, (first, count) in enumerate(PARTS):
        here = slice(first, first + count)
        if step == 3:
            stay[here] = keep[here] + gots[part][...]
            continue
        mine = place_of(at, part, step)
        for which, out in ((mine, 0), (1 - mine, 1)):
            rows = pl.ds(pl.multiple_of(which * size, size), size)
            value = keep[here, rows] + gots[part][:, rows]
            if out == 0:
                stay[here] = value
            else:
                sends[part][...] = value
    if step == 1:
        pair = sends[2]
        pair[at[3]] = own[...]
        pair[1 - at[3]] = got[...]
    if step == 3:
        line, moments = sends
        for which, piece in ((at[2], own), (1 - at[2], got)):
            for far in range(2):
                line[far * 2 + which] = piece[far, :SLOTS].reshape(SLOTS * 16, CO)
                moments[far * 2 + which] = piece[far, SLOTS]


def moment_kernel(
    at, rate, own, got, moments, line, line_one, line_two, scaled_one, scaled_two, lines,
):
    for index, piece in enumerate((line, line_one, line_two)):
        lines[index] = piece[...]
    count = SLOTS * BLK
    total = (own[...].astype(WIDE) + got[...].astype(WIDE)).reshape(count, CO)
    squares = total * total
    decay = rate[0]
    mean = jnp.sum(squares, axis=1, keepdims=True) * (1.0 / CO)
    row_moment = jnp.concatenate([moments[:, slot : slot + 1] for slot in range(SLOTS)], axis=0)
    new_row = decay * row_moment + (1.0 - decay) * mean
    value = (total * lax.rsqrt(new_row)).astype(LOW).reshape(SLOTS, BLK, CO)
    split = PARTS[0][1]
    scaled_one[...] = value[:split]
    scaled_two[: SLOTS - split] = value[split:]
    weighted = squares / new_row
    cut = count - BLK
    last_small = at[4] == 1
    rows = []
    for values in (squares, weighted, jnp.broadcast_to(new_row, (count, CO))):
        large = jnp.sum(values[:cut], axis=0, keepdims=True)
        last = jnp.sum(values[cut:], axis=0, keepdims=True)
        rows.append(large + jnp.where(last_small, 0.0, last))
        rows.append(jnp.where(last_small, last, 0.0))
    spread = jnp.broadcast_to(new_row, (count, 128))
    spread = jnp.concatenate([spread, jnp.zeros((512 - count, 128), WIDE)], axis=0)
    rows += [jnp.transpose(spread[:CO])[:1], jnp.transpose(spread[CO:])[:1]]
    message = jnp.concatenate(rows, axis=0)
    high = message.astype(LOW).astype(WIDE)
    message = jnp.concatenate([high, message - high, jnp.zeros((16, CO), WIDE)], axis=0)
    scaled_two[SLOTS - split] = message.astype(LOW)


def store_factors(total, decay, col_moment, new_col, factor):
    for kernel in range(2):
        count = 27.0 * CI if kernel == 0 else float(CO)
        col = decay * col_moment[kernel : kernel + 1] + (1.0 - decay) * (
            total[kernel : kernel + 1] / count
        )
        row_mean = total[4 + kernel : 5 + kernel] / count
        square = row_mean * jnp.sum(
            total[2 + kernel : 3 + kernel] / col, axis=1, keepdims=True
        )
        clip = jnp.maximum(1.0, jnp.sqrt(square / (count * CO)))
        new_col[kernel : kernel + 1] = col
        factor[kernel : kernel + 1] = 1.0 / (jnp.sqrt(col / row_mean) * clip)


def moments_kernel(at, block_order, mine, peer, out, plan, table, rows, inverse):
    core = at[4]
    owner = at[3] * 4 + at[2] * 2 + core

    def place_block(local, carry):
        block = block_order[owner * (NB // 8) + local]
        half = (block >= 8 * SLOTS).astype(jnp.int32)
        slot, place = (block - half * (8 * SLOTS)) // 8, lax.rem(block, 8)
        high, middle, low = place // 4, lax.rem(place // 2, 2), lax.rem(place, 2)
        other = jnp.where(half == 0, low * 4 + high * 2 + middle, middle * 4 + low * 2 + high)
        sender = jnp.where(slot < PARTS[1][0], other, place)
        side = half ^ core
        plan[local * 8] = side
        plan[local * 8 + 1] = slot
        plan[local * 8 + 2] = place * BLK
        plan[local * 8 + 3] = (block >= NB3).astype(jnp.int32)
        plan[local * 8 + 4] = (side * 8 + sender) * 4 + slot // 4
        plan[local * 8 + 5] = lax.rem(128 + (lax.rem(local, 4) - lax.rem(slot, 4)) * BLK, 128)
        return carry

    lax.fori_loop(0, NB // 8, place_block, 0, unroll=4)
    for side, ref in enumerate((mine, peer)):
        for line in range(4):
            values = ref[line].astype(WIDE)
            values = values[:, :128] + values[:, 128:]
            table[pl.ds(pl.multiple_of((line * 2 + (core ^ side)) * 8, 8), 8), :] = values[:8]

    def invert(stored, carry):
        inverse[block_order[stored]] = stored
        return carry

    lax.fori_loop(0, NB, invert, 0, unroll=8)
    rows[...] = jnp.zeros((128, 128), WIDE)
    for part, (first, count) in enumerate(PARTS):
        place = place_of(at, part, 0) * 4 + place_of(at, part, 1) * 2 + place_of(at, part, 2)
        for slot in range(first, first + count):
            stored = inverse[(core * SLOTS + slot) * 8 + place]
            owner, local = stored // (NB // 8), lax.rem(stored, NB // 8)
            row = table[pl.ds(owner * 8 + local // 4, 1), :]
            turn = lax.rem(128 - lax.rem(local, 4) * BLK, 128)
            rows[slot : slot + 1] = pltpu.roll(row, turn, 1)
    out[...] = jnp.transpose(rows[...])[:BLK]


def order_kernel(at, block_order, mine, mine_far, peer, peer_far, out):
    count = NB // 8
    quarters = count // 4
    for flip_core, (pieces, far) in enumerate(((mine, mine_far), (peer, peer_far))):
        core = at[4] ^ flip_core
        for index, piece in enumerate((pieces.at[0], pieces.at[1], pieces.at[2], far)):
            quarter = (at[1] ^ (index % 2)) * 2 + (at[0] ^ (index // 2))
            for local in range(quarters):
                for line in range(4):
                    block = block_order[(line * 2 + core) * count + quarter * quarters + local]
                    to = pl.ds(pl.multiple_of(block * BLK, BLK), BLK)
                    out[to, :] = piece[line, local * BLK : local * BLK + BLK]


def widen_kernel(step, at, after, *refs):
    size = 256 >> (step + 1)
    ins, outs = refs[:4], refs[4:]
    for part, (first, count) in enumerate(GATHERED):
        mine = place_of(at, part, step)
        for index, which in enumerate((mine, 1 - mine)):
            rows = pl.ds(pl.multiple_of(which * size, size), size)
            value = ins[2 * part + index][...]
            if step == 0:
                outs[0][first : first + count, rows] = value
            else:
                outs[part][:, rows] = value


def window(views, starts):
    return jnp.concatenate([views[pl.ds(start, HW * HW), :] for start in starts], axis=0)


def old_hidden_kernel(views, natural, hidden):
    total = jnp.zeros((PIX, CO), WIDE)
    for tap in range(27):
        weights = natural[tap * CI : tap * CI + CI]
        starts = [view_start(tap, frame) for frame in range(FR)]
        total = total + jnp.dot(window(views, starts), weights, preferred_element_type=WIDE)
    hidden[...] = total


def add_taps(views, scaled, core):
    total = jnp.zeros((PIX, CO), WIDE)
    for slot in range(SLOTS):
        starts = [core_start(core, slot, frame) for frame in range(FR)]
        weights = scaled[slot]
        if slot == SLOTS - 1:
            weights = jnp.where(core == 0, weights.astype(WIDE), 0.0).astype(LOW)
        total = total + jnp.dot(window(views, starts), weights, preferred_element_type=WIDE)
    return total


def half_hidden_kernel(at, views, scaled, hidden):
    hidden[...] = add_taps(views, scaled, at[4])


def finish_kernel(
    at, plan, rate, col_moment, views, natural, master, mine, peer, old, own_part,
    update_far, master_far, new_row, new_col, next_output,
    factor, row_table, update_rows, new_master, stored,
):
    core = at[4]
    total = jnp.zeros((8, CO), WIDE)
    for side, piece in enumerate((mine, peer)):
        for sender in range(8):
            message = piece[MESSAGE, sender * BLK : sender * BLK + 16].astype(WIDE)
            message = message[:8] + message[8:]
            total = total + message
            for line in range(4):
                to = (side * 8 + sender) * 4 + line
                row_table[to : to + 1] = message[
                    6 + line // 2 : 7 + line // 2, line % 2 * 128 : line % 2 * 128 + 128
                ]
    store_factors(total, rate[0], col_moment, new_col, factor)

    lane = lax.broadcasted_iota(jnp.int32, (1, 128), 1)
    for line in range(7):
        values = jnp.zeros((1, 128), WIDE)
        for part in range(4):
            local = line * 4 + part
            side, slot, first, kernel, from_row, turn = (plan[local * 8 + item] for item in range(6))
            rows = slice(local * BLK, local * BLK + BLK)
            there = pl.ds(pl.multiple_of(first, BLK), BLK)
            value = jnp.where(
                side == 0, mine[slot, there, :].astype(WIDE), peer[slot, there, :].astype(WIDE)
            )
            update = value * factor[pl.ds(kernel, 1), :]
            update_rows[rows, :] = update
            new_master[rows, :] = master[rows, :] - learn_rate * update
            here = (lane >= part * BLK) & (lane < part * BLK + BLK)
            turned = pltpu.roll(row_table[pl.ds(from_row, 1), :], turn, 1)
            values = jnp.where(here, turned, values)
        new_row[line : line + 1] = values
    copies = fetch(((update_rows, update_far), (new_master, master_far)), stored)

    change = own_part[...] + add_taps(views, peer, 1 - core)
    hidden = old[...] - (learn_rate * factor[0:1]) * change
    small = jnp.where(core == 1, mine[SLOTS - 1].astype(WIDE), peer[SLOTS - 1].astype(WIDE))
    weights = natural[27 * CI :].astype(WIDE) - small * (learn_rate * factor[1:2])
    next_output[...] = jnp.dot(
        jax.nn.silu(hidden).astype(LOW), weights.astype(LOW), preferred_element_type=WIDE
    ).astype(LOW)
    for copy in copies:
        copy.wait()


def shards(
    step_count,
    block_order,
    saved_tiles,
    pre_act,
    grad_output,
    pointwise_live,
    master_rows,
    row_moment,
    col_moment,
    next_tiles,
):
    group, shard = lax.axis_index("group"), lax.axis_index("shard")
    axis_y, axis_x = group // 2, group % 2
    far, near, core = shard // 4, shard // 2 % 2, shard % 2
    at = jnp.stack([axis_x, axis_y, near, far, core]).astype(jnp.int32)
    decay_rate = 1.0 - step_count.astype(WIDE) ** (-decay_power)

    tile_peer = swap(saved_tiles, MASK_CORE)
    pre_peer = swap(pre_act, MASK_CORE)
    grad_peer = swap(grad_output, MASK_CORE)
    rows_far = [far_away(array) for array in (pre_act, grad_output, pointwise_live)]
    brought = call(
        own_kernel,
        [((BROUGHT, CI), LOW)],
        [SMEM, VMEM] + [HBM] * 3,
        scratch=[
            pltpu.VMEM((PIX, CO), LOW),
            pltpu.VMEM((PIX, CO), LOW),
            pltpu.VMEM((CO, CO), LOW),
            pltpu.SemaphoreType.DMA((3,)),
        ],
        moved=4 << 20,
    )(at, saved_tiles[0], *rows_far)[0]

    keep, *sends = call(
        term_kernel,
        [((SLOTS, 128, CO), LOW)] + [((count, 128, CO), LOW) for _, count in PARTS],
        [SMEM] + [VMEM] * 4 + [HBM] * 2,
        scratch=[
            pltpu.VMEM((BROUGHT, CI), LOW),
            pltpu.VMEM((2, 2 * PIX, CO), LOW),
            pltpu.VMEM((CO, CO), LOW),
            pltpu.SemaphoreType.DMA((2,)),
        ],
        flops=2 * 14 * 1024 * 256 * 256,
        moved=6 << 20,
        room=12,
    )(at, brought, tile_peer[0], pre_peer, grad_peer, *rows_far[1:])

    packed = call(
        pack_kernel,
        [((SLOTS + 1, 16, CO), LOW)],
        [SMEM] + [HBM] * 3,
        scratch=[
            pltpu.VMEM((SLOTS * 16, CO), WIDE),
            pltpu.VMEM((16, 128), WIDE),
            pltpu.SemaphoreType.DMA((2,)),
        ],
    )(at, keep, far_away(master_rows), far_away(row_moment.reshape(7, 128)))[0]
    packed_far = swap(packed, MASK_FAR)
    views = call(shift_kernel, [((3 * SHIFTED, CI), LOW)], [VMEM], moved=3 << 20)(next_tiles[0])[0]

    for step in range(1, 4):
        gots = [swap_part(send, part, step - 1) for part, send in enumerate(sends)]
        size = 256 >> (step + 1)
        outs = [((SLOTS, size, CO), LOW)] + [((count, size, CO), LOW) for _, count in PARTS]
        if step == 1:
            extra = [packed, packed_far]
            outs = outs + [((2, SLOTS + 1, 16, CO), LOW)]
        elif step == 2:
            extra = []
        else:
            extra = [pair, pair_near]
            outs = [((SLOTS, BLK, CO), LOW), ((4, SLOTS * 16, CO), LOW), ((4, 16, CO), LOW)]
        keep, *sends = call(
            functools.partial(fold_kernel, step),
            outs,
            [SMEM] + [VMEM] * (len(extra) + 3),
            moved=1 << 20,
        )(at, *extra, keep, *gots)
        if step == 1:
            pair = sends.pop()
            pair_near = swap(pair, MASK_NEAR)
    line, moments = sends
    line_one, line_two = swap(line, MASK_Y), swap(line, MASK_X)
    own_moment, plan = call(
        moments_kernel,
        [((BLK, 128), WIDE), ((NB,), jnp.int32)],
        [SMEM] * 2 + [VMEM] * 2,
        out_specs=[VMEM, SMEM],
        pin=False,
        scratch=[
            pltpu.VMEM((64, 128), WIDE),
            pltpu.VMEM((128, 128), WIDE),
            pltpu.SMEM((NB,), jnp.int32),
        ],
    )(at, block_order, moments, swap(moments, MASK_CORE))
    *scaled, lines = call(
        moment_kernel,
        [((count, BLK, CO), LOW) for _, count in GATHERED] + [((3, 4, SLOTS * 16, CO), LOW)],
        [SMEM] * 2 + [VMEM] * 6,
        moved=2 << 20,
    )(at, decay_rate, keep, swap(keep, MASK_FAR), own_moment, line, line_one, line_two)
    line_far = swap(line_one, MASK_X)
    natural = call(
        order_kernel, [((NB * BLK, CO), LOW)], [SMEM] * 2 + [VMEM] * 4, moved=8 << 20
    )(at, block_order, lines, line_far, swap(lines, MASK_CORE), swap(line_far, MASK_CORE))[0]

    joined = scaled
    for step in range(2, -1, -1):
        pieces = []
        for part, value in enumerate(joined):
            pieces += [value, swap_part(value, part, step)]
        size = 256 >> step
        outs = [((count, size, CO), LOW) for _, count in GATHERED]
        if step == 0:
            outs = [((SLOTS + 1, size, CO), LOW)]
        joined = call(
            functools.partial(widen_kernel, step), outs, [SMEM, HBM] + [VMEM] * len(pieces)
        )(at, (natural, line_far, views)[step], *pieces)
    mine = joined[0]
    peer = swap(mine, MASK_CORE)
    old = call(
        old_hidden_kernel,
        [((PIX, CO), WIDE)],
        [VMEM] * 2,
        flops=2 * 27 * 512 * 256 * 256,
        moved=6 << 20,
    )(views, natural)[0]
    half = call(
        half_hidden_kernel,
        [((PIX, CO), WIDE)],
        [SMEM] + [VMEM] * 2,
        flops=2 * 14 * 512 * 256 * 256,
        moved=4 << 20,
    )(at, views, mine)[0]

    outs = [
        ((NB // 8 * BLK, CO), WIDE),
        ((NB // 8 * BLK, CO), WIDE),
        ((7, 128), WIDE),
        ((2, CO), WIDE),
        ((PIX, CO), LOW),
    ]
    update_rows, new_master, new_row, new_col, next_output = call(
        finish_kernel,
        outs,
        [SMEM] * 3 + [VMEM] * 8,
        out_specs=[HBM] * 2 + [VMEM] * 3,
        scratch=[
            pltpu.VMEM((2, CO), WIDE),
            pltpu.VMEM((64, 128), WIDE),
            pltpu.VMEM((NB // 8 * BLK, CO), WIDE),
            pltpu.VMEM((NB // 8 * BLK, CO), WIDE),
            pltpu.SemaphoreType.DMA((2,)),
        ],
        pin=False,
        flops=2 * 16 * 512 * 256 * 256,
        moved=16 << 20,
        room=16,
    )(at, plan, decay_rate, col_moment, views, natural, master_rows, mine, peer, old, half)
    return (update_rows, new_master, new_row.reshape(-1), new_col, next_output)


def solution(mesh):
    in_specs = (
        P(),
        P(),
        P(("group", "shard"), None, None, None, None),
        P(("group", "shard"), None),
        P(("group", "shard"), None),
        P(),
        P("shard", None),
        P("shard"),
        P(),
        P(("group", "shard"), None, None, None, None),
    )
    out_specs = (P("shard", None), P("shard", None), P("shard"), P(), P(("group", "shard"), None))
    body = shards if (mesh.shape["group"], mesh.shape["shard"]) == (4, 8) else general_shards
    return jax.shard_map(body, mesh=mesh, in_specs=in_specs, out_specs=out_specs, check_vma=False)
```

```python
import functools
import jax
import jax.numpy as jnp
from jax import lax
from jax.experimental import pallas as pl
from jax.experimental.pallas import tpu as pltpu
from jax.sharding import PartitionSpec as P

CI = 256
CO = 256
BLK = 32
FR = 2
HW = 16
NB3 = 216
NB = 224


learn_rate = 0.002
decay_power = 0.8


def silu_slope(values):
    sigma = jax.nn.sigmoid(values)
    return sigma * (1.0 + values * (1.0 - sigma))


def tap_views(frames):
    views = []
    for frame_off in range(3):
        for row_off in range(3):
            for col_off in range(3):
                window = frames[
                    frame_off : frame_off + FR, row_off : row_off + HW, col_off : col_off + HW, :
                ]
                views.append(window.reshape(FR * HW * HW, CI))
    return views


def contract_rows(left, right):
    return lax.dot_general(
        left, right, (((0,), (0,)), ((), ())), preferred_element_type=jnp.float32
    )


def kernel_sums(values, is_small):
    large_part = jnp.sum(jnp.where(is_small[:, None], 0.0, values), axis=0)
    small_part = jnp.sum(jnp.where(is_small[:, None], values, 0.0), axis=0)
    return jnp.stack([large_part, small_part])


def general_shards(
    step_count,
    block_order,
    saved_tiles,
    pre_act,
    grad_output,
    pointwise_live,
    master_rows,
    row_moment,
    col_moment,
    next_tiles,
):
    pre_float = pre_act.astype(jnp.float32)
    activation = jax.nn.silu(pre_float).astype(jnp.bfloat16)
    grad_act = lax.dot_general(
        grad_output, pointwise_live, (((1,), (1,)), ((), ())), preferred_element_type=jnp.float32
    )
    grad_pre = (grad_act * silu_slope(pre_float)).astype(jnp.bfloat16)
    pieces = [contract_rows(view, grad_pre) for view in tap_views(saved_tiles[0])]
    pieces.append(contract_rows(activation, grad_output))
    own_term = jnp.concatenate(pieces, axis=0).astype(jnp.bfloat16)
    total_rows = NB * BLK
    stored = jnp.take(own_term.reshape(NB, BLK, CO), block_order, axis=0).reshape(total_rows, CO)
    own_rows = master_rows.shape[0]
    partial_value = lax.psum_scatter(stored, "shard", scatter_dimension=0, tiled=True).astype(
        jnp.float32
    )
    gradient = lax.psum(partial_value, "group")
    owner = lax.axis_index("shard")
    own_count = own_rows // BLK
    own_blocks = lax.dynamic_slice_in_dim(block_order, owner * own_count, own_count)
    is_small = jnp.repeat(own_blocks >= NB3, BLK, total_repeat_length=own_rows)
    decay_rate = 1.0 - step_count.astype(jnp.float32)[0] ** (-decay_power)
    counts = jnp.array([27 * CI, CO], jnp.float32)
    squares = gradient * gradient
    new_row = decay_rate * row_moment + (1.0 - decay_rate) * jnp.mean(squares, axis=1)
    col_part = kernel_sums(squares, is_small)
    row_part = kernel_sums(new_row[:, None], is_small)[:, 0]
    weighted = kernel_sums(squares / new_row[:, None], is_small)
    col_total, weight_total, row_total = lax.psum((col_part, weighted, row_part), "shard")
    new_col = decay_rate * col_moment + (1.0 - decay_rate) * col_total / counts[:, None]
    row_mean = row_total / counts
    col_rows = jnp.where(is_small[:, None], new_col[1], new_col[0])
    mean_rows = jnp.where(is_small, row_mean[1], row_mean[0])
    scaled = gradient / jnp.sqrt(new_row[:, None] * col_rows / mean_rows[:, None])
    square_total = row_mean * jnp.sum(weight_total / new_col, axis=1)
    clip_factor = jnp.maximum(1.0, jnp.sqrt(square_total / (counts * CO)))
    update_rows = scaled / jnp.where(is_small, clip_factor[1], clip_factor[0])[:, None]
    new_master = master_rows - learn_rate * update_rows
    weights_low = new_master.astype(jnp.bfloat16)
    gathered = lax.all_gather(weights_low, "shard", axis=0, tiled=True)
    inverse = jnp.zeros((NB,), jnp.int32).at[block_order].set(jnp.arange(NB, dtype=jnp.int32))
    natural = jnp.take(gathered.reshape(NB, BLK, CO), inverse, axis=0).reshape(total_rows, CO)
    spatial = natural[: 27 * CI].reshape(27, CI, CO)
    pointwise = natural[27 * CI :]
    hidden_sum = jnp.zeros((FR * HW * HW, CO), jnp.float32)
    for index_tap, view in enumerate(tap_views(next_tiles[0])):
        hidden_sum = hidden_sum + jnp.dot(
            view, spatial[index_tap], preferred_element_type=jnp.float32
        )
    hidden_act = jax.nn.silu(hidden_sum).astype(jnp.bfloat16)
    next_output = jnp.dot(hidden_act, pointwise, preferred_element_type=jnp.float32).astype(
        jnp.bfloat16
    )
    return (update_rows, new_master, new_row, new_col, next_output)


AXES = ("group", "shard")
SLOTS = 14
PIX = FR * HW * HW
SHIFTED = (FR + 2) * (HW + 2) * HW
SLOPES = 3 * SHIFTED
ACTS = SLOPES + PIX
BROUGHT = ACTS + PIX
LOW = jnp.bfloat16
WIDE = jnp.float32
VMEM = pl.BlockSpec(memory_space=pltpu.VMEM)
SMEM = pl.BlockSpec(memory_space=pltpu.SMEM)
HBM = pl.BlockSpec(memory_space=pl.ANY)
MASK_CORE, MASK_NEAR, MASK_FAR, MASK_X, MASK_Y = 1, 2, 4, 8, 16
PARTS = ((0, 10), (10, 4))
ORDERS = (((0, 1, 2), (1, 2, 0)), ((2, 0, 1), (2, 1, 0)))
MESSAGE = SLOTS
GATHERED = ((0, 10), (10, 5))
MASKS = (MASK_X, MASK_Y, MASK_NEAR)


def swap(value, mask):
    return lax.ppermute(value, AXES, [(at, at ^ mask) for at in range(32)])


def swap_mixed(value, masks):
    return lax.ppermute(value, AXES, [(at, at ^ masks[at & 1]) for at in range(32)])


def swap_part(value, part, step):
    return swap_mixed(value, [MASKS[ORDERS[part][core][step]] for core in range(2)])


def place_of(at, part, step):
    zero, one = (ORDERS[part][core][step] for core in range(2))
    return at[zero] if zero == one else jnp.where(at[4] == 0, at[zero], at[one])


def call(kernel, outs, in_specs, out_specs=None, scratch=(), flops=0, moved=0, room=8, pin=True):
    return pl.pallas_call(
        kernel,
        out_shape=[(pltpu.VMEM if pin else jax.ShapeDtypeStruct)(*out) for out in outs],
        in_specs=in_specs,
        out_specs=out_specs or [VMEM] * len(outs),
        scratch_shapes=list(scratch),
        compiler_params=pltpu.CompilerParams(vmem_limit_bytes=room << 20),
        cost_estimate=pl.CostEstimate(flops=flops, bytes_accessed=moved, transcendentals=0),
    )


def far_away(array):
    return pltpu.with_memory_space_constraint(array, pltpu.HBM)


def store_shifted(tile, out):
    for col_off in range(3):
        out[col_off * SHIFTED : (col_off + 1) * SHIFTED] = tile[
            :, :, col_off : col_off + HW, :
        ].reshape(SHIFTED, CI)


def shift_kernel(tile, out):
    store_shifted(tile, out)


def store_factors_of(pre, grad, pointwise, out):
    values = pre[...].astype(WIDE)
    sigma = jax.nn.sigmoid(values)
    grad_act = lax.dot_general(
        grad[...], pointwise[...], (((1,), (1,)), ((), ())), preferred_element_type=WIDE
    )
    out[SLOPES:ACTS] = (grad_act * (sigma * (1.0 + values * (1.0 - sigma)))).astype(LOW)
    out[ACTS:] = (values * sigma).astype(LOW)


def view_start(tap, frame):
    frame_off, row_off, col_off = tap // 9, tap // 3 % 3, tap % 3
    return col_off * SHIFTED + ((frame + frame_off) * (HW + 2) + row_off) * HW


def core_start(core, slot, frame):
    return pl.multiple_of(
        jnp.where(core == 0, view_start(slot, frame), view_start(min(SLOTS + slot, 26), frame)), HW
    )


def fetch(pairs, arrived):
    copies = [
        pltpu.make_async_copy(source, target, arrived.at[index])
        for index, (source, target) in enumerate(pairs)
    ]
    for copy in copies:
        copy.start()
    return copies


def own_kernel(
    at, tile, pre_far, grad_far, pointwise_far, brought, grad, pointwise, pre, arrived
):
    copies = fetch(((pre_far, pre), (grad_far, grad), (pointwise_far, pointwise)), arrived)
    store_shifted(tile, brought)
    for copy in copies:
        copy.wait()
    store_factors_of(pre, grad, pointwise, brought)


def pack_kernel(at, after, master_far, row_moment_far, packed, master, row_moment, arrived):
    quarter = pl.multiple_of((at[1] * 2 + at[0]) * (SLOTS * 16), SLOTS * 16)
    row_moment[...] = jnp.zeros((16, 128), WIDE)
    copies = fetch(
        (
            (master_far.at[pl.ds(quarter, SLOTS * 16), :], master),
            (row_moment_far, row_moment.at[pl.ds(0, 7), :]),
        ),
        arrived,
    )
    for copy in copies:
        copy.wait()
    packed[:SLOTS] = master[...].astype(LOW).reshape(SLOTS, 16, CO)
    high = row_moment[...].astype(LOW).astype(WIDE)
    packed[SLOTS] = jnp.concatenate([high, row_moment[...] - high], axis=1).astype(LOW)


def term_kernel(
    at, own, tile_peer, pre_peer, grad_peer, grad, pointwise, keep, send_one, send_two, peer, rights
):
    core = at[4]
    store_shifted(tile_peer, peer)
    store_factors_of(pre_peer, grad_peer, pointwise, peer)
    rights[0, :PIX] = own[SLOPES:ACTS]
    rights[0, PIX:] = peer[SLOPES:ACTS]
    rights[1, :PIX] = grad[...]
    rights[1, PIX:] = grad_peer[...]
    for slot in range(SLOTS):
        pieces = []
        for ref in (own, peer):
            for frame in range(FR):
                start = core_start(core, slot, frame)
                if slot == SLOTS - 1:
                    start = jnp.where(core == 0, start, ACTS + frame * HW * HW)
                pieces.append(ref[pl.ds(pl.multiple_of(start, HW), HW * HW), :])
        right = rights[core] if slot == SLOTS - 1 else rights[0]
        total = contract_rows(jnp.concatenate(pieces, axis=0), right)
        for part, ((first, count), send) in enumerate(zip(PARTS, (send_one, send_two))):
            if first <= slot < first + count:
                low, high, at_low = total[:128], total[128:], place_of(at, part, 0) == 0
                keep[slot] = jnp.where(at_low, low, high).astype(LOW)
                send[slot - first] = jnp.where(at_low, high, low).astype(LOW)


def fold_kernel(step, at, *refs):
    size = 256 >> (step + 1)
    extra = 0 if step == 2 else 2
    own, got = refs[:extra] or (None, None)
    refs = refs[extra:]
    keep, gots, stay, sends = refs[0], refs[1:3], refs[3], refs[4:]
    for part, (first, count) in enumerate(PARTS):
        here = slice(first, first + count)
        if step == 3:
            stay[here] = keep[here] + gots[part][...]
            continue
        mine = place_of(at, part, step)
        for which, out in ((mine, 0), (1 - mine, 1)):
            rows = pl.ds(pl.multiple_of(which * size, size), size)
            value = keep[here, rows] + gots[part][:, rows]
            if out == 0:
                stay[here] = value
            else:
                sends[part][...] = value
    if step == 1:
        pair = sends[2]
        pair[at[3]] = own[...]
        pair[1 - at[3]] = got[...]
    if step == 3:
        line, moments = sends
        for which, piece in ((at[2], own), (1 - at[2], got)):
            for far in range(2):
                line[far * 2 + which] = piece[far, :SLOTS].reshape(SLOTS * 16, CO)
                moments[far * 2 + which] = piece[far, SLOTS]


def moment_kernel(
    at, rate, own, got, moments, line, line_one, line_two, scaled_one, scaled_two, lines,
):
    for index, piece in enumerate((line, line_one, line_two)):
        lines[index] = piece[...]
    count = SLOTS * BLK
    total = (own[...].astype(WIDE) + got[...].astype(WIDE)).reshape(count, CO)
    squares = total * total
    decay = rate[0]
    mean = jnp.sum(squares, axis=1, keepdims=True) * (1.0 / CO)
    row_moment = jnp.concatenate([moments[:, slot : slot + 1] for slot in range(SLOTS)], axis=0)
    new_row = decay * row_moment + (1.0 - decay) * mean
    value = (total * lax.rsqrt(new_row)).astype(LOW).reshape(SLOTS, BLK, CO)
    split = PARTS[0][1]
    scaled_one[...] = value[:split]
    scaled_two[: SLOTS - split] = value[split:]
    weighted = squares / new_row
    cut = count - BLK
    last_small = at[4] == 1
    rows = []
    for values in (squares, weighted, jnp.broadcast_to(new_row, (count, CO))):
        large = jnp.sum(values[:cut], axis=0, keepdims=True)
        last = jnp.sum(values[cut:], axis=0, keepdims=True)
        rows.append(large + jnp.where(last_small, 0.0, last))
        rows.append(jnp.where(last_small, last, 0.0))
    spread = jnp.broadcast_to(new_row, (count, 128))
    spread = jnp.concatenate([spread, jnp.zeros((512 - count, 128), WIDE)], axis=0)
    rows += [jnp.transpose(spread[:CO])[:1], jnp.transpose(spread[CO:])[:1]]
    message = jnp.concatenate(rows, axis=0)
    high = message.astype(LOW).astype(WIDE)
    message = jnp.concatenate([high, message - high, jnp.zeros((16, CO), WIDE)], axis=0)
    scaled_two[SLOTS - split] = message.astype(LOW)


def store_factors(total, decay, col_moment, new_col, factor):
    for kernel in range(2):
        count = 27.0 * CI if kernel == 0 else float(CO)
        col = decay * col_moment[kernel : kernel + 1] + (1.0 - decay) * (
            total[kernel : kernel + 1] / count
        )
        row_mean = total[4 + kernel : 5 + kernel] / count
        square = row_mean * jnp.sum(
            total[2 + kernel : 3 + kernel] / col, axis=1, keepdims=True
        )
        clip = jnp.maximum(1.0, jnp.sqrt(square / (count * CO)))
        new_col[kernel : kernel + 1] = col
        factor[kernel : kernel + 1] = 1.0 / (jnp.sqrt(col / row_mean) * clip)


def moments_kernel(at, block_order, mine, peer, out, plan, table, rows, inverse):
    core = at[4]
    owner = at[3] * 4 + at[2] * 2 + core

    def place_block(local, carry):
        block = block_order[owner * (NB // 8) + local]
        half = (block >= 8 * SLOTS).astype(jnp.int32)
        slot, place = (block - half * (8 * SLOTS)) // 8, lax.rem(block, 8)
        high, middle, low = place // 4, lax.rem(place // 2, 2), lax.rem(place, 2)
        other = jnp.where(half == 0, low * 4 + high * 2 + middle, middle * 4 + high * 2 + low)
        sender = jnp.where(slot < PARTS[1][0], other, place)
        side = half ^ core
        plan[local * 8] = side
        plan[local * 8 + 1] = slot
        plan[local * 8 + 2] = place * BLK
        plan[local * 8 + 3] = (block >= NB3).astype(jnp.int32)
        plan[local * 8 + 4] = (side * 8 + sender) * 4 + slot // 4
        plan[local * 8 + 5] = lax.rem(128 + (lax.rem(local, 4) - lax.rem(slot, 4)) * BLK, 128)
        return carry

    lax.fori_loop(0, NB // 8, place_block, 0, unroll=4)
    for side, ref in enumerate((mine, peer)):
        for line in range(4):
            values = ref[line].astype(WIDE)
            values = values[:, :128] + values[:, 128:]
            table[pl.ds(pl.multiple_of((line * 2 + (core ^ side)) * 8, 8), 8), :] = values[:8]

    def invert(stored, carry):
        inverse[block_order[stored]] = stored
        return carry

    lax.fori_loop(0, NB, invert, 0, unroll=8)
    rows[...] = jnp.zeros((128, 128), WIDE)
    for part, (first, count) in enumerate(PARTS):
        place = place_of(at, part, 0) * 4 + place_of(at, part, 1) * 2 + place_of(at, part, 2)
        for slot in range(first, first + count):
            stored = inverse[(core * SLOTS + slot) * 8 + place]
            owner, local = stored // (NB // 8), lax.rem(stored, NB // 8)
            row = table[pl.ds(owner * 8 + local // 4, 1), :]
            turn = lax.rem(128 - lax.rem(local, 4) * BLK, 128)
            rows[slot : slot + 1] = pltpu.roll(row, turn, 1)
    out[...] = jnp.transpose(rows[...])[:BLK]


def order_kernel(at, block_order, mine, mine_low, mine_high, peer, peer_low, peer_high, out):
    count = NB // 8
    quarters = count // 4
    for flip_core, (pieces, low, high) in enumerate(
        ((mine, mine_low, mine_high), (peer, peer_low, peer_high))
    ):
        core = at[4] ^ flip_core
        for index in range(4):
            flip_x = jnp.where(core == 0, index // 2, index % 2)
            quarter = (at[1] ^ (index // 2) ^ (index % 2) ^ flip_x) * 2 + (at[0] ^ flip_x)
            for local in range(quarters):
                for line in range(4):
                    block = block_order[(line * 2 + core) * count + quarter * quarters + local]
                    to = pl.ds(pl.multiple_of(block * BLK, BLK), BLK)
                    rows = slice(local * BLK, local * BLK + BLK)
                    if index < 3:
                        out[to, :] = pieces[index, line, rows]
                    else:
                        out[to, :] = (low, high)[line // 2][line % 2, rows]


def widen_kernel(step, at, after, *refs):
    size = 256 >> (step + 1)
    ins, outs = refs[:4], refs[4:]
    if step == 1:
        outs[2][...], outs[3][...] = after[:2], after[2:]
    for part, (first, count) in enumerate(GATHERED):
        mine = place_of(at, part, step)
        for index, which in enumerate((mine, 1 - mine)):
            rows = pl.ds(pl.multiple_of(which * size, size), size)
            value = ins[2 * part + index][...]
            if step == 0:
                outs[0][first : first + count, rows] = value
            else:
                outs[part][:, rows] = value


def window(views, starts):
    return jnp.concatenate([views[pl.ds(start, HW * HW), :] for start in starts], axis=0)


def old_hidden_kernel(views, natural, hidden):
    total = jnp.zeros((PIX, CO), WIDE)
    for tap in range(27):
        weights = natural[tap * CI : tap * CI + CI]
        starts = [view_start(tap, frame) for frame in range(FR)]
        total = total + jnp.dot(window(views, starts), weights, preferred_element_type=WIDE)
    hidden[...] = total


def add_taps(views, scaled, core):
    total = jnp.zeros((PIX, CO), WIDE)
    for slot in range(SLOTS):
        starts = [core_start(core, slot, frame) for frame in range(FR)]
        weights = scaled[slot]
        if slot == SLOTS - 1:
            weights = jnp.where(core == 0, weights.astype(WIDE), 0.0).astype(LOW)
        total = total + jnp.dot(window(views, starts), weights, preferred_element_type=WIDE)
    return total


def half_hidden_kernel(at, views, scaled, hidden):
    hidden[...] = add_taps(views, scaled, at[4])


def finish_kernel(
    at, plan, rate, col_moment, views, natural, master, mine, peer, old, own_part,
    update_far, master_far, new_row, new_col, next_output,
    factor, row_table, update_rows, new_master, stored,
):
    core = at[4]
    total = jnp.zeros((8, CO), WIDE)
    for side, piece in enumerate((mine, peer)):
        for sender in range(8):
            message = piece[MESSAGE, sender * BLK : sender * BLK + 16].astype(WIDE)
            message = message[:8] + message[8:]
            total = total + message
            for line in range(4):
                to = (side * 8 + sender) * 4 + line
                row_table[to : to + 1] = message[
                    6 + line // 2 : 7 + line // 2, line % 2 * 128 : line % 2 * 128 + 128
                ]
    store_factors(total, rate[0], col_moment, new_col, factor)

    lane = lax.broadcasted_iota(jnp.int32, (1, 128), 1)
    copies = []
    for line in range(7):
        values = jnp.zeros((1, 128), WIDE)
        for part in range(4):
            local = line * 4 + part
            side, slot, first, kernel, from_row, turn = (plan[local * 8 + item] for item in range(6))
            rows = slice(local * BLK, local * BLK + BLK)
            there = pl.ds(pl.multiple_of(first, BLK), BLK)
            value = jnp.where(
                side == 0, mine[slot, there, :].astype(WIDE), peer[slot, there, :].astype(WIDE)
            )
            update = value * factor[pl.ds(kernel, 1), :]
            update_rows[rows, :] = update
            new_master[rows, :] = master[rows, :] - learn_rate * update
            here = (lane >= part * BLK) & (lane < part * BLK + BLK)
            turned = pltpu.roll(row_table[pl.ds(from_row, 1), :], turn, 1)
            values = jnp.where(here, turned, values)
        new_row[line : line + 1] = values
        there = pl.ds(line * 4 * BLK, 4 * BLK)
        pairs = ((update_rows, update_far), (new_master, master_far))
        copies += fetch(
            [(source.at[there, :], target.at[there, :]) for source, target in pairs],
            stored.at[line],
        )

    change = own_part[...] + add_taps(views, peer, 1 - core)
    hidden = old[...] - (learn_rate * factor[0:1]) * change
    small = jnp.where(core == 1, mine[SLOTS - 1].astype(WIDE), peer[SLOTS - 1].astype(WIDE))
    weights = natural[27 * CI :].astype(WIDE) - small * (learn_rate * factor[1:2])
    next_output[...] = jnp.dot(
        jax.nn.silu(hidden).astype(LOW), weights.astype(LOW), preferred_element_type=WIDE
    ).astype(LOW)
    for copy in copies:
        copy.wait()


def shards(
    step_count,
    block_order,
    saved_tiles,
    pre_act,
    grad_output,
    pointwise_live,
    master_rows,
    row_moment,
    col_moment,
    next_tiles,
):
    group, shard = lax.axis_index("group"), lax.axis_index("shard")
    axis_y, axis_x = group // 2, group % 2
    far, near, core = shard // 4, shard // 2 % 2, shard % 2
    at = jnp.stack([axis_x, axis_y, near, far, core]).astype(jnp.int32)
    decay_rate = 1.0 - step_count.astype(WIDE) ** (-decay_power)

    tile_peer = swap(saved_tiles, MASK_CORE)
    pre_peer = swap(pre_act, MASK_CORE)
    grad_peer = swap(grad_output, MASK_CORE)
    rows_far = [far_away(array) for array in (pre_act, grad_output, pointwise_live)]
    brought, grad_near, pointwise_near = call(
        own_kernel,
        [((BROUGHT, CI), LOW), ((PIX, CO), LOW), ((CO, CO), LOW)],
        [SMEM, VMEM] + [HBM] * 3,
        scratch=[pltpu.VMEM((PIX, CO), LOW), pltpu.SemaphoreType.DMA((3,))],
        moved=4 << 20,
    )(at, saved_tiles[0], *rows_far)

    keep, *sends = call(
        term_kernel,
        [((SLOTS, 128, CO), LOW)] + [((count, 128, CO), LOW) for _, count in PARTS],
        [SMEM] + [VMEM] * 6,
        scratch=[pltpu.VMEM((BROUGHT, CI), LOW), pltpu.VMEM((2, 2 * PIX, CO), LOW)],
        flops=2 * 14 * 1024 * 256 * 256,
        moved=6 << 20,
        room=12,
    )(at, brought, tile_peer[0], pre_peer, grad_peer, grad_near, pointwise_near)

    packed = call(
        pack_kernel,
        [((SLOTS + 1, 16, CO), LOW)],
        [SMEM] + [HBM] * 3,
        scratch=[
            pltpu.VMEM((SLOTS * 16, CO), WIDE),
            pltpu.VMEM((16, 128), WIDE),
            pltpu.SemaphoreType.DMA((2,)),
        ],
    )(at, keep, far_away(master_rows), far_away(row_moment.reshape(7, 128)))[0]
    packed_far = swap(packed, MASK_FAR)
    views = call(shift_kernel, [((3 * SHIFTED, CI), LOW)], [VMEM], moved=3 << 20)(next_tiles[0])[0]

    for step in range(1, 4):
        gots = [swap_part(send, part, step - 1) for part, send in enumerate(sends)]
        size = 256 >> (step + 1)
        outs = [((SLOTS, size, CO), LOW)] + [((count, size, CO), LOW) for _, count in PARTS]
        if step == 1:
            extra = [packed, packed_far]
            outs = outs + [((2, SLOTS + 1, 16, CO), LOW)]
        elif step == 2:
            extra = []
        else:
            extra = [pair, pair_near]
            outs = [((SLOTS, BLK, CO), LOW), ((4, SLOTS * 16, CO), LOW), ((4, 16, CO), LOW)]
        keep, *sends = call(
            functools.partial(fold_kernel, step),
            outs,
            [SMEM] + [VMEM] * (len(extra) + 3),
            moved=1 << 20,
        )(at, *extra, keep, *gots)
        if step == 1:
            pair = sends.pop()
            pair_near = swap(pair, MASK_NEAR)
    line, moments = sends
    line_one, line_two = swap_mixed(line, (MASK_Y, MASK_X)), swap_mixed(line, (MASK_X, MASK_Y))
    own_moment, plan = call(
        moments_kernel,
        [((BLK, 128), WIDE), ((NB,), jnp.int32)],
        [SMEM] * 2 + [VMEM] * 2,
        out_specs=[VMEM, SMEM],
        pin=False,
        scratch=[
            pltpu.VMEM((64, 128), WIDE),
            pltpu.VMEM((128, 128), WIDE),
            pltpu.SMEM((NB,), jnp.int32),
        ],
    )(at, block_order, moments, swap(moments, MASK_CORE))
    *scaled, lines = call(
        moment_kernel,
        [((count, BLK, CO), LOW) for _, count in GATHERED] + [((3, 4, SLOTS * 16, CO), LOW)],
        [SMEM] * 2 + [VMEM] * 6,
        moved=2 << 20,
    )(at, decay_rate, keep, swap(keep, MASK_FAR), own_moment, line, line_one, line_two)
    line_far = swap_mixed(line_one, (MASK_X, MASK_Y))
    joined, natural = scaled, None
    for step in range(2, -1, -1):
        pieces = []
        for part, value in enumerate(joined):
            pieces += [value, swap_part(value, part, step)]
        size = 256 >> step
        outs = [((count, size, CO), LOW) for _, count in GATHERED]
        if step == 0:
            outs = [((SLOTS + 1, size, CO), LOW)]
        if step == 1:
            outs = outs + [((2, SLOTS * 16, CO), LOW)] * 2
        joined = call(
            functools.partial(widen_kernel, step),
            outs,
            [SMEM, VMEM if step == 1 else HBM] + [VMEM] * len(pieces),
        )(at, (natural, line_far, views)[step], *pieces)
        if step == 1:
            parts = [lines, *joined[2:]]
            joined = joined[:2]
            natural = call(
                order_kernel, [((NB * BLK, CO), LOW)], [SMEM] * 2 + [VMEM] * 6, moved=8 << 20
            )(at, block_order, *parts, *[swap(part, MASK_CORE) for part in parts])[0]
    mine = joined[0]
    peer = swap(mine, MASK_CORE)
    old = call(
        old_hidden_kernel,
        [((PIX, CO), WIDE)],
        [VMEM] * 2,
        flops=2 * 27 * 512 * 256 * 256,
        moved=6 << 20,
    )(views, natural)[0]
    half = call(
        half_hidden_kernel,
        [((PIX, CO), WIDE)],
        [SMEM] + [VMEM] * 2,
        flops=2 * 14 * 512 * 256 * 256,
        moved=4 << 20,
    )(at, views, mine)[0]

    outs = [
        ((NB // 8 * BLK, CO), WIDE),
        ((NB // 8 * BLK, CO), WIDE),
        ((7, 128), WIDE),
        ((2, CO), WIDE),
        ((PIX, CO), LOW),
    ]
    update_rows, new_master, new_row, new_col, next_output = call(
        finish_kernel,
        outs,
        [SMEM] * 3 + [VMEM] * 8,
        out_specs=[HBM] * 2 + [VMEM] * 3,
        scratch=[
            pltpu.VMEM((2, CO), WIDE),
            pltpu.VMEM((64, 128), WIDE),
            pltpu.VMEM((NB // 8 * BLK, CO), WIDE),
            pltpu.VMEM((NB // 8 * BLK, CO), WIDE),
            pltpu.SemaphoreType.DMA((7, 2)),
        ],
        pin=False,
        flops=2 * 16 * 512 * 256 * 256,
        moved=16 << 20,
        room=16,
    )(at, plan, decay_rate, col_moment, views, natural, master_rows, mine, peer, old, half)
    return (update_rows, new_master, new_row.reshape(-1), new_col, next_output)


def solution(mesh):
    in_specs = (
        P(),
        P(),
        P(("group", "shard"), None, None, None, None),
        P(("group", "shard"), None),
        P(("group", "shard"), None),
        P(),
        P("shard", None),
        P("shard"),
        P(),
        P(("group", "shard"), None, None, None, None),
    )
    out_specs = (P("shard", None), P("shard", None), P("shard"), P(), P(("group", "shard"), None))
    body = shards if (mesh.shape["group"], mesh.shape["shard"]) == (4, 8) else general_shards
    return jax.shard_map(body, mesh=mesh, in_specs=in_specs, out_specs=out_specs, check_vma=False)
```

```python
import functools
import jax
import jax.numpy as jnp
from jax import lax
from jax.experimental import pallas as pl
from jax.experimental.pallas import tpu as pltpu
from jax.sharding import PartitionSpec as P

CI = 256
CO = 256
BLK = 32
FR = 2
HW = 16
NB3 = 216
NB = 224


learn_rate = 0.002
decay_power = 0.8


def silu_slope(values):
    sigma = jax.nn.sigmoid(values)
    return sigma * (1.0 + values * (1.0 - sigma))


def tap_views(frames):
    views = []
    for frame_off in range(3):
        for row_off in range(3):
            for col_off in range(3):
                window = frames[
                    frame_off : frame_off + FR, row_off : row_off + HW, col_off : col_off + HW, :
                ]
                views.append(window.reshape(FR * HW * HW, CI))
    return views


def contract_rows(left, right):
    return lax.dot_general(
        left, right, (((0,), (0,)), ((), ())), preferred_element_type=jnp.float32
    )


def kernel_sums(values, is_small):
    large_part = jnp.sum(jnp.where(is_small[:, None], 0.0, values), axis=0)
    small_part = jnp.sum(jnp.where(is_small[:, None], values, 0.0), axis=0)
    return jnp.stack([large_part, small_part])


def general_shards(
    step_count,
    block_order,
    saved_tiles,
    pre_act,
    grad_output,
    pointwise_live,
    master_rows,
    row_moment,
    col_moment,
    next_tiles,
):
    pre_float = pre_act.astype(jnp.float32)
    activation = jax.nn.silu(pre_float).astype(jnp.bfloat16)
    grad_act = lax.dot_general(
        grad_output, pointwise_live, (((1,), (1,)), ((), ())), preferred_element_type=jnp.float32
    )
    grad_pre = (grad_act * silu_slope(pre_float)).astype(jnp.bfloat16)
    pieces = [contract_rows(view, grad_pre) for view in tap_views(saved_tiles[0])]
    pieces.append(contract_rows(activation, grad_output))
    own_term = jnp.concatenate(pieces, axis=0).astype(jnp.bfloat16)
    total_rows = NB * BLK
    stored = jnp.take(own_term.reshape(NB, BLK, CO), block_order, axis=0).reshape(total_rows, CO)
    own_rows = master_rows.shape[0]
    partial_value = lax.psum_scatter(stored, "shard", scatter_dimension=0, tiled=True).astype(
        jnp.float32
    )
    gradient = lax.psum(partial_value, "group")
    owner = lax.axis_index("shard")
    own_count = own_rows // BLK
    own_blocks = lax.dynamic_slice_in_dim(block_order, owner * own_count, own_count)
    is_small = jnp.repeat(own_blocks >= NB3, BLK, total_repeat_length=own_rows)
    decay_rate = 1.0 - step_count.astype(jnp.float32)[0] ** (-decay_power)
    counts = jnp.array([27 * CI, CO], jnp.float32)
    squares = gradient * gradient
    new_row = decay_rate * row_moment + (1.0 - decay_rate) * jnp.mean(squares, axis=1)
    col_part = kernel_sums(squares, is_small)
    row_part = kernel_sums(new_row[:, None], is_small)[:, 0]
    weighted = kernel_sums(squares / new_row[:, None], is_small)
    col_total, weight_total, row_total = lax.psum((col_part, weighted, row_part), "shard")
    new_col = decay_rate * col_moment + (1.0 - decay_rate) * col_total / counts[:, None]
    row_mean = row_total / counts
    col_rows = jnp.where(is_small[:, None], new_col[1], new_col[0])
    mean_rows = jnp.where(is_small, row_mean[1], row_mean[0])
    scaled = gradient / jnp.sqrt(new_row[:, None] * col_rows / mean_rows[:, None])
    square_total = row_mean * jnp.sum(weight_total / new_col, axis=1)
    clip_factor = jnp.maximum(1.0, jnp.sqrt(square_total / (counts * CO)))
    update_rows = scaled / jnp.where(is_small, clip_factor[1], clip_factor[0])[:, None]
    new_master = master_rows - learn_rate * update_rows
    weights_low = new_master.astype(jnp.bfloat16)
    gathered = lax.all_gather(weights_low, "shard", axis=0, tiled=True)
    inverse = jnp.zeros((NB,), jnp.int32).at[block_order].set(jnp.arange(NB, dtype=jnp.int32))
    natural = jnp.take(gathered.reshape(NB, BLK, CO), inverse, axis=0).reshape(total_rows, CO)
    spatial = natural[: 27 * CI].reshape(27, CI, CO)
    pointwise = natural[27 * CI :]
    hidden_sum = jnp.zeros((FR * HW * HW, CO), jnp.float32)
    for index_tap, view in enumerate(tap_views(next_tiles[0])):
        hidden_sum = hidden_sum + jnp.dot(
            view, spatial[index_tap], preferred_element_type=jnp.float32
        )
    hidden_act = jax.nn.silu(hidden_sum).astype(jnp.bfloat16)
    next_output = jnp.dot(hidden_act, pointwise, preferred_element_type=jnp.float32).astype(
        jnp.bfloat16
    )
    return (update_rows, new_master, new_row, new_col, next_output)


AXES = ("group", "shard")
SLOTS = 14
PIX = FR * HW * HW
SHIFTED = (FR + 2) * (HW + 2) * HW
SLOPES = 3 * SHIFTED
ACTS = SLOPES + PIX
BROUGHT = ACTS + PIX
LOW = jnp.bfloat16
WIDE = jnp.float32
VMEM = pl.BlockSpec(memory_space=pltpu.VMEM)
SMEM = pl.BlockSpec(memory_space=pltpu.SMEM)
HBM = pl.BlockSpec(memory_space=pl.ANY)
MASK_CORE, MASK_NEAR, MASK_FAR, MASK_X, MASK_Y = 1, 2, 4, 8, 16
PARTS = ((0, 10), (10, 4))
ORDERS = (((0, 1, 2), (1, 0, 2)), ((2, 0, 1), (2, 1, 0)))
MESSAGE = SLOTS
GATHERED = ((0, 10), (10, 5))
MASKS = (MASK_X, MASK_Y, MASK_NEAR)


def swap(value, mask):
    return lax.ppermute(value, AXES, [(at, at ^ mask) for at in range(32)])


def swap_mixed(value, masks):
    return lax.ppermute(value, AXES, [(at, at ^ masks[at & 1]) for at in range(32)])


def swap_part(value, part, step):
    return swap_mixed(value, [MASKS[ORDERS[part][core][step]] for core in range(2)])


def place_of(at, part, step):
    zero, one = (ORDERS[part][core][step] for core in range(2))
    return at[zero] if zero == one else jnp.where(at[4] == 0, at[zero], at[one])


def position():
    group, shard = lax.axis_index("group"), lax.axis_index("shard")
    return group % 2, group // 2, shard // 2 % 2, shard // 4, shard % 2


def call(kernel, outs, in_specs, out_specs=None, scratch=(), flops=0, moved=0, room=8, pin=True):
    return pl.pallas_call(
        lambda *refs: kernel(position(), *refs),
        out_shape=[(pltpu.VMEM if pin else jax.ShapeDtypeStruct)(*out) for out in outs],
        in_specs=in_specs,
        out_specs=out_specs or [VMEM] * len(outs),
        scratch_shapes=list(scratch),
        compiler_params=pltpu.CompilerParams(vmem_limit_bytes=room << 20),
        cost_estimate=pl.CostEstimate(flops=flops, bytes_accessed=moved, transcendentals=0),
    )


def far_away(array):
    return pltpu.with_memory_space_constraint(array, pltpu.HBM)


def store_shifted(tile, out):
    for col_off in range(3):
        out[col_off * SHIFTED : (col_off + 1) * SHIFTED] = tile[
            :, :, col_off : col_off + HW, :
        ].reshape(SHIFTED, CI)


def shift_kernel(at, tile, out):
    store_shifted(tile, out)


def store_factors_of(pre, grad, pointwise, out):
    values = pre[...].astype(WIDE)
    sigma = jax.nn.sigmoid(values)
    grad_act = lax.dot_general(
        grad[...], pointwise[...], (((1,), (1,)), ((), ())), preferred_element_type=WIDE
    )
    out[SLOPES:ACTS] = (grad_act * (sigma * (1.0 + values * (1.0 - sigma)))).astype(LOW)
    out[ACTS:] = (values * sigma).astype(LOW)


def view_start(tap, frame):
    frame_off, row_off, col_off = tap // 9, tap // 3 % 3, tap % 3
    return col_off * SHIFTED + ((frame + frame_off) * (HW + 2) + row_off) * HW


def core_start(core, slot, frame):
    return pl.multiple_of(
        jnp.where(core == 0, view_start(slot, frame), view_start(min(SLOTS + slot, 26), frame)), HW
    )


def fetch(pairs, arrived):
    copies = [
        pltpu.make_async_copy(source, target, arrived.at[index])
        for index, (source, target) in enumerate(pairs)
    ]
    for copy in copies:
        copy.start()
    return copies


def own_kernel(
    at, tile, pre_far, grad_far, pointwise_far, brought, grad, pointwise, pre, arrived
):
    copies = fetch(((pre_far, pre), (grad_far, grad), (pointwise_far, pointwise)), arrived)
    store_shifted(tile, brought)
    for copy in copies:
        copy.wait()
    store_factors_of(pre, grad, pointwise, brought)


def pack_kernel(at, after, master_far, row_moment_far, packed, master, row_moment, arrived):
    quarter = pl.multiple_of((at[1] * 2 + at[0]) * (SLOTS * 16), SLOTS * 16)
    row_moment[...] = jnp.zeros((16, 128), WIDE)
    copies = fetch(
        (
            (master_far.at[pl.ds(quarter, SLOTS * 16), :], master),
            (row_moment_far, row_moment.at[pl.ds(0, 7), :]),
        ),
        arrived,
    )
    for copy in copies:
        copy.wait()
    packed[:SLOTS] = master[...].astype(LOW).reshape(SLOTS, 16, CO)
    high = row_moment[...].astype(LOW).astype(WIDE)
    packed[SLOTS] = jnp.concatenate([high, row_moment[...] - high], axis=1).astype(LOW)


def term_kernel(
    at, own, tile_peer, pre_peer, grad_peer, grad, pointwise, keep, send_one, send_two, peer, rights
):
    core = at[4]
    store_shifted(tile_peer, peer)
    store_factors_of(pre_peer, grad_peer, pointwise, peer)
    rights[0, :PIX] = own[SLOPES:ACTS]
    rights[0, PIX:] = peer[SLOPES:ACTS]
    rights[1, :PIX] = grad[...]
    rights[1, PIX:] = grad_peer[...]
    for slot in range(SLOTS):
        pieces = []
        for ref in (own, peer):
            for frame in range(FR):
                start = core_start(core, slot, frame)
                if slot == SLOTS - 1:
                    start = jnp.where(core == 0, start, ACTS + frame * HW * HW)
                pieces.append(ref[pl.ds(pl.multiple_of(start, HW), HW * HW), :])
        right = rights[core] if slot == SLOTS - 1 else rights[0]
        total = contract_rows(jnp.concatenate(pieces, axis=0), right)
        for part, ((first, count), send) in enumerate(zip(PARTS, (send_one, send_two))):
            if first <= slot < first + count:
                low, high, at_low = total[:128], total[128:], place_of(at, part, 0) == 0
                keep[slot] = jnp.where(at_low, low, high).astype(LOW)
                send[slot - first] = jnp.where(at_low, high, low).astype(LOW)


def fold_kernel(step, at, *refs):
    size = 256 >> (step + 1)
    extra = 0 if step == 2 else 2
    own, got = refs[:extra] or (None, None)
    refs = refs[extra:]
    keep, gots, stay, sends = refs[0], refs[1:3], refs[3], refs[4:]
    for part, (first, count) in enumerate(PARTS):
        here = slice(first, first + count)
        if step == 3:
            stay[here] = keep[here] + gots[part][...]
            continue
        mine = place_of(at, part, step)
        for which, out in ((mine, 0), (1 - mine, 1)):
            rows = pl.ds(pl.multiple_of(which * size, size), size)
            value = keep[here, rows] + gots[part][:, rows]
            if out == 0:
                stay[here] = value
            else:
                sends[part][...] = value
    if step == 1:
        pair = sends[2]
        pair[at[3]] = own[...]
        pair[1 - at[3]] = got[...]
    if step == 3:
        line, moments = sends
        for which, piece in ((at[2], own), (1 - at[2], got)):
            for far in range(2):
                line[far * 2 + which] = piece[far, :SLOTS].reshape(SLOTS * 16, CO)
                moments[far * 2 + which] = piece[far, SLOTS]


def moment_kernel(
    at, rate, own, got, moments, line, line_one, line_two, scaled_one, scaled_two, lines,
):
    for index, piece in enumerate((line, line_one, line_two)):
        lines[index] = piece[...]
    count = SLOTS * BLK
    total = (own[...].astype(WIDE) + got[...].astype(WIDE)).reshape(count, CO)
    squares = total * total
    decay = rate[0]
    mean = jnp.sum(squares, axis=1, keepdims=True) * (1.0 / CO)
    row_moment = jnp.concatenate([moments[:, slot : slot + 1] for slot in range(SLOTS)], axis=0)
    new_row = decay * row_moment + (1.0 - decay) * mean
    value = (total * lax.rsqrt(new_row)).astype(LOW).reshape(SLOTS, BLK, CO)
    split = PARTS[0][1]
    scaled_one[...] = value[:split]
    scaled_two[: SLOTS - split] = value[split:]
    weighted = squares / new_row
    cut = count - BLK
    last_small = at[4] == 1
    rows = []
    for values in (squares, weighted, jnp.broadcast_to(new_row, (count, CO))):
        large = jnp.sum(values[:cut], axis=0, keepdims=True)
        last = jnp.sum(values[cut:], axis=0, keepdims=True)
        rows.append(large + jnp.where(last_small, 0.0, last))
        rows.append(jnp.where(last_small, last, 0.0))
    spread = jnp.broadcast_to(new_row, (count, 128))
    spread = jnp.concatenate([spread, jnp.zeros((512 - count, 128), WIDE)], axis=0)
    rows += [jnp.transpose(spread[:CO])[:1], jnp.transpose(spread[CO:])[:1]]
    message = jnp.concatenate(rows, axis=0)
    high = message.astype(LOW).astype(WIDE)
    message = jnp.concatenate([high, message - high, jnp.zeros((16, CO), WIDE)], axis=0)
    scaled_two[SLOTS - split] = message.astype(LOW)


def store_factors(total, decay, col_moment, new_col, factor):
    for kernel in range(2):
        count = 27.0 * CI if kernel == 0 else float(CO)
        col = decay * col_moment[kernel : kernel + 1] + (1.0 - decay) * (
            total[kernel : kernel + 1] / count
        )
        row_mean = total[4 + kernel : 5 + kernel] / count
        square = row_mean * jnp.sum(
            total[2 + kernel : 3 + kernel] / col, axis=1, keepdims=True
        )
        clip = jnp.maximum(1.0, jnp.sqrt(square / (count * CO)))
        new_col[kernel : kernel + 1] = col
        factor[kernel : kernel + 1] = 1.0 / (jnp.sqrt(col / row_mean) * clip)


def moments_kernel(at, block_order, mine, peer, out, plan, table, rows, inverse):
    core = at[4]
    owner = at[3] * 4 + at[2] * 2 + core

    def place_block(local, carry):
        block = block_order[owner * (NB // 8) + local]
        half = (block >= 8 * SLOTS).astype(jnp.int32)
        slot, place = (block - half * (8 * SLOTS)) // 8, lax.rem(block, 8)
        high, middle, low = place // 4, lax.rem(place // 2, 2), lax.rem(place, 2)
        other = low * 4 + high * 2 + middle
        sender = jnp.where(slot < PARTS[1][0], other, place)
        side = half ^ core
        plan[local * 8] = side
        plan[local * 8 + 1] = slot
        plan[local * 8 + 2] = place * BLK
        plan[local * 8 + 3] = (block >= NB3).astype(jnp.int32)
        plan[local * 8 + 4] = (side * 8 + sender) * 4 + slot // 4
        plan[local * 8 + 5] = lax.rem(128 + (lax.rem(local, 4) - lax.rem(slot, 4)) * BLK, 128)
        return carry

    lax.fori_loop(0, NB // 8, place_block, 0, unroll=4)
    for side, ref in enumerate((mine, peer)):
        for line in range(4):
            values = ref[line].astype(WIDE)
            values = values[:, :128] + values[:, 128:]
            table[pl.ds(pl.multiple_of((line * 2 + (core ^ side)) * 8, 8), 8), :] = values[:8]

    def invert(stored, carry):
        inverse[block_order[stored]] = stored
        return carry

    lax.fori_loop(0, NB, invert, 0, unroll=8)
    rows[...] = jnp.zeros((128, 128), WIDE)
    for part, (first, count) in enumerate(PARTS):
        place = place_of(at, part, 0) * 4 + place_of(at, part, 1) * 2 + place_of(at, part, 2)
        for slot in range(first, first + count):
            stored = inverse[(core * SLOTS + slot) * 8 + place]
            owner, local = stored // (NB // 8), lax.rem(stored, NB // 8)
            row = table[pl.ds(owner * 8 + local // 4, 1), :]
            turn = lax.rem(128 - lax.rem(local, 4) * BLK, 128)
            rows[slot : slot + 1] = pltpu.roll(row, turn, 1)
    out[...] = jnp.transpose(rows[...])[:BLK]


def order_kernel(at, block_order, mine, mine_low, mine_high, peer, peer_low, peer_high, out):
    count = NB // 8
    quarters = count // 4
    for flip_core, (pieces, low, high) in enumerate(
        ((mine, mine_low, mine_high), (peer, peer_low, peer_high))
    ):
        core = at[4] ^ flip_core
        for index in range(4):
            flip_x = jnp.where(core == 0, index // 2, index % 2)
            quarter = (at[1] ^ (index // 2) ^ (index % 2) ^ flip_x) * 2 + (at[0] ^ flip_x)
            for local in range(quarters):
                for line in range(4):
                    block = block_order[(line * 2 + core) * count + quarter * quarters + local]
                    to = pl.ds(pl.multiple_of(block * BLK, BLK), BLK)
                    rows = slice(local * BLK, local * BLK + BLK)
                    if index < 3:
                        out[to, :] = pieces[index, line, rows]
                    else:
                        out[to, :] = (low, high)[line // 2][line % 2, rows]


def widen_kernel(step, at, after, *refs):
    size = 256 >> (step + 1)
    ins, outs = refs[:4], refs[4:]
    if step == 1:
        outs[2][...], outs[3][...] = after[:2], after[2:]
    for part, (first, count) in enumerate(GATHERED):
        mine = place_of(at, part, step)
        for index, which in enumerate((mine, 1 - mine)):
            rows = pl.ds(pl.multiple_of(which * size, size), size)
            value = ins[2 * part + index][...]
            if step == 0:
                outs[0][first : first + count, rows] = value
            else:
                outs[part][:, rows] = value


def window(views, starts):
    return jnp.concatenate([views[pl.ds(start, HW * HW), :] for start in starts], axis=0)


def old_hidden_kernel(at, views, natural, hidden):
    total = jnp.zeros((PIX, CO), WIDE)
    for tap in range(27):
        weights = natural[tap * CI : tap * CI + CI]
        starts = [view_start(tap, frame) for frame in range(FR)]
        total = total + jnp.dot(window(views, starts), weights, preferred_element_type=WIDE)
    hidden[...] = total


def add_taps(views, scaled, core):
    total = jnp.zeros((PIX, CO), WIDE)
    for slot in range(SLOTS):
        starts = [core_start(core, slot, frame) for frame in range(FR)]
        weights = scaled[slot]
        if slot == SLOTS - 1:
            weights = jnp.where(core == 0, weights.astype(WIDE), 0.0).astype(LOW)
        total = total + jnp.dot(window(views, starts), weights, preferred_element_type=WIDE)
    return total


def half_hidden_kernel(at, views, scaled, hidden):
    hidden[...] = add_taps(views, scaled, at[4])


def finish_kernel(
    at, plan, rate, col_moment, views, natural, master, mine, peer, old, own_part,
    update_far, master_far, new_row, new_col, next_output,
    factor, row_table, update_rows, new_master, stored,
):
    core = at[4]
    sums = [
        [
            piece[MESSAGE, sender * BLK : sender * BLK + 8].astype(WIDE)
            + piece[MESSAGE, sender * BLK + 8 : sender * BLK + 16].astype(WIDE)
            for sender in range(8)
        ]
        for piece in (mine, peer)
    ]
    total = sum(sums[0][1:] + sums[1], sums[0][0])
    store_factors(total, rate[0], col_moment, new_col, factor)

    copies = []
    for line in range(7):
        for local in range(line * 4, line * 4 + 4):
            side, slot, first, kernel = (plan[local * 8 + item] for item in range(4))
            rows = slice(local * BLK, local * BLK + BLK)
            there = pl.ds(pl.multiple_of(first, BLK), BLK)
            value = jnp.where(
                side == 0, mine[slot, there, :].astype(WIDE), peer[slot, there, :].astype(WIDE)
            )
            update = value * factor[pl.ds(kernel, 1), :]
            update_rows[rows, :] = update
            new_master[rows, :] = master[rows, :] - learn_rate * update
        there = pl.ds(line * 4 * BLK, 4 * BLK)
        pairs = ((update_rows, update_far), (new_master, master_far))
        copies += fetch(
            [(source.at[there, :], target.at[there, :]) for source, target in pairs],
            stored.at[line],
        )

    change = own_part[...] + add_taps(views, peer, 1 - core)
    hidden = old[...] - (learn_rate * factor[0:1]) * change
    small = jnp.where(core == 1, mine[SLOTS - 1].astype(WIDE), peer[SLOTS - 1].astype(WIDE))
    weights = natural[27 * CI :].astype(WIDE) - small * (learn_rate * factor[1:2])
    next_output[...] = jnp.dot(
        jax.nn.silu(hidden).astype(LOW), weights.astype(LOW), preferred_element_type=WIDE
    ).astype(LOW)

    for side, messages in enumerate(sums):
        for sender in range(8):
            for line in range(4):
                to = (side * 8 + sender) * 4 + line
                row_table[to : to + 1] = messages[sender][
                    6 + line // 2 : 7 + line // 2, line % 2 * 128 : line % 2 * 128 + 128
                ]
    lane = lax.broadcasted_iota(jnp.int32, (1, 128), 1)
    for line in range(7):
        values = jnp.zeros((1, 128), WIDE)
        for part in range(4):
            from_row, turn = (plan[(line * 4 + part) * 8 + item] for item in (4, 5))
            here = (lane >= part * BLK) & (lane < part * BLK + BLK)
            turned = pltpu.roll(row_table[pl.ds(from_row, 1), :], turn, 1)
            values = jnp.where(here, turned, values)
        new_row[line : line + 1] = values
    for copy in copies:
        copy.wait()


def shards(
    step_count,
    block_order,
    saved_tiles,
    pre_act,
    grad_output,
    pointwise_live,
    master_rows,
    row_moment,
    col_moment,
    next_tiles,
):
    decay_rate = 1.0 - step_count.astype(WIDE) ** (-decay_power)

    tile_peer = swap(saved_tiles, MASK_CORE)
    pre_peer = swap(pre_act, MASK_CORE)
    grad_peer = swap(grad_output, MASK_CORE)
    rows_far = [far_away(array) for array in (pre_act, grad_output, pointwise_live)]
    brought, grad_near, pointwise_near = call(
        own_kernel,
        [((BROUGHT, CI), LOW), ((PIX, CO), LOW), ((CO, CO), LOW)],
        [VMEM] + [HBM] * 3,
        scratch=[pltpu.VMEM((PIX, CO), LOW), pltpu.SemaphoreType.DMA((3,))],
        moved=4 << 20,
    )(saved_tiles[0], *rows_far)

    keep, *sends = call(
        term_kernel,
        [((SLOTS, 128, CO), LOW)] + [((count, 128, CO), LOW) for _, count in PARTS],
        [VMEM] * 6,
        scratch=[pltpu.VMEM((BROUGHT, CI), LOW), pltpu.VMEM((2, 2 * PIX, CO), LOW)],
        flops=2 * 14 * 1024 * 256 * 256,
        moved=6 << 20,
        room=12,
    )(brought, tile_peer[0], pre_peer, grad_peer, grad_near, pointwise_near)

    packed = call(
        pack_kernel,
        [((SLOTS + 1, 16, CO), LOW)],
        [HBM] * 3,
        scratch=[
            pltpu.VMEM((SLOTS * 16, CO), WIDE),
            pltpu.VMEM((16, 128), WIDE),
            pltpu.SemaphoreType.DMA((2,)),
        ],
    )(keep, far_away(master_rows), far_away(row_moment.reshape(7, 128)))[0]
    packed_far = swap(packed, MASK_FAR)
    views = call(shift_kernel, [((3 * SHIFTED, CI), LOW)], [VMEM], moved=3 << 20)(next_tiles[0])[0]

    for step in range(1, 4):
        gots = [swap_part(send, part, step - 1) for part, send in enumerate(sends)]
        size = 256 >> (step + 1)
        outs = [((SLOTS, size, CO), LOW)] + [((count, size, CO), LOW) for _, count in PARTS]
        if step == 1:
            extra = [packed, packed_far]
            outs = outs + [((2, SLOTS + 1, 16, CO), LOW)]
        elif step == 2:
            extra = []
        else:
            extra = [pair, pair_near]
            outs = [((SLOTS, BLK, CO), LOW), ((4, SLOTS * 16, CO), LOW), ((4, 16, CO), LOW)]
        keep, *sends = call(
            functools.partial(fold_kernel, step),
            outs,
            [VMEM] * (len(extra) + 3),
            moved=1 << 20,
        )(*extra, keep, *gots)
        if step == 1:
            pair = sends.pop()
            pair_near = swap(pair, MASK_NEAR)
    line, moments = sends
    line_one, line_two = swap_mixed(line, (MASK_Y, MASK_X)), swap_mixed(line, (MASK_X, MASK_Y))
    own_moment, plan = call(
        moments_kernel,
        [((BLK, 128), WIDE), ((NB,), jnp.int32)],
        [SMEM] + [VMEM] * 2,
        out_specs=[VMEM, SMEM],
        pin=False,
        scratch=[
            pltpu.VMEM((64, 128), WIDE),
            pltpu.VMEM((128, 128), WIDE),
            pltpu.SMEM((NB,), jnp.int32),
        ],
    )(block_order, moments, swap(moments, MASK_CORE))
    *scaled, lines = call(
        moment_kernel,
        [((count, BLK, CO), LOW) for _, count in GATHERED] + [((3, 4, SLOTS * 16, CO), LOW)],
        [SMEM] + [VMEM] * 6,
        moved=2 << 20,
    )(decay_rate, keep, swap(keep, MASK_FAR), own_moment, line, line_one, line_two)
    line_far = swap_mixed(line_one, (MASK_X, MASK_Y))
    joined, natural = scaled, None
    for step in range(2, -1, -1):
        pieces = []
        for part, value in enumerate(joined):
            pieces += [value, swap_part(value, part, step)]
        size = 256 >> step
        outs = [((count, size, CO), LOW) for _, count in GATHERED]
        if step == 0:
            outs = [((SLOTS + 1, size, CO), LOW)]
        if step == 1:
            outs = outs + [((2, SLOTS * 16, CO), LOW)] * 2
        joined = call(
            functools.partial(widen_kernel, step),
            outs,
            [VMEM if step == 1 else HBM] + [VMEM] * len(pieces),
        )((natural, line_far, views)[step], *pieces)
        if step == 1:
            parts = [lines, *joined[2:]]
            joined = joined[:2]
            natural = call(
                order_kernel, [((NB * BLK, CO), LOW)], [SMEM] + [VMEM] * 6, moved=8 << 20
            )(block_order, *parts, *[swap(part, MASK_CORE) for part in parts])[0]
    mine = joined[0]
    peer = swap(mine, MASK_CORE)
    old = call(
        old_hidden_kernel,
        [((PIX, CO), WIDE)],
        [VMEM] * 2,
        flops=2 * 27 * 512 * 256 * 256,
        moved=6 << 20,
    )(views, natural)[0]
    half = call(
        half_hidden_kernel,
        [((PIX, CO), WIDE)],
        [VMEM] * 2,
        flops=2 * 14 * 512 * 256 * 256,
        moved=4 << 20,
    )(views, mine)[0]

    outs = [
        ((NB // 8 * BLK, CO), WIDE),
        ((NB // 8 * BLK, CO), WIDE),
        ((7, 128), WIDE),
        ((2, CO), WIDE),
        ((PIX, CO), LOW),
    ]
    update_rows, new_master, new_row, new_col, next_output = call(
        finish_kernel,
        outs,
        [SMEM] * 2 + [VMEM] * 8,
        out_specs=[HBM] * 2 + [VMEM] * 3,
        scratch=[
            pltpu.VMEM((2, CO), WIDE),
            pltpu.VMEM((64, 128), WIDE),
            pltpu.VMEM((NB // 8 * BLK, CO), WIDE),
            pltpu.VMEM((NB // 8 * BLK, CO), WIDE),
            pltpu.SemaphoreType.DMA((7, 2)),
        ],
        pin=False,
        flops=2 * 16 * 512 * 256 * 256,
        moved=16 << 20,
        room=16,
    )(plan, decay_rate, col_moment, views, natural, master_rows, mine, peer, old, half)
    return (update_rows, new_master, new_row.reshape(-1), new_col, next_output)


def solution(mesh):
    in_specs = (
        P(),
        P(),
        P(("group", "shard"), None, None, None, None),
        P(("group", "shard"), None),
        P(("group", "shard"), None),
        P(),
        P("shard", None),
        P("shard"),
        P(),
        P(("group", "shard"), None, None, None, None),
    )
    out_specs = (P("shard", None), P("shard", None), P("shard"), P(), P(("group", "shard"), None))
    body = shards if (mesh.shape["group"], mesh.shape["shard"]) == (4, 8) else general_shards
    return jax.shard_map(body, mesh=mesh, in_specs=in_specs, out_specs=out_specs, check_vma=False)
```

```python
import functools
import jax
import jax.numpy as jnp
from jax import lax
from jax.experimental import pallas as pl
from jax.experimental.pallas import tpu as pltpu
from jax.sharding import PartitionSpec as P

CI = 256
CO = 256
BLK = 32
FR = 2
HW = 16
NB3 = 216
NB = 224


learn_rate = 0.002
decay_power = 0.8


def silu_slope(values):
    sigma = jax.nn.sigmoid(values)
    return sigma * (1.0 + values * (1.0 - sigma))


def tap_views(frames):
    views = []
    for frame_off in range(3):
        for row_off in range(3):
            for col_off in range(3):
                window = frames[
                    frame_off : frame_off + FR, row_off : row_off + HW, col_off : col_off + HW, :
                ]
                views.append(window.reshape(FR * HW * HW, CI))
    return views


def contract_rows(left, right):
    return lax.dot_general(
        left, right, (((0,), (0,)), ((), ())), preferred_element_type=jnp.float32
    )


def kernel_sums(values, is_small):
    large_part = jnp.sum(jnp.where(is_small[:, None], 0.0, values), axis=0)
    small_part = jnp.sum(jnp.where(is_small[:, None], values, 0.0), axis=0)
    return jnp.stack([large_part, small_part])


def general_shards(
    step_count,
    block_order,
    saved_tiles,
    pre_act,
    grad_output,
    pointwise_live,
    master_rows,
    row_moment,
    col_moment,
    next_tiles,
):
    pre_float = pre_act.astype(jnp.float32)
    activation = jax.nn.silu(pre_float).astype(jnp.bfloat16)
    grad_act = lax.dot_general(
        grad_output, pointwise_live, (((1,), (1,)), ((), ())), preferred_element_type=jnp.float32
    )
    grad_pre = (grad_act * silu_slope(pre_float)).astype(jnp.bfloat16)
    pieces = [contract_rows(view, grad_pre) for view in tap_views(saved_tiles[0])]
    pieces.append(contract_rows(activation, grad_output))
    own_term = jnp.concatenate(pieces, axis=0).astype(jnp.bfloat16)
    total_rows = NB * BLK
    stored = jnp.take(own_term.reshape(NB, BLK, CO), block_order, axis=0).reshape(total_rows, CO)
    own_rows = master_rows.shape[0]
    partial_value = lax.psum_scatter(stored, "shard", scatter_dimension=0, tiled=True).astype(
        jnp.float32
    )
    gradient = lax.psum(partial_value, "group")
    owner = lax.axis_index("shard")
    own_count = own_rows // BLK
    own_blocks = lax.dynamic_slice_in_dim(block_order, owner * own_count, own_count)
    is_small = jnp.repeat(own_blocks >= NB3, BLK, total_repeat_length=own_rows)
    decay_rate = 1.0 - step_count.astype(jnp.float32)[0] ** (-decay_power)
    counts = jnp.array([27 * CI, CO], jnp.float32)
    squares = gradient * gradient
    new_row = decay_rate * row_moment + (1.0 - decay_rate) * jnp.mean(squares, axis=1)
    col_part = kernel_sums(squares, is_small)
    row_part = kernel_sums(new_row[:, None], is_small)[:, 0]
    weighted = kernel_sums(squares / new_row[:, None], is_small)
    col_total, weight_total, row_total = lax.psum((col_part, weighted, row_part), "shard")
    new_col = decay_rate * col_moment + (1.0 - decay_rate) * col_total / counts[:, None]
    row_mean = row_total / counts
    col_rows = jnp.where(is_small[:, None], new_col[1], new_col[0])
    mean_rows = jnp.where(is_small, row_mean[1], row_mean[0])
    scaled = gradient / jnp.sqrt(new_row[:, None] * col_rows / mean_rows[:, None])
    square_total = row_mean * jnp.sum(weight_total / new_col, axis=1)
    clip_factor = jnp.maximum(1.0, jnp.sqrt(square_total / (counts * CO)))
    update_rows = scaled / jnp.where(is_small, clip_factor[1], clip_factor[0])[:, None]
    new_master = master_rows - learn_rate * update_rows
    weights_low = new_master.astype(jnp.bfloat16)
    gathered = lax.all_gather(weights_low, "shard", axis=0, tiled=True)
    inverse = jnp.zeros((NB,), jnp.int32).at[block_order].set(jnp.arange(NB, dtype=jnp.int32))
    natural = jnp.take(gathered.reshape(NB, BLK, CO), inverse, axis=0).reshape(total_rows, CO)
    spatial = natural[: 27 * CI].reshape(27, CI, CO)
    pointwise = natural[27 * CI :]
    hidden_sum = jnp.zeros((FR * HW * HW, CO), jnp.float32)
    for index_tap, view in enumerate(tap_views(next_tiles[0])):
        hidden_sum = hidden_sum + jnp.dot(
            view, spatial[index_tap], preferred_element_type=jnp.float32
        )
    hidden_act = jax.nn.silu(hidden_sum).astype(jnp.bfloat16)
    next_output = jnp.dot(hidden_act, pointwise, preferred_element_type=jnp.float32).astype(
        jnp.bfloat16
    )
    return (update_rows, new_master, new_row, new_col, next_output)


AXES = ("group", "shard")
SLOTS = 14
PIX = FR * HW * HW
SHIFTED = (FR + 2) * (HW + 2) * HW
SLOPES = 3 * SHIFTED
ACTS = SLOPES + PIX
BROUGHT = ACTS + PIX
LOW = jnp.bfloat16
WIDE = jnp.float32
VMEM = pl.BlockSpec(memory_space=pltpu.VMEM)
SMEM = pl.BlockSpec(memory_space=pltpu.SMEM)
HBM = pl.BlockSpec(memory_space=pl.ANY)
MASK_CORE, MASK_NEAR, MASK_FAR, MASK_X, MASK_Y = 1, 2, 4, 8, 16
PARTS = ((0, 10), (10, 4))
ORDERS = (((0, 1, 2), (1, 0, 2)), ((2, 0, 1), (2, 1, 0)))
MESSAGE = SLOTS
GATHERED = ((0, 10), (10, 5))
MASKS = (MASK_X, MASK_Y, MASK_NEAR)


def swap(value, mask):
    return lax.ppermute(value, AXES, [(at, at ^ mask) for at in range(32)])


def swap_mixed(value, masks):
    return lax.ppermute(value, AXES, [(at, at ^ masks[at & 1]) for at in range(32)])


def swap_part(value, part, step):
    return swap_mixed(value, [MASKS[ORDERS[part][core][step]] for core in range(2)])


def place_of(at, part, step):
    zero, one = (ORDERS[part][core][step] for core in range(2))
    return at[zero] if zero == one else jnp.where(at[4] == 0, at[zero], at[one])


def position():
    group, shard = lax.axis_index("group"), lax.axis_index("shard")
    return group % 2, group // 2, shard // 2 % 2, shard // 4, shard % 2


def call(kernel, outs, in_specs, out_specs=None, scratch=(), flops=0, moved=0, room=8, pin=True):
    return pl.pallas_call(
        lambda *refs: kernel(position(), *refs),
        out_shape=[(pltpu.VMEM if pin else jax.ShapeDtypeStruct)(*out) for out in outs],
        in_specs=in_specs,
        out_specs=out_specs or [VMEM] * len(outs),
        scratch_shapes=list(scratch),
        compiler_params=pltpu.CompilerParams(vmem_limit_bytes=room << 20),
        cost_estimate=pl.CostEstimate(flops=flops, bytes_accessed=moved, transcendentals=0),
    )


def far_away(array):
    return pltpu.with_memory_space_constraint(array, pltpu.HBM)


def store_shifted(tile, out):
    for col_off in range(3):
        out[col_off * SHIFTED : (col_off + 1) * SHIFTED] = tile[
            :, :, col_off : col_off + HW, :
        ].reshape(SHIFTED, CI)


def shift_kernel(at, tile, out):
    store_shifted(tile, out)


def store_factors_of(pre, grad, pointwise, out):
    values = pre[...].astype(WIDE)
    sigma = jax.nn.sigmoid(values)
    grad_act = lax.dot_general(
        grad[...], pointwise[...], (((1,), (1,)), ((), ())), preferred_element_type=WIDE
    )
    out[SLOPES:ACTS] = (grad_act * (sigma * (1.0 + values * (1.0 - sigma)))).astype(LOW)
    out[ACTS:] = (values * sigma).astype(LOW)


def view_start(tap, frame):
    frame_off, row_off, col_off = tap // 9, tap // 3 % 3, tap % 3
    return col_off * SHIFTED + ((frame + frame_off) * (HW + 2) + row_off) * HW


def core_start(core, slot, frame):
    return pl.multiple_of(
        jnp.where(core == 0, view_start(slot, frame), view_start(min(SLOTS + slot, 26), frame)), HW
    )


def fetch(pairs, arrived):
    copies = [
        pltpu.make_async_copy(source, target, arrived.at[index])
        for index, (source, target) in enumerate(pairs)
    ]
    for copy in copies:
        copy.start()
    return copies


def own_kernel(
    at, tile, pre_far, grad_far, pointwise_far, brought, grad, pointwise, pre, arrived
):
    copies = fetch(((pre_far, pre), (grad_far, grad), (pointwise_far, pointwise)), arrived)
    store_shifted(tile, brought)
    for copy in copies:
        copy.wait()
    store_factors_of(pre, grad, pointwise, brought)


def pack_kernel(at, after, master_far, row_moment_far, packed, master, row_moment, arrived):
    quarter = pl.multiple_of((at[1] * 2 + at[0]) * (SLOTS * 16), SLOTS * 16)
    row_moment[...] = jnp.zeros((16, 128), WIDE)
    copies = fetch(
        (
            (master_far.at[pl.ds(quarter, SLOTS * 16), :], master),
            (row_moment_far, row_moment.at[pl.ds(0, 7), :]),
        ),
        arrived,
    )
    for copy in copies:
        copy.wait()
    packed[:SLOTS] = master[...].astype(LOW).reshape(SLOTS, 16, CO)
    high = row_moment[...].astype(LOW).astype(WIDE)
    packed[SLOTS] = jnp.concatenate([high, row_moment[...] - high], axis=1).astype(LOW)


def term_kernel(
    at, own, tile_peer, pre_peer, grad_peer, grad, pointwise, keep, send_one, send_two, peer, rights
):
    core = at[4]
    store_shifted(tile_peer, peer)
    store_factors_of(pre_peer, grad_peer, pointwise, peer)
    rights[0, :PIX] = own[SLOPES:ACTS]
    rights[0, PIX:] = peer[SLOPES:ACTS]
    rights[1, :PIX] = grad[...]
    rights[1, PIX:] = grad_peer[...]
    for slot in range(SLOTS):
        pieces = []
        for ref in (own, peer):
            for frame in range(FR):
                start = core_start(core, slot, frame)
                if slot == SLOTS - 1:
                    start = jnp.where(core == 0, start, ACTS + frame * HW * HW)
                pieces.append(ref[pl.ds(pl.multiple_of(start, HW), HW * HW), :])
        right = rights[core] if slot == SLOTS - 1 else rights[0]
        total = contract_rows(jnp.concatenate(pieces, axis=0), right)
        for part, ((first, count), send) in enumerate(zip(PARTS, (send_one, send_two))):
            if first <= slot < first + count:
                low, high, at_low = total[:128], total[128:], place_of(at, part, 0) == 0
                keep[slot] = jnp.where(at_low, low, high).astype(LOW)
                send[slot - first] = jnp.where(at_low, high, low).astype(LOW)


def fold_kernel(step, at, *refs):
    size = 256 >> (step + 1)
    extra = 0 if step == 2 else 2
    own, got = refs[:extra] or (None, None)
    refs = refs[extra:]
    keep, gots, stay, sends = refs[0], refs[1:3], refs[3], refs[4:]
    for part, (first, count) in enumerate(PARTS):
        here = slice(first, first + count)
        if step == 3:
            stay[here] = keep[here] + gots[part][...]
            continue
        mine = place_of(at, part, step)
        for which, out in ((mine, 0), (1 - mine, 1)):
            rows = pl.ds(pl.multiple_of(which * size, size), size)
            value = keep[here, rows] + gots[part][:, rows]
            if out == 0:
                stay[here] = value
            else:
                sends[part][...] = value
    if step == 1:
        pair = sends[2]
        pair[at[3]] = own[...]
        pair[1 - at[3]] = got[...]
    if step == 3:
        line, moments = sends
        for which, piece in ((at[2], own), (1 - at[2], got)):
            for far in range(2):
                line[far * 2 + which] = piece[far, :SLOTS].reshape(SLOTS * 16, CO)
                moments[far * 2 + which] = piece[far, SLOTS]


def moment_kernel(
    at, rate, own, got, moments, line, line_one, line_two, scaled_one, scaled_two, lines,
):
    for index, piece in enumerate((line, line_one, line_two)):
        lines[index] = piece[...]
    count = SLOTS * BLK
    total = (own[...].astype(WIDE) + got[...].astype(WIDE)).reshape(count, CO)
    squares = total * total
    decay = rate[0]
    mean = jnp.sum(squares, axis=1, keepdims=True) * (1.0 / CO)
    row_moment = jnp.concatenate([moments[:, slot : slot + 1] for slot in range(SLOTS)], axis=0)
    new_row = decay * row_moment + (1.0 - decay) * mean
    value = (total * lax.rsqrt(new_row)).astype(LOW).reshape(SLOTS, BLK, CO)
    split = PARTS[0][1]
    scaled_one[...] = value[:split]
    scaled_two[: SLOTS - split] = value[split:]
    weighted = squares / new_row
    cut = count - BLK
    last_small = at[4] == 1
    rows = []
    for values in (squares, weighted, jnp.broadcast_to(new_row, (count, CO))):
        large = jnp.sum(values[:cut], axis=0, keepdims=True)
        last = jnp.sum(values[cut:], axis=0, keepdims=True)
        rows.append(large + jnp.where(last_small, 0.0, last))
        rows.append(jnp.where(last_small, last, 0.0))
    spread = jnp.broadcast_to(new_row, (count, 128))
    spread = jnp.concatenate([spread, jnp.zeros((512 - count, 128), WIDE)], axis=0)
    rows += [jnp.transpose(spread[:CO])[:1], jnp.transpose(spread[CO:])[:1]]
    message = jnp.concatenate(rows, axis=0)
    high = message.astype(LOW).astype(WIDE)
    message = jnp.concatenate([high, message - high, jnp.zeros((16, CO), WIDE)], axis=0)
    scaled_two[SLOTS - split] = message.astype(LOW)


def store_factors(total, decay, col_moment, new_col, factor):
    for kernel in range(2):
        count = 27.0 * CI if kernel == 0 else float(CO)
        col = decay * col_moment[kernel : kernel + 1] + (1.0 - decay) * (
            total[kernel : kernel + 1] / count
        )
        row_mean = total[4 + kernel : 5 + kernel] / count
        square = row_mean * jnp.sum(
            total[2 + kernel : 3 + kernel] / col, axis=1, keepdims=True
        )
        clip = jnp.maximum(1.0, jnp.sqrt(square / (count * CO)))
        new_col[kernel : kernel + 1] = col
        factor[kernel : kernel + 1] = 1.0 / (jnp.sqrt(col / row_mean) * clip)


def moments_kernel(at, block_order, mine, peer, out, plan, table, rows, inverse):
    core = at[4]
    owner = at[3] * 4 + at[2] * 2 + core

    def place_block(local, carry):
        block = block_order[owner * (NB // 8) + local]
        half = (block >= 8 * SLOTS).astype(jnp.int32)
        slot, place = (block - half * (8 * SLOTS)) // 8, lax.rem(block, 8)
        high, middle, low = place // 4, lax.rem(place // 2, 2), lax.rem(place, 2)
        other = low * 4 + high * 2 + middle
        sender = jnp.where(slot < PARTS[1][0], other, place)
        side = half ^ core
        plan[local * 8] = side
        plan[local * 8 + 1] = slot
        plan[local * 8 + 2] = place * BLK
        plan[local * 8 + 3] = (block >= NB3).astype(jnp.int32)
        plan[local * 8 + 4] = (side * 8 + sender) * 4 + slot // 4
        plan[local * 8 + 5] = lax.rem(128 + (lax.rem(local, 4) - lax.rem(slot, 4)) * BLK, 128)
        return carry

    lax.fori_loop(0, NB // 8, place_block, 0, unroll=4)
    for side, ref in enumerate((mine, peer)):
        for line in range(4):
            values = ref[line].astype(WIDE)
            values = values[:, :128] + values[:, 128:]
            table[pl.ds(pl.multiple_of((line * 2 + (core ^ side)) * 8, 8), 8), :] = values[:8]

    def invert(stored, carry):
        inverse[block_order[stored]] = stored
        return carry

    lax.fori_loop(0, NB, invert, 0, unroll=8)
    rows[...] = jnp.zeros((128, 128), WIDE)
    for part, (first, count) in enumerate(PARTS):
        place = place_of(at, part, 0) * 4 + place_of(at, part, 1) * 2 + place_of(at, part, 2)
        for slot in range(first, first + count):
            stored = inverse[(core * SLOTS + slot) * 8 + place]
            owner, local = stored // (NB // 8), lax.rem(stored, NB // 8)
            row = table[pl.ds(owner * 8 + local // 4, 1), :]
            turn = lax.rem(128 - lax.rem(local, 4) * BLK, 128)
            rows[slot : slot + 1] = pltpu.roll(row, turn, 1)
    out[...] = jnp.transpose(rows[...])[:BLK]


def order_kernel(at, block_order, mine, mine_low, mine_high, peer, peer_low, peer_high, out):
    count = NB // 8
    quarters = count // 4
    for flip_core, (pieces, low, high) in enumerate(
        ((mine, mine_low, mine_high), (peer, peer_low, peer_high))
    ):
        core = at[4] ^ flip_core
        for index in range(4):
            flip_x = jnp.where(core == 0, index // 2, index % 2)
            quarter = (at[1] ^ (index // 2) ^ (index % 2) ^ flip_x) * 2 + (at[0] ^ flip_x)
            for local in range(quarters):
                for line in range(4):
                    block = block_order[(line * 2 + core) * count + quarter * quarters + local]
                    to = pl.ds(pl.multiple_of(block * BLK, BLK), BLK)
                    rows = slice(local * BLK, local * BLK + BLK)
                    if index < 3:
                        out[to, :] = pieces[index, line, rows]
                    else:
                        out[to, :] = (low, high)[line // 2][line % 2, rows]


def widen_kernel(step, at, after, *refs):
    size = 256 >> (step + 1)
    ins, outs = refs[:4], refs[4:]
    if step == 1:
        outs[2][...], outs[3][...] = after[:2], after[2:]
    for part, (first, count) in enumerate(GATHERED):
        mine = place_of(at, part, step)
        for index, which in enumerate((mine, 1 - mine)):
            rows = pl.ds(pl.multiple_of(which * size, size), size)
            value = ins[2 * part + index][...]
            if step == 0:
                outs[0][first : first + count, rows] = value
            else:
                outs[part][:, rows] = value


def window(views, starts):
    return jnp.concatenate([views[pl.ds(start, HW * HW), :] for start in starts], axis=0)


def old_hidden_kernel(at, views, natural, hidden):
    total = jnp.zeros((PIX, CO), WIDE)
    for tap in range(27):
        weights = natural[tap * CI : tap * CI + CI]
        starts = [view_start(tap, frame) for frame in range(FR)]
        total = total + jnp.dot(window(views, starts), weights, preferred_element_type=WIDE)
    hidden[...] = total


def add_taps(views, scaled, core):
    total = jnp.zeros((PIX, CO), WIDE)
    for slot in range(SLOTS):
        starts = [core_start(core, slot, frame) for frame in range(FR)]
        weights = scaled[slot]
        if slot == SLOTS - 1:
            weights = jnp.where(core == 0, weights.astype(WIDE), 0.0).astype(LOW)
        total = total + jnp.dot(window(views, starts), weights, preferred_element_type=WIDE)
    return total


def half_hidden_kernel(at, views, scaled, hidden):
    hidden[...] = add_taps(views, scaled, at[4])


def finish_kernel(
    at, plan, rate, col_moment, views, natural, master, mine, peer, old, own_part,
    update_far, master_far, row_far, col_far, output_far,
    factor, row_table, update_rows, new_master, new_row, new_col, next_output, stored, rest_stored,
):
    core = at[4]
    sums = [
        [
            piece[MESSAGE, sender * BLK : sender * BLK + 8].astype(WIDE)
            + piece[MESSAGE, sender * BLK + 8 : sender * BLK + 16].astype(WIDE)
            for sender in range(8)
        ]
        for piece in (mine, peer)
    ]
    total = sum(sums[0][1:] + sums[1], sums[0][0])
    store_factors(total, rate[0], col_moment, new_col, factor)

    def store(source, target, index):
        copy = pltpu.make_async_copy(source, target, rest_stored.at[index])
        copy.start()
        return [copy]

    copies = store(new_col, col_far, 0)

    for line in range(7):
        for local in range(line * 4, line * 4 + 4):
            side, slot, first, kernel = (plan[local * 8 + item] for item in range(4))
            rows = slice(local * BLK, local * BLK + BLK)
            there = pl.ds(pl.multiple_of(first, BLK), BLK)
            value = jnp.where(
                side == 0, mine[slot, there, :].astype(WIDE), peer[slot, there, :].astype(WIDE)
            )
            update = value * factor[pl.ds(kernel, 1), :]
            update_rows[rows, :] = update
            new_master[rows, :] = master[rows, :] - learn_rate * update
        there = pl.ds(line * 4 * BLK, 4 * BLK)
        pairs = ((update_rows, update_far), (new_master, master_far))
        copies += fetch(
            [(source.at[there, :], target.at[there, :]) for source, target in pairs],
            stored.at[line],
        )

    change = own_part[...] + add_taps(views, peer, 1 - core)
    hidden = old[...] - (learn_rate * factor[0:1]) * change
    small = jnp.where(core == 1, mine[SLOTS - 1].astype(WIDE), peer[SLOTS - 1].astype(WIDE))
    weights = natural[27 * CI :].astype(WIDE) - small * (learn_rate * factor[1:2])
    next_output[...] = jnp.dot(
        jax.nn.silu(hidden).astype(LOW), weights.astype(LOW), preferred_element_type=WIDE
    ).astype(LOW)
    copies += store(next_output, output_far, 1)

    for side, messages in enumerate(sums):
        for sender in range(8):
            for line in range(4):
                to = (side * 8 + sender) * 4 + line
                row_table[to : to + 1] = messages[sender][
                    6 + line // 2 : 7 + line // 2, line % 2 * 128 : line % 2 * 128 + 128
                ]
    lane = lax.broadcasted_iota(jnp.int32, (1, 128), 1)
    for line in range(7):
        values = jnp.zeros((1, 128), WIDE)
        for part in range(4):
            from_row, turn = (plan[(line * 4 + part) * 8 + item] for item in (4, 5))
            here = (lane >= part * BLK) & (lane < part * BLK + BLK)
            turned = pltpu.roll(row_table[pl.ds(from_row, 1), :], turn, 1)
            values = jnp.where(here, turned, values)
        new_row[line : line + 1] = values
    copies += store(new_row, row_far, 2)
    for copy in copies:
        copy.wait()


def shards(
    step_count,
    block_order,
    saved_tiles,
    pre_act,
    grad_output,
    pointwise_live,
    master_rows,
    row_moment,
    col_moment,
    next_tiles,
):
    decay_rate = 1.0 - step_count.astype(WIDE) ** (-decay_power)

    tile_peer = swap(saved_tiles, MASK_CORE)
    pre_peer = swap(pre_act, MASK_CORE)
    grad_peer = swap(grad_output, MASK_CORE)
    rows_far = [far_away(array) for array in (pre_act, grad_output, pointwise_live)]
    brought, grad_near, pointwise_near = call(
        own_kernel,
        [((BROUGHT, CI), LOW), ((PIX, CO), LOW), ((CO, CO), LOW)],
        [VMEM] + [HBM] * 3,
        scratch=[pltpu.VMEM((PIX, CO), LOW), pltpu.SemaphoreType.DMA((3,))],
        moved=4 << 20,
    )(saved_tiles[0], *rows_far)

    keep, *sends = call(
        term_kernel,
        [((SLOTS, 128, CO), LOW)] + [((count, 128, CO), LOW) for _, count in PARTS],
        [VMEM] * 6,
        scratch=[pltpu.VMEM((BROUGHT, CI), LOW), pltpu.VMEM((2, 2 * PIX, CO), LOW)],
        flops=2 * 14 * 1024 * 256 * 256,
        moved=6 << 20,
        room=12,
    )(brought, tile_peer[0], pre_peer, grad_peer, grad_near, pointwise_near)

    packed = call(
        pack_kernel,
        [((SLOTS + 1, 16, CO), LOW)],
        [HBM] * 3,
        scratch=[
            pltpu.VMEM((SLOTS * 16, CO), WIDE),
            pltpu.VMEM((16, 128), WIDE),
            pltpu.SemaphoreType.DMA((2,)),
        ],
    )(keep, far_away(master_rows), far_away(row_moment.reshape(7, 128)))[0]
    packed_far = swap(packed, MASK_FAR)
    views = call(shift_kernel, [((3 * SHIFTED, CI), LOW)], [VMEM], moved=3 << 20)(next_tiles[0])[0]

    for step in range(1, 4):
        gots = [swap_part(send, part, step - 1) for part, send in enumerate(sends)]
        size = 256 >> (step + 1)
        outs = [((SLOTS, size, CO), LOW)] + [((count, size, CO), LOW) for _, count in PARTS]
        if step == 1:
            extra = [packed, packed_far]
            outs = outs + [((2, SLOTS + 1, 16, CO), LOW)]
        elif step == 2:
            extra = []
        else:
            extra = [pair, pair_near]
            outs = [((SLOTS, BLK, CO), LOW), ((4, SLOTS * 16, CO), LOW), ((4, 16, CO), LOW)]
        keep, *sends = call(
            functools.partial(fold_kernel, step),
            outs,
            [VMEM] * (len(extra) + 3),
            moved=1 << 20,
        )(*extra, keep, *gots)
        if step == 1:
            pair = sends.pop()
            pair_near = swap(pair, MASK_NEAR)
    line, moments = sends
    line_one, line_two = swap_mixed(line, (MASK_Y, MASK_X)), swap_mixed(line, (MASK_X, MASK_Y))
    own_moment, plan = call(
        moments_kernel,
        [((BLK, 128), WIDE), ((NB,), jnp.int32)],
        [SMEM] + [VMEM] * 2,
        out_specs=[VMEM, SMEM],
        pin=False,
        scratch=[
            pltpu.VMEM((64, 128), WIDE),
            pltpu.VMEM((128, 128), WIDE),
            pltpu.SMEM((NB,), jnp.int32),
        ],
    )(block_order, moments, swap(moments, MASK_CORE))
    *scaled, lines = call(
        moment_kernel,
        [((count, BLK, CO), LOW) for _, count in GATHERED] + [((3, 4, SLOTS * 16, CO), LOW)],
        [SMEM] + [VMEM] * 6,
        moved=2 << 20,
    )(decay_rate, keep, swap(keep, MASK_FAR), own_moment, line, line_one, line_two)
    line_far = swap_mixed(line_one, (MASK_X, MASK_Y))
    joined, natural = scaled, None
    for step in range(2, -1, -1):
        pieces = []
        for part, value in enumerate(joined):
            pieces += [value, swap_part(value, part, step)]
        size = 256 >> step
        outs = [((count, size, CO), LOW) for _, count in GATHERED]
        if step == 0:
            outs = [((SLOTS + 1, size, CO), LOW)]
        if step == 1:
            outs = outs + [((2, SLOTS * 16, CO), LOW)] * 2
        joined = call(
            functools.partial(widen_kernel, step),
            outs,
            [VMEM if step == 1 else HBM] + [VMEM] * len(pieces),
        )((natural, line_far, views)[step], *pieces)
        if step == 1:
            parts = [lines, *joined[2:]]
            joined = joined[:2]
            natural = call(
                order_kernel, [((NB * BLK, CO), LOW)], [SMEM] + [VMEM] * 6, moved=8 << 20
            )(block_order, *parts, *[swap(part, MASK_CORE) for part in parts])[0]
    mine = joined[0]
    peer = swap(mine, MASK_CORE)
    old = call(
        old_hidden_kernel,
        [((PIX, CO), WIDE)],
        [VMEM] * 2,
        flops=2 * 27 * 512 * 256 * 256,
        moved=6 << 20,
    )(views, natural)[0]
    half = call(
        half_hidden_kernel,
        [((PIX, CO), WIDE)],
        [VMEM] * 2,
        flops=2 * 14 * 512 * 256 * 256,
        moved=4 << 20,
    )(views, mine)[0]

    outs = [
        ((NB // 8 * BLK, CO), WIDE),
        ((NB // 8 * BLK, CO), WIDE),
        ((7, 128), WIDE),
        ((2, CO), WIDE),
        ((PIX, CO), LOW),
    ]
    update_rows, new_master, new_row, new_col, next_output = call(
        finish_kernel,
        outs,
        [SMEM] * 2 + [VMEM] * 8,
        out_specs=[HBM] * 5,
        scratch=[
            pltpu.VMEM((2, CO), WIDE),
            pltpu.VMEM((64, 128), WIDE),
            pltpu.VMEM((NB // 8 * BLK, CO), WIDE),
            pltpu.VMEM((NB // 8 * BLK, CO), WIDE),
            pltpu.VMEM((7, 128), WIDE),
            pltpu.VMEM((2, CO), WIDE),
            pltpu.VMEM((PIX, CO), LOW),
            pltpu.SemaphoreType.DMA((7, 2)),
            pltpu.SemaphoreType.DMA((3,)),
        ],
        pin=False,
        flops=2 * 16 * 512 * 256 * 256,
        moved=16 << 20,
        room=16,
    )(plan, decay_rate, col_moment, views, natural, master_rows, mine, peer, old, half)
    return (update_rows, new_master, new_row.reshape(-1), new_col, next_output)


def solution(mesh):
    in_specs = (
        P(),
        P(),
        P(("group", "shard"), None, None, None, None),
        P(("group", "shard"), None),
        P(("group", "shard"), None),
        P(),
        P("shard", None),
        P("shard"),
        P(),
        P(("group", "shard"), None, None, None, None),
    )
    out_specs = (P("shard", None), P("shard", None), P("shard"), P(), P(("group", "shard"), None))
    body = shards if (mesh.shape["group"], mesh.shape["shard"]) == (4, 8) else general_shards
    return jax.shard_map(body, mesh=mesh, in_specs=in_specs, out_specs=out_specs, check_vma=False)
```

```python
import functools
import jax
import jax.numpy as jnp
from jax import lax
from jax.experimental import pallas as pl
from jax.experimental.pallas import tpu as pltpu
from jax.sharding import PartitionSpec as P

CI = 256
CO = 256
BLK = 32
FR = 2
HW = 16
NB3 = 216
NB = 224


learn_rate = 0.002
decay_power = 0.8


def silu_slope(values):
    sigma = jax.nn.sigmoid(values)
    return sigma * (1.0 + values * (1.0 - sigma))


def tap_views(frames):
    views = []
    for frame_off in range(3):
        for row_off in range(3):
            for col_off in range(3):
                window = frames[
                    frame_off : frame_off + FR, row_off : row_off + HW, col_off : col_off + HW, :
                ]
                views.append(window.reshape(FR * HW * HW, CI))
    return views


def contract_rows(left, right):
    return lax.dot_general(
        left, right, (((0,), (0,)), ((), ())), preferred_element_type=jnp.float32
    )


def kernel_sums(values, is_small):
    large_part = jnp.sum(jnp.where(is_small[:, None], 0.0, values), axis=0)
    small_part = jnp.sum(jnp.where(is_small[:, None], values, 0.0), axis=0)
    return jnp.stack([large_part, small_part])


def general_shards(
    step_count,
    block_order,
    saved_tiles,
    pre_act,
    grad_output,
    pointwise_live,
    master_rows,
    row_moment,
    col_moment,
    next_tiles,
):
    pre_float = pre_act.astype(jnp.float32)
    activation = jax.nn.silu(pre_float).astype(jnp.bfloat16)
    grad_act = lax.dot_general(
        grad_output, pointwise_live, (((1,), (1,)), ((), ())), preferred_element_type=jnp.float32
    )
    grad_pre = (grad_act * silu_slope(pre_float)).astype(jnp.bfloat16)
    pieces = [contract_rows(view, grad_pre) for view in tap_views(saved_tiles[0])]
    pieces.append(contract_rows(activation, grad_output))
    own_term = jnp.concatenate(pieces, axis=0).astype(jnp.bfloat16)
    total_rows = NB * BLK
    stored = jnp.take(own_term.reshape(NB, BLK, CO), block_order, axis=0).reshape(total_rows, CO)
    own_rows = master_rows.shape[0]
    partial_value = lax.psum_scatter(stored, "shard", scatter_dimension=0, tiled=True).astype(
        jnp.float32
    )
    gradient = lax.psum(partial_value, "group")
    owner = lax.axis_index("shard")
    own_count = own_rows // BLK
    own_blocks = lax.dynamic_slice_in_dim(block_order, owner * own_count, own_count)
    is_small = jnp.repeat(own_blocks >= NB3, BLK, total_repeat_length=own_rows)
    decay_rate = 1.0 - step_count.astype(jnp.float32)[0] ** (-decay_power)
    counts = jnp.array([27 * CI, CO], jnp.float32)
    squares = gradient * gradient
    new_row = decay_rate * row_moment + (1.0 - decay_rate) * jnp.mean(squares, axis=1)
    col_part = kernel_sums(squares, is_small)
    row_part = kernel_sums(new_row[:, None], is_small)[:, 0]
    weighted = kernel_sums(squares / new_row[:, None], is_small)
    col_total, weight_total, row_total = lax.psum((col_part, weighted, row_part), "shard")
    new_col = decay_rate * col_moment + (1.0 - decay_rate) * col_total / counts[:, None]
    row_mean = row_total / counts
    col_rows = jnp.where(is_small[:, None], new_col[1], new_col[0])
    mean_rows = jnp.where(is_small, row_mean[1], row_mean[0])
    scaled = gradient / jnp.sqrt(new_row[:, None] * col_rows / mean_rows[:, None])
    square_total = row_mean * jnp.sum(weight_total / new_col, axis=1)
    clip_factor = jnp.maximum(1.0, jnp.sqrt(square_total / (counts * CO)))
    update_rows = scaled / jnp.where(is_small, clip_factor[1], clip_factor[0])[:, None]
    new_master = master_rows - learn_rate * update_rows
    weights_low = new_master.astype(jnp.bfloat16)
    gathered = lax.all_gather(weights_low, "shard", axis=0, tiled=True)
    inverse = jnp.zeros((NB,), jnp.int32).at[block_order].set(jnp.arange(NB, dtype=jnp.int32))
    natural = jnp.take(gathered.reshape(NB, BLK, CO), inverse, axis=0).reshape(total_rows, CO)
    spatial = natural[: 27 * CI].reshape(27, CI, CO)
    pointwise = natural[27 * CI :]
    hidden_sum = jnp.zeros((FR * HW * HW, CO), jnp.float32)
    for index_tap, view in enumerate(tap_views(next_tiles[0])):
        hidden_sum = hidden_sum + jnp.dot(
            view, spatial[index_tap], preferred_element_type=jnp.float32
        )
    hidden_act = jax.nn.silu(hidden_sum).astype(jnp.bfloat16)
    next_output = jnp.dot(hidden_act, pointwise, preferred_element_type=jnp.float32).astype(
        jnp.bfloat16
    )
    return (update_rows, new_master, new_row, new_col, next_output)


AXES = ("group", "shard")
SLOTS = 14
PIX = FR * HW * HW
SHIFTED = (FR + 2) * (HW + 2) * HW
SLOPES = 3 * SHIFTED
ACTS = SLOPES + PIX
BROUGHT = ACTS + PIX
LOW = jnp.bfloat16
WIDE = jnp.float32
VMEM = pl.BlockSpec(memory_space=pltpu.VMEM)
SMEM = pl.BlockSpec(memory_space=pltpu.SMEM)
HBM = pl.BlockSpec(memory_space=pl.ANY)
MASK_CORE, MASK_NEAR, MASK_FAR, MASK_X, MASK_Y = 1, 2, 4, 8, 16
PARTS = ((0, 10), (10, 4))
ORDERS = (((0, 1, 2), (1, 0, 2)), ((2, 0, 1), (2, 1, 0)))
MESSAGE = SLOTS
GATHERED = ((0, 10), (10, 5))
MASKS = (MASK_X, MASK_Y, MASK_NEAR)


def swap(value, mask):
    return lax.ppermute(value, AXES, [(at, at ^ mask) for at in range(32)])


def swap_mixed(value, masks):
    return lax.ppermute(value, AXES, [(at, at ^ masks[at & 1]) for at in range(32)])


def swap_part(value, part, step):
    return swap_mixed(value, [MASKS[ORDERS[part][core][step]] for core in range(2)])


def place_of(at, part, step):
    zero, one = (ORDERS[part][core][step] for core in range(2))
    return at[zero] if zero == one else jnp.where(at[4] == 0, at[zero], at[one])


def position():
    group, shard = lax.axis_index("group"), lax.axis_index("shard")
    return group % 2, group // 2, shard // 2 % 2, shard // 4, shard % 2


def call(kernel, outs, in_specs, out_specs=None, scratch=(), flops=0, moved=0, room=8, pin=True):
    return pl.pallas_call(
        lambda *refs: kernel(position(), *refs),
        out_shape=[(pltpu.VMEM if pin else jax.ShapeDtypeStruct)(*out) for out in outs],
        in_specs=in_specs,
        out_specs=out_specs or [VMEM] * len(outs),
        scratch_shapes=list(scratch),
        compiler_params=pltpu.CompilerParams(vmem_limit_bytes=room << 20),
        cost_estimate=pl.CostEstimate(flops=flops, bytes_accessed=moved, transcendentals=0),
    )


def far_away(array):
    return pltpu.with_memory_space_constraint(array, pltpu.HBM)


def store_shifted(tile, out):
    for col_off in range(3):
        out[col_off * SHIFTED : (col_off + 1) * SHIFTED] = tile[
            :, :, col_off : col_off + HW, :
        ].reshape(SHIFTED, CI)


def shift_kernel(at, tile, out):
    store_shifted(tile, out)


def store_factors_of(pre, grad, pointwise, out):
    values = pre[...].astype(WIDE)
    sigma = jax.nn.sigmoid(values)
    grad_act = lax.dot_general(
        grad[...], pointwise[...], (((1,), (1,)), ((), ())), preferred_element_type=WIDE
    )
    out[SLOPES:ACTS] = (grad_act * (sigma * (1.0 + values * (1.0 - sigma)))).astype(LOW)
    out[ACTS:] = (values * sigma).astype(LOW)


def view_start(tap, frame):
    frame_off, row_off, col_off = tap // 9, tap // 3 % 3, tap % 3
    return col_off * SHIFTED + ((frame + frame_off) * (HW + 2) + row_off) * HW


def core_start(core, slot, frame):
    return pl.multiple_of(
        jnp.where(core == 0, view_start(slot, frame), view_start(min(SLOTS + slot, 26), frame)), HW
    )


def fetch(pairs, arrived):
    copies = [
        pltpu.make_async_copy(source, target, arrived.at[index])
        for index, (source, target) in enumerate(pairs)
    ]
    for copy in copies:
        copy.start()
    return copies


def own_kernel(
    at, tile, pre_far, grad_far, pointwise_far, brought, grad, pointwise, pre, arrived
):
    copies = fetch(((pre_far, pre), (grad_far, grad), (pointwise_far, pointwise)), arrived)
    store_shifted(tile, brought)
    for copy in copies:
        copy.wait()
    store_factors_of(pre, grad, pointwise, brought)


def pack_kernel(at, after, master_far, row_moment_far, packed, master, row_moment, arrived):
    quarter = pl.multiple_of((at[1] * 2 + at[0]) * (SLOTS * 16), SLOTS * 16)
    row_moment[...] = jnp.zeros((16, 128), WIDE)
    copies = fetch(
        (
            (master_far.at[pl.ds(quarter, SLOTS * 16), :], master),
            (row_moment_far, row_moment.at[pl.ds(0, 7), :]),
        ),
        arrived,
    )
    for copy in copies:
        copy.wait()
    packed[:SLOTS] = master[...].astype(LOW).reshape(SLOTS, 16, CO)
    high = row_moment[...].astype(LOW).astype(WIDE)
    packed[SLOTS] = jnp.concatenate([high, row_moment[...] - high], axis=1).astype(LOW)


def term_kernel(
    at, own, tile_peer, pre_peer, grad_peer, grad, pointwise, keep, send_one, send_two, peer, rights
):
    core = at[4]
    store_shifted(tile_peer, peer)
    store_factors_of(pre_peer, grad_peer, pointwise, peer)
    rights[0, :PIX] = own[SLOPES:ACTS]
    rights[0, PIX:] = peer[SLOPES:ACTS]
    rights[1, :PIX] = grad[...]
    rights[1, PIX:] = grad_peer[...]
    for slot in range(SLOTS):
        pieces = []
        for ref in (own, peer):
            for frame in range(FR):
                start = core_start(core, slot, frame)
                if slot == SLOTS - 1:
                    start = jnp.where(core == 0, start, ACTS + frame * HW * HW)
                pieces.append(ref[pl.ds(pl.multiple_of(start, HW), HW * HW), :])
        right = rights[core] if slot == SLOTS - 1 else rights[0]
        total = contract_rows(jnp.concatenate(pieces, axis=0), right)
        for part, ((first, count), send) in enumerate(zip(PARTS, (send_one, send_two))):
            if first <= slot < first + count:
                low, high, at_low = total[:128], total[128:], place_of(at, part, 0) == 0
                keep[slot] = jnp.where(at_low, low, high).astype(LOW)
                send[slot - first] = jnp.where(at_low, high, low).astype(LOW)


def fold_kernel(step, at, *refs):
    size = 256 >> (step + 1)
    extra = 0 if step == 2 else 2
    own, got = refs[:extra] or (None, None)
    refs = refs[extra:]
    keep, gots, stay, sends = refs[0], refs[1:3], refs[3], refs[4:]
    for part, (first, count) in enumerate(PARTS):
        here = slice(first, first + count)
        if step == 3:
            stay[here] = keep[here] + gots[part][...]
            continue
        mine = place_of(at, part, step)
        for which, out in ((mine, 0), (1 - mine, 1)):
            rows = pl.ds(pl.multiple_of(which * size, size), size)
            value = keep[here, rows] + gots[part][:, rows]
            if out == 0:
                stay[here] = value
            else:
                sends[part][...] = value
    if step == 1:
        pair = sends[2]
        pair[at[3]] = own[...]
        pair[1 - at[3]] = got[...]
    if step == 3:
        line, moments = sends
        for which, piece in ((at[2], own), (1 - at[2], got)):
            for far in range(2):
                line[far * 2 + which] = piece[far, :SLOTS].reshape(SLOTS * 16, CO)
                moments[far * 2 + which] = piece[far, SLOTS]


def moment_kernel(
    at, rate, own, got, moments, line, line_one, line_two, scaled_one, scaled_two, lines,
):
    for index, piece in enumerate((line, line_one, line_two)):
        lines[index] = piece[...]
    count = SLOTS * BLK
    total = (own[...].astype(WIDE) + got[...].astype(WIDE)).reshape(count, CO)
    squares = total * total
    decay = rate[0]
    mean = jnp.sum(squares, axis=1, keepdims=True) * (1.0 / CO)
    row_moment = jnp.concatenate([moments[:, slot : slot + 1] for slot in range(SLOTS)], axis=0)
    new_row = decay * row_moment + (1.0 - decay) * mean
    value = (total * lax.rsqrt(new_row)).astype(LOW).reshape(SLOTS, BLK, CO)
    split = PARTS[0][1]
    scaled_one[...] = value[:split]
    scaled_two[: SLOTS - split] = value[split:]
    weighted = squares / new_row
    cut = count - BLK
    last_small = at[4] == 1
    rows = []
    for values in (squares, weighted, jnp.broadcast_to(new_row, (count, CO))):
        large = jnp.sum(values[:cut], axis=0, keepdims=True)
        last = jnp.sum(values[cut:], axis=0, keepdims=True)
        rows.append(large + jnp.where(last_small, 0.0, last))
        rows.append(jnp.where(last_small, last, 0.0))
    spread = jnp.broadcast_to(new_row, (count, 128))
    spread = jnp.concatenate([spread, jnp.zeros((512 - count, 128), WIDE)], axis=0)
    rows += [jnp.transpose(spread[:CO])[:1], jnp.transpose(spread[CO:])[:1]]
    message = jnp.concatenate(rows, axis=0)
    high = message.astype(LOW).astype(WIDE)
    message = jnp.concatenate([high, message - high, jnp.zeros((16, CO), WIDE)], axis=0)
    scaled_two[SLOTS - split] = message.astype(LOW)


def store_factors(total, decay, col_moment, new_col, factor):
    for kernel in range(2):
        count = 27.0 * CI if kernel == 0 else float(CO)
        col = decay * col_moment[kernel : kernel + 1] + (1.0 - decay) * (
            total[kernel : kernel + 1] / count
        )
        row_mean = total[4 + kernel : 5 + kernel] / count
        square = row_mean * jnp.sum(
            total[2 + kernel : 3 + kernel] / col, axis=1, keepdims=True
        )
        clip = jnp.maximum(1.0, jnp.sqrt(square / (count * CO)))
        new_col[kernel : kernel + 1] = col
        factor[kernel : kernel + 1] = 1.0 / (jnp.sqrt(col / row_mean) * clip)


def moments_kernel(at, block_order, mine, peer, out, plan, table, rows, inverse):
    core = at[4]
    owner = at[3] * 4 + at[2] * 2 + core

    def place_block(local, carry):
        block = block_order[owner * (NB // 8) + local]
        half = (block >= 8 * SLOTS).astype(jnp.int32)
        slot, place = (block - half * (8 * SLOTS)) // 8, lax.rem(block, 8)
        high, middle, low = place // 4, lax.rem(place // 2, 2), lax.rem(place, 2)
        other = low * 4 + high * 2 + middle
        sender = jnp.where(slot < PARTS[1][0], other, place)
        side = half ^ core
        plan[local * 8] = side
        plan[local * 8 + 1] = slot
        plan[local * 8 + 2] = place * BLK
        plan[local * 8 + 3] = (block >= NB3).astype(jnp.int32)
        plan[local * 8 + 4] = (side * 8 + sender) * 4 + slot // 4
        plan[local * 8 + 5] = lax.rem(128 + (lax.rem(local, 4) - lax.rem(slot, 4)) * BLK, 128)
        return carry

    lax.fori_loop(0, NB // 8, place_block, 0, unroll=4)
    for side, ref in enumerate((mine, peer)):
        for line in range(4):
            values = ref[line].astype(WIDE)
            values = values[:, :128] + values[:, 128:]
            table[pl.ds(pl.multiple_of((line * 2 + (core ^ side)) * 8, 8), 8), :] = values[:8]

    def invert(stored, carry):
        inverse[block_order[stored]] = stored
        return carry

    lax.fori_loop(0, NB, invert, 0, unroll=8)
    rows[...] = jnp.zeros((128, 128), WIDE)
    for part, (first, count) in enumerate(PARTS):
        place = place_of(at, part, 0) * 4 + place_of(at, part, 1) * 2 + place_of(at, part, 2)
        for slot in range(first, first + count):
            stored = inverse[(core * SLOTS + slot) * 8 + place]
            owner, local = stored // (NB // 8), lax.rem(stored, NB // 8)
            row = table[pl.ds(owner * 8 + local // 4, 1), :]
            turn = lax.rem(128 - lax.rem(local, 4) * BLK, 128)
            rows[slot : slot + 1] = pltpu.roll(row, turn, 1)
    out[...] = jnp.transpose(rows[...])[:BLK]


def order_kernel(at, block_order, mine, mine_low, mine_high, peer, peer_low, peer_high, out):
    count = NB // 8
    quarters = count // 4
    for flip_core, (pieces, low, high) in enumerate(
        ((mine, mine_low, mine_high), (peer, peer_low, peer_high))
    ):
        core = at[4] ^ flip_core
        for index in range(4):
            flip_x = jnp.where(core == 0, index // 2, index % 2)
            quarter = (at[1] ^ (index // 2) ^ (index % 2) ^ flip_x) * 2 + (at[0] ^ flip_x)
            for local in range(quarters):
                for line in range(4):
                    block = block_order[(line * 2 + core) * count + quarter * quarters + local]
                    to = pl.ds(pl.multiple_of(block * BLK, BLK), BLK)
                    rows = slice(local * BLK, local * BLK + BLK)
                    if index < 3:
                        out[to, :] = pieces[index, line, rows]
                    else:
                        out[to, :] = (low, high)[line // 2][line % 2, rows]


def widen_kernel(step, at, after, *refs):
    size = 256 >> (step + 1)
    ins, outs = refs[:4], refs[4:]
    if step == 1:
        outs[2][...], outs[3][...] = after[:2], after[2:]
    for part, (first, count) in enumerate(GATHERED):
        mine = place_of(at, part, step)
        for index, which in enumerate((mine, 1 - mine)):
            rows = pl.ds(pl.multiple_of(which * size, size), size)
            value = ins[2 * part + index][...]
            if step == 0:
                outs[0][first : first + count, rows] = value
            else:
                outs[part][:, rows] = value


def window(views, starts):
    return jnp.concatenate([views[pl.ds(start, HW * HW), :] for start in starts], axis=0)


def old_hidden_kernel(at, views, natural, hidden):
    total = jnp.zeros((PIX, CO), WIDE)
    for tap in range(27):
        weights = natural[tap * CI : tap * CI + CI]
        starts = [view_start(tap, frame) for frame in range(FR)]
        total = total + jnp.dot(window(views, starts), weights, preferred_element_type=WIDE)
    hidden[...] = total


def add_taps(views, scaled, core):
    total = jnp.zeros((PIX, CO), WIDE)
    for slot in range(SLOTS):
        starts = [core_start(core, slot, frame) for frame in range(FR)]
        weights = scaled[slot]
        if slot == SLOTS - 1:
            weights = jnp.where(core == 0, weights.astype(WIDE), 0.0).astype(LOW)
        total = total + jnp.dot(window(views, starts), weights, preferred_element_type=WIDE)
    return total


def half_hidden_kernel(at, views, scaled, hidden):
    hidden[...] = add_taps(views, scaled, at[4])


def finish_kernel(
    at, plan, rate, col_moment, views, natural, master, mine, peer, old, own_part,
    update_far, master_far, row_far, col_far, output_far,
    factor, row_table, update_rows, new_master, new_row, new_col, next_output, stored, rest_stored,
):
    core = at[4]
    sums = []
    for piece in (mine, peer):
        messages = [
            piece[MESSAGE, sender * BLK : sender * BLK + 16].astype(WIDE) for sender in range(8)
        ]
        sums.append([message[:8] + message[8:] for message in messages])
    total = sum(sums[0][1:] + sums[1], sums[0][0])
    store_factors(total, rate[0], col_moment, new_col, factor)

    def store(source, target, index):
        copy = pltpu.make_async_copy(source, target, rest_stored.at[index])
        copy.start()
        return [copy]

    copies = store(new_col, col_far, 0)

    for line in range(7):
        for local in range(line * 4, line * 4 + 4):
            side, slot, first, kernel = (plan[local * 8 + item] for item in range(4))
            rows = slice(local * BLK, local * BLK + BLK)
            there = pl.ds(pl.multiple_of(first, BLK), BLK)
            value = jnp.where(
                side == 0, mine[slot, there, :].astype(WIDE), peer[slot, there, :].astype(WIDE)
            )
            update = value * factor[pl.ds(kernel, 1), :]
            update_rows[rows, :] = update
            new_master[rows, :] = master[rows, :] - learn_rate * update
        there = pl.ds(line * 4 * BLK, 4 * BLK)
        pairs = ((update_rows, update_far), (new_master, master_far))
        copies += fetch(
            [(source.at[there, :], target.at[there, :]) for source, target in pairs],
            stored.at[line],
        )

    change = own_part[...] + add_taps(views, peer, 1 - core)
    hidden = old[...] - (learn_rate * factor[0:1]) * change
    small = jnp.where(core == 1, mine[SLOTS - 1].astype(WIDE), peer[SLOTS - 1].astype(WIDE))
    weights = natural[27 * CI :].astype(WIDE) - small * (learn_rate * factor[1:2])
    next_output[...] = jnp.dot(
        jax.nn.silu(hidden).astype(LOW), weights.astype(LOW), preferred_element_type=WIDE
    ).astype(LOW)
    copies += store(next_output, output_far, 1)

    for side, messages in enumerate(sums):
        for sender in range(8):
            for line in range(4):
                to = (side * 8 + sender) * 4 + line
                row_table[to : to + 1] = messages[sender][
                    6 + line // 2 : 7 + line // 2, line % 2 * 128 : line % 2 * 128 + 128
                ]
    lane = lax.broadcasted_iota(jnp.int32, (1, 128), 1)
    for line in range(7):
        values = jnp.zeros((1, 128), WIDE)
        for part in range(4):
            from_row, turn = (plan[(line * 4 + part) * 8 + item] for item in (4, 5))
            here = (lane >= part * BLK) & (lane < part * BLK + BLK)
            turned = pltpu.roll(row_table[pl.ds(from_row, 1), :], turn, 1)
            values = jnp.where(here, turned, values)
        new_row[line : line + 1] = values
    copies += store(new_row, row_far, 2)
    for copy in copies:
        copy.wait()


def shards(
    step_count,
    block_order,
    saved_tiles,
    pre_act,
    grad_output,
    pointwise_live,
    master_rows,
    row_moment,
    col_moment,
    next_tiles,
):
    decay_rate = 1.0 - step_count.astype(WIDE) ** (-decay_power)

    tile_peer = swap(saved_tiles, MASK_CORE)
    pre_peer = swap(pre_act, MASK_CORE)
    grad_peer = swap(grad_output, MASK_CORE)
    rows_far = [far_away(array) for array in (pre_act, grad_output, pointwise_live)]
    brought, grad_near, pointwise_near = call(
        own_kernel,
        [((BROUGHT, CI), LOW), ((PIX, CO), LOW), ((CO, CO), LOW)],
        [VMEM] + [HBM] * 3,
        scratch=[pltpu.VMEM((PIX, CO), LOW), pltpu.SemaphoreType.DMA((3,))],
        moved=4 << 20,
    )(saved_tiles[0], *rows_far)

    keep, *sends = call(
        term_kernel,
        [((SLOTS, 128, CO), LOW)] + [((count, 128, CO), LOW) for _, count in PARTS],
        [VMEM] * 6,
        scratch=[pltpu.VMEM((BROUGHT, CI), LOW), pltpu.VMEM((2, 2 * PIX, CO), LOW)],
        flops=2 * 14 * 1024 * 256 * 256,
        moved=6 << 20,
        room=12,
    )(brought, tile_peer[0], pre_peer, grad_peer, grad_near, pointwise_near)

    packed = call(
        pack_kernel,
        [((SLOTS + 1, 16, CO), LOW)],
        [HBM] * 3,
        scratch=[
            pltpu.VMEM((SLOTS * 16, CO), WIDE),
            pltpu.VMEM((16, 128), WIDE),
            pltpu.SemaphoreType.DMA((2,)),
        ],
    )(keep, far_away(master_rows), far_away(row_moment.reshape(7, 128)))[0]
    packed_far = swap(packed, MASK_FAR)
    views = call(shift_kernel, [((3 * SHIFTED, CI), LOW)], [VMEM], moved=3 << 20)(next_tiles[0])[0]

    for step in range(1, 4):
        gots = [swap_part(send, part, step - 1) for part, send in enumerate(sends)]
        size = 256 >> (step + 1)
        outs = [((SLOTS, size, CO), LOW)] + [((count, size, CO), LOW) for _, count in PARTS]
        if step == 1:
            extra = [packed, packed_far]
            outs = outs + [((2, SLOTS + 1, 16, CO), LOW)]
        elif step == 2:
            extra = []
        else:
            extra = [pair, pair_near]
            outs = [((SLOTS, BLK, CO), LOW), ((4, SLOTS * 16, CO), LOW), ((4, 16, CO), LOW)]
        keep, *sends = call(
            functools.partial(fold_kernel, step),
            outs,
            [VMEM] * (len(extra) + 3),
            moved=1 << 20,
        )(*extra, keep, *gots)
        if step == 1:
            pair = sends.pop()
            pair_near = swap(pair, MASK_NEAR)
    line, moments = sends
    line_one, line_two = swap_mixed(line, (MASK_Y, MASK_X)), swap_mixed(line, (MASK_X, MASK_Y))
    own_moment, plan = call(
        moments_kernel,
        [((BLK, 128), WIDE), ((NB,), jnp.int32)],
        [SMEM] + [VMEM] * 2,
        out_specs=[VMEM, SMEM],
        pin=False,
        scratch=[
            pltpu.VMEM((64, 128), WIDE),
            pltpu.VMEM((128, 128), WIDE),
            pltpu.SMEM((NB,), jnp.int32),
        ],
    )(block_order, moments, swap(moments, MASK_CORE))
    *scaled, lines = call(
        moment_kernel,
        [((count, BLK, CO), LOW) for _, count in GATHERED] + [((3, 4, SLOTS * 16, CO), LOW)],
        [SMEM] + [VMEM] * 6,
        moved=2 << 20,
    )(decay_rate, keep, swap(keep, MASK_FAR), own_moment, line, line_one, line_two)
    line_far = swap_mixed(line_one, (MASK_X, MASK_Y))
    joined, natural = scaled, None
    for step in range(2, -1, -1):
        pieces = []
        for part, value in enumerate(joined):
            pieces += [value, swap_part(value, part, step)]
        size = 256 >> step
        outs = [((count, size, CO), LOW) for _, count in GATHERED]
        if step == 0:
            outs = [((SLOTS + 1, size, CO), LOW)]
        if step == 1:
            outs = outs + [((2, SLOTS * 16, CO), LOW)] * 2
        joined = call(
            functools.partial(widen_kernel, step),
            outs,
            [VMEM if step == 1 else HBM] + [VMEM] * len(pieces),
        )((natural, line_far, views)[step], *pieces)
        if step == 1:
            parts = [lines, *joined[2:]]
            joined = joined[:2]
            natural = call(
                order_kernel, [((NB * BLK, CO), LOW)], [SMEM] + [VMEM] * 6, moved=8 << 20
            )(block_order, *parts, *[swap(part, MASK_CORE) for part in parts])[0]
    mine = joined[0]
    peer = swap(mine, MASK_CORE)
    old = call(
        old_hidden_kernel,
        [((PIX, CO), WIDE)],
        [VMEM] * 2,
        flops=2 * 27 * 512 * 256 * 256,
        moved=6 << 20,
    )(views, natural)[0]
    half = call(
        half_hidden_kernel,
        [((PIX, CO), WIDE)],
        [VMEM] * 2,
        flops=2 * 14 * 512 * 256 * 256,
        moved=4 << 20,
    )(views, mine)[0]

    outs = [
        ((NB // 8 * BLK, CO), WIDE),
        ((NB // 8 * BLK, CO), WIDE),
        ((7, 128), WIDE),
        ((2, CO), WIDE),
        ((PIX, CO), LOW),
    ]
    update_rows, new_master, new_row, new_col, next_output = call(
        finish_kernel,
        outs,
        [SMEM] * 2 + [VMEM] * 8,
        out_specs=[HBM] * 5,
        scratch=[
            pltpu.VMEM((2, CO), WIDE),
            pltpu.VMEM((64, 128), WIDE),
            pltpu.VMEM((NB // 8 * BLK, CO), WIDE),
            pltpu.VMEM((NB // 8 * BLK, CO), WIDE),
            pltpu.VMEM((7, 128), WIDE),
            pltpu.VMEM((2, CO), WIDE),
            pltpu.VMEM((PIX, CO), LOW),
            pltpu.SemaphoreType.DMA((7, 2)),
            pltpu.SemaphoreType.DMA((3,)),
        ],
        pin=False,
        flops=2 * 16 * 512 * 256 * 256,
        moved=16 << 20,
        room=16,
    )(plan, decay_rate, col_moment, views, natural, master_rows, mine, peer, old, half)
    return (update_rows, new_master, new_row.reshape(-1), new_col, next_output)


def solution(mesh):
    in_specs = (
        P(),
        P(),
        P(("group", "shard"), None, None, None, None),
        P(("group", "shard"), None),
        P(("group", "shard"), None),
        P(),
        P("shard", None),
        P("shard"),
        P(),
        P(("group", "shard"), None, None, None, None),
    )
    out_specs = (P("shard", None), P("shard", None), P("shard"), P(), P(("group", "shard"), None))
    body = shards if (mesh.shape["group"], mesh.shape["shard"]) == (4, 8) else general_shards
    return jax.shard_map(body, mesh=mesh, in_specs=in_specs, out_specs=out_specs, check_vma=False)
```

```python
import functools
import jax
import jax.numpy as jnp
from jax import lax
from jax.experimental import pallas as pl
from jax.experimental.pallas import tpu as pltpu
from jax.sharding import PartitionSpec as P

CI = 256
CO = 256
BLK = 32
FR = 2
HW = 16
NB3 = 216
NB = 224


learn_rate = 0.002
decay_power = 0.8


def silu_slope(values):
    sigma = jax.nn.sigmoid(values)
    return sigma * (1.0 + values * (1.0 - sigma))


def tap_views(frames):
    views = []
    for frame_off in range(3):
        for row_off in range(3):
            for col_off in range(3):
                window = frames[
                    frame_off : frame_off + FR, row_off : row_off + HW, col_off : col_off + HW, :
                ]
                views.append(window.reshape(FR * HW * HW, CI))
    return views


def contract_rows(left, right):
    return lax.dot_general(
        left, right, (((0,), (0,)), ((), ())), preferred_element_type=jnp.float32
    )


def kernel_sums(values, is_small):
    large_part = jnp.sum(jnp.where(is_small[:, None], 0.0, values), axis=0)
    small_part = jnp.sum(jnp.where(is_small[:, None], values, 0.0), axis=0)
    return jnp.stack([large_part, small_part])


def general_shards(
    step_count,
    block_order,
    saved_tiles,
    pre_act,
    grad_output,
    pointwise_live,
    master_rows,
    row_moment,
    col_moment,
    next_tiles,
):
    pre_float = pre_act.astype(jnp.float32)
    activation = jax.nn.silu(pre_float).astype(jnp.bfloat16)
    grad_act = lax.dot_general(
        grad_output, pointwise_live, (((1,), (1,)), ((), ())), preferred_element_type=jnp.float32
    )
    grad_pre = (grad_act * silu_slope(pre_float)).astype(jnp.bfloat16)
    pieces = [contract_rows(view, grad_pre) for view in tap_views(saved_tiles[0])]
    pieces.append(contract_rows(activation, grad_output))
    own_term = jnp.concatenate(pieces, axis=0).astype(jnp.bfloat16)
    total_rows = NB * BLK
    stored = jnp.take(own_term.reshape(NB, BLK, CO), block_order, axis=0).reshape(total_rows, CO)
    own_rows = master_rows.shape[0]
    partial_value = lax.psum_scatter(stored, "shard", scatter_dimension=0, tiled=True).astype(
        jnp.float32
    )
    gradient = lax.psum(partial_value, "group")
    owner = lax.axis_index("shard")
    own_count = own_rows // BLK
    own_blocks = lax.dynamic_slice_in_dim(block_order, owner * own_count, own_count)
    is_small = jnp.repeat(own_blocks >= NB3, BLK, total_repeat_length=own_rows)
    decay_rate = 1.0 - step_count.astype(jnp.float32)[0] ** (-decay_power)
    counts = jnp.array([27 * CI, CO], jnp.float32)
    squares = gradient * gradient
    new_row = decay_rate * row_moment + (1.0 - decay_rate) * jnp.mean(squares, axis=1)
    col_part = kernel_sums(squares, is_small)
    row_part = kernel_sums(new_row[:, None], is_small)[:, 0]
    weighted = kernel_sums(squares / new_row[:, None], is_small)
    col_total, weight_total, row_total = lax.psum((col_part, weighted, row_part), "shard")
    new_col = decay_rate * col_moment + (1.0 - decay_rate) * col_total / counts[:, None]
    row_mean = row_total / counts
    col_rows = jnp.where(is_small[:, None], new_col[1], new_col[0])
    mean_rows = jnp.where(is_small, row_mean[1], row_mean[0])
    scaled = gradient / jnp.sqrt(new_row[:, None] * col_rows / mean_rows[:, None])
    square_total = row_mean * jnp.sum(weight_total / new_col, axis=1)
    clip_factor = jnp.maximum(1.0, jnp.sqrt(square_total / (counts * CO)))
    update_rows = scaled / jnp.where(is_small, clip_factor[1], clip_factor[0])[:, None]
    new_master = master_rows - learn_rate * update_rows
    weights_low = new_master.astype(jnp.bfloat16)
    gathered = lax.all_gather(weights_low, "shard", axis=0, tiled=True)
    inverse = jnp.zeros((NB,), jnp.int32).at[block_order].set(jnp.arange(NB, dtype=jnp.int32))
    natural = jnp.take(gathered.reshape(NB, BLK, CO), inverse, axis=0).reshape(total_rows, CO)
    spatial = natural[: 27 * CI].reshape(27, CI, CO)
    pointwise = natural[27 * CI :]
    hidden_sum = jnp.zeros((FR * HW * HW, CO), jnp.float32)
    for index_tap, view in enumerate(tap_views(next_tiles[0])):
        hidden_sum = hidden_sum + jnp.dot(
            view, spatial[index_tap], preferred_element_type=jnp.float32
        )
    hidden_act = jax.nn.silu(hidden_sum).astype(jnp.bfloat16)
    next_output = jnp.dot(hidden_act, pointwise, preferred_element_type=jnp.float32).astype(
        jnp.bfloat16
    )
    return (update_rows, new_master, new_row, new_col, next_output)


AXES = ("group", "shard")
SLOTS = 14
PIX = FR * HW * HW
SHIFTED = (FR + 2) * (HW + 2) * HW
SLOPES = 3 * SHIFTED
ACTS = SLOPES + PIX
BROUGHT = ACTS + PIX
LOW = jnp.bfloat16
WIDE = jnp.float32
VMEM = pl.BlockSpec(memory_space=pltpu.VMEM)
SMEM = pl.BlockSpec(memory_space=pltpu.SMEM)
HBM = pl.BlockSpec(memory_space=pl.ANY)
MASK_CORE, MASK_NEAR, MASK_FAR, MASK_X, MASK_Y = 1, 2, 4, 8, 16
PARTS = ((0, 11), (11, 3))
ORDERS = (((0, 1, 2), (1, 0, 2)), ((2, 0, 1), (2, 1, 0)))
MESSAGE = SLOTS
GATHERED = ((0, 11), (11, 4))
MASKS = (MASK_X, MASK_Y, MASK_NEAR)


def swap(value, mask):
    return lax.ppermute(value, AXES, [(at, at ^ mask) for at in range(32)])


def swap_mixed(value, masks):
    return lax.ppermute(value, AXES, [(at, at ^ masks[at & 1]) for at in range(32)])


def swap_part(value, part, step):
    return swap_mixed(value, [MASKS[ORDERS[part][core][step]] for core in range(2)])


def place_of(at, part, step):
    zero, one = (ORDERS[part][core][step] for core in range(2))
    return at[zero] if zero == one else jnp.where(at[4] == 0, at[zero], at[one])


def position():
    group, shard = lax.axis_index("group"), lax.axis_index("shard")
    return group % 2, group // 2, shard // 2 % 2, shard // 4, shard % 2


def call(kernel, outs, in_specs, out_specs=None, scratch=(), flops=0, moved=0, room=8, pin=True):
    return pl.pallas_call(
        lambda *refs: kernel(position(), *refs),
        out_shape=[(pltpu.VMEM if pin else jax.ShapeDtypeStruct)(*out) for out in outs],
        in_specs=in_specs,
        out_specs=out_specs or [VMEM] * len(outs),
        scratch_shapes=list(scratch),
        compiler_params=pltpu.CompilerParams(vmem_limit_bytes=room << 20),
        cost_estimate=pl.CostEstimate(flops=flops, bytes_accessed=moved, transcendentals=0),
    )


def far_away(array):
    return pltpu.with_memory_space_constraint(array, pltpu.HBM)


def store_shifted(tile, out):
    for col_off in range(3):
        out[col_off * SHIFTED : (col_off + 1) * SHIFTED] = tile[
            :, :, col_off : col_off + HW, :
        ].reshape(SHIFTED, CI)


def shift_kernel(at, tile, out):
    store_shifted(tile, out)


def store_factors_of(pre, grad, pointwise, out):
    values = pre[...].astype(WIDE)
    sigma = jax.nn.sigmoid(values)
    grad_act = lax.dot_general(
        grad[...], pointwise[...], (((1,), (1,)), ((), ())), preferred_element_type=WIDE
    )
    out[SLOPES:ACTS] = (grad_act * (sigma * (1.0 + values * (1.0 - sigma)))).astype(LOW)
    out[ACTS:] = (values * sigma).astype(LOW)


def view_start(tap, frame):
    frame_off, row_off, col_off = tap // 9, tap // 3 % 3, tap % 3
    return col_off * SHIFTED + ((frame + frame_off) * (HW + 2) + row_off) * HW


def core_start(core, slot, frame):
    return pl.multiple_of(
        jnp.where(core == 0, view_start(slot, frame), view_start(min(SLOTS + slot, 26), frame)), HW
    )


def fetch(pairs, arrived):
    copies = [
        pltpu.make_async_copy(source, target, arrived.at[index])
        for index, (source, target) in enumerate(pairs)
    ]
    for copy in copies:
        copy.start()
    return copies


def own_kernel(
    at, tile, pre_far, grad_far, pointwise_far, brought, grad, pointwise, pre, arrived
):
    copies = fetch(((pre_far, pre), (grad_far, grad), (pointwise_far, pointwise)), arrived)
    store_shifted(tile, brought)
    for copy in copies:
        copy.wait()
    store_factors_of(pre, grad, pointwise, brought)


def pack_kernel(at, after, master_far, row_moment_far, packed, master, row_moment, arrived):
    quarter = pl.multiple_of((at[1] * 2 + at[0]) * (SLOTS * 16), SLOTS * 16)
    row_moment[...] = jnp.zeros((16, 128), WIDE)
    copies = fetch(
        (
            (master_far.at[pl.ds(quarter, SLOTS * 16), :], master),
            (row_moment_far, row_moment.at[pl.ds(0, 7), :]),
        ),
        arrived,
    )
    for copy in copies:
        copy.wait()
    packed[:SLOTS] = master[...].astype(LOW).reshape(SLOTS, 16, CO)
    high = row_moment[...].astype(LOW).astype(WIDE)
    packed[SLOTS] = jnp.concatenate([high, row_moment[...] - high], axis=1).astype(LOW)


def term_kernel(
    at, own, tile_peer, pre_peer, grad_peer, grad, pointwise, keep, send_one, send_two, peer, rights
):
    core = at[4]
    store_shifted(tile_peer, peer)
    store_factors_of(pre_peer, grad_peer, pointwise, peer)
    rights[0, :PIX] = own[SLOPES:ACTS]
    rights[0, PIX:] = peer[SLOPES:ACTS]
    rights[1, :PIX] = grad[...]
    rights[1, PIX:] = grad_peer[...]
    for slot in range(SLOTS):
        pieces = []
        for ref in (own, peer):
            for frame in range(FR):
                start = core_start(core, slot, frame)
                if slot == SLOTS - 1:
                    start = jnp.where(core == 0, start, ACTS + frame * HW * HW)
                pieces.append(ref[pl.ds(pl.multiple_of(start, HW), HW * HW), :])
        right = rights[core] if slot == SLOTS - 1 else rights[0]
        total = contract_rows(jnp.concatenate(pieces, axis=0), right)
        for part, ((first, count), send) in enumerate(zip(PARTS, (send_one, send_two))):
            if first <= slot < first + count:
                low, high, at_low = total[:128], total[128:], place_of(at, part, 0) == 0
                keep[slot] = jnp.where(at_low, low, high).astype(LOW)
                send[slot - first] = jnp.where(at_low, high, low).astype(LOW)


def fold_kernel(step, at, *refs):
    size = 256 >> (step + 1)
    extra = 0 if step == 2 else 2
    own, got = refs[:extra] or (None, None)
    refs = refs[extra:]
    keep, gots, stay, sends = refs[0], refs[1:3], refs[3], refs[4:]
    for part, (first, count) in enumerate(PARTS):
        here = slice(first, first + count)
        if step == 3:
            stay[here] = keep[here] + gots[part][...]
            continue
        mine = place_of(at, part, step)
        for which, out in ((mine, 0), (1 - mine, 1)):
            rows = pl.ds(pl.multiple_of(which * size, size), size)
            value = keep[here, rows] + gots[part][:, rows]
            if out == 0:
                stay[here] = value
            else:
                sends[part][...] = value
    if step == 1:
        pair = sends[2]
        pair[at[3]] = own[...]
        pair[1 - at[3]] = got[...]
    if step == 3:
        line, moments = sends
        for which, piece in ((at[2], own), (1 - at[2], got)):
            for far in range(2):
                line[far * 2 + which] = piece[far, :SLOTS].reshape(SLOTS * 16, CO)
                moments[far * 2 + which] = piece[far, SLOTS]


def moment_kernel(
    at, rate, own, got, moments, line, line_one, line_two, scaled_one, scaled_two, lines,
):
    for index, piece in enumerate((line, line_one, line_two)):
        lines[index] = piece[...]
    count = SLOTS * BLK
    total = (own[...].astype(WIDE) + got[...].astype(WIDE)).reshape(count, CO)
    squares = total * total
    decay = rate[0]
    mean = jnp.sum(squares, axis=1, keepdims=True) * (1.0 / CO)
    row_moment = jnp.concatenate([moments[:, slot : slot + 1] for slot in range(SLOTS)], axis=0)
    new_row = decay * row_moment + (1.0 - decay) * mean
    value = (total * lax.rsqrt(new_row)).astype(LOW).reshape(SLOTS, BLK, CO)
    split = PARTS[0][1]
    scaled_one[...] = value[:split]
    scaled_two[: SLOTS - split] = value[split:]
    weighted = squares / new_row
    cut = count - BLK
    last_small = at[4] == 1
    rows = []
    for values in (squares, weighted, jnp.broadcast_to(new_row, (count, CO))):
        large = jnp.sum(values[:cut], axis=0, keepdims=True)
        last = jnp.sum(values[cut:], axis=0, keepdims=True)
        rows.append(large + jnp.where(last_small, 0.0, last))
        rows.append(jnp.where(last_small, last, 0.0))
    spread = jnp.broadcast_to(new_row, (count, 128))
    spread = jnp.concatenate([spread, jnp.zeros((512 - count, 128), WIDE)], axis=0)
    rows += [jnp.transpose(spread[:CO])[:1], jnp.transpose(spread[CO:])[:1]]
    message = jnp.concatenate(rows, axis=0)
    high = message.astype(LOW).astype(WIDE)
    message = jnp.concatenate([high, message - high, jnp.zeros((16, CO), WIDE)], axis=0)
    scaled_two[SLOTS - split] = message.astype(LOW)


def store_factors(total, decay, col_moment, new_col, factor):
    for kernel in range(2):
        count = 27.0 * CI if kernel == 0 else float(CO)
        col = decay * col_moment[kernel : kernel + 1] + (1.0 - decay) * (
            total[kernel : kernel + 1] / count
        )
        row_mean = total[4 + kernel : 5 + kernel] / count
        square = row_mean * jnp.sum(
            total[2 + kernel : 3 + kernel] / col, axis=1, keepdims=True
        )
        clip = jnp.maximum(1.0, jnp.sqrt(square / (count * CO)))
        new_col[kernel : kernel + 1] = col
        factor[kernel : kernel + 1] = 1.0 / (jnp.sqrt(col / row_mean) * clip)


def moments_kernel(at, block_order, mine, peer, out, plan, table, rows, inverse):
    core = at[4]
    owner = at[3] * 4 + at[2] * 2 + core

    def place_block(local, carry):
        block = block_order[owner * (NB // 8) + local]
        half = (block >= 8 * SLOTS).astype(jnp.int32)
        slot, place = (block - half * (8 * SLOTS)) // 8, lax.rem(block, 8)
        high, middle, low = place // 4, lax.rem(place // 2, 2), lax.rem(place, 2)
        other = low * 4 + high * 2 + middle
        sender = jnp.where(slot < PARTS[1][0], other, place)
        side = half ^ core
        plan[local * 8] = side
        plan[local * 8 + 1] = slot
        plan[local * 8 + 2] = place * BLK
        plan[local * 8 + 3] = (block >= NB3).astype(jnp.int32)
        plan[local * 8 + 4] = (side * 8 + sender) * 4 + slot // 4
        plan[local * 8 + 5] = lax.rem(128 + (lax.rem(local, 4) - lax.rem(slot, 4)) * BLK, 128)
        return carry

    lax.fori_loop(0, NB // 8, place_block, 0, unroll=4)
    for side, ref in enumerate((mine, peer)):
        for line in range(4):
            values = ref[line].astype(WIDE)
            values = values[:, :128] + values[:, 128:]
            table[pl.ds(pl.multiple_of((line * 2 + (core ^ side)) * 8, 8), 8), :] = values[:8]

    def invert(stored, carry):
        inverse[block_order[stored]] = stored
        return carry

    lax.fori_loop(0, NB, invert, 0, unroll=8)
    rows[...] = jnp.zeros((128, 128), WIDE)
    for part, (first, count) in enumerate(PARTS):
        place = place_of(at, part, 0) * 4 + place_of(at, part, 1) * 2 + place_of(at, part, 2)
        for slot in range(first, first + count):
            stored = inverse[(core * SLOTS + slot) * 8 + place]
            owner, local = stored // (NB // 8), lax.rem(stored, NB // 8)
            row = table[pl.ds(owner * 8 + local // 4, 1), :]
            turn = lax.rem(128 - lax.rem(local, 4) * BLK, 128)
            rows[slot : slot + 1] = pltpu.roll(row, turn, 1)
    out[...] = jnp.transpose(rows[...])[:BLK]


def order_kernel(at, block_order, mine, mine_low, mine_high, peer, peer_low, peer_high, out):
    count = NB // 8
    quarters = count // 4
    for flip_core, (pieces, low, high) in enumerate(
        ((mine, mine_low, mine_high), (peer, peer_low, peer_high))
    ):
        core = at[4] ^ flip_core
        for index in range(4):
            flip_x = jnp.where(core == 0, index // 2, index % 2)
            quarter = (at[1] ^ (index // 2) ^ (index % 2) ^ flip_x) * 2 + (at[0] ^ flip_x)
            for local in range(quarters):
                for line in range(4):
                    block = block_order[(line * 2 + core) * count + quarter * quarters + local]
                    to = pl.ds(pl.multiple_of(block * BLK, BLK), BLK)
                    rows = slice(local * BLK, local * BLK + BLK)
                    if index < 3:
                        out[to, :] = pieces[index, line, rows]
                    else:
                        out[to, :] = (low, high)[line // 2][line % 2, rows]


def widen_kernel(step, at, after, *refs):
    size = 256 >> (step + 1)
    ins, outs = refs[:4], refs[4:]
    if step == 1:
        outs[2][...], outs[3][...] = after[:2], after[2:]
    for part, (first, count) in enumerate(GATHERED):
        mine = place_of(at, part, step)
        for index, which in enumerate((mine, 1 - mine)):
            rows = pl.ds(pl.multiple_of(which * size, size), size)
            value = ins[2 * part + index][...]
            if step == 0:
                outs[0][first : first + count, rows] = value
            else:
                outs[part][:, rows] = value


def window(views, starts):
    return jnp.concatenate([views[pl.ds(start, HW * HW), :] for start in starts], axis=0)


def old_hidden_kernel(at, views, natural, hidden):
    total = jnp.zeros((PIX, CO), WIDE)
    for tap in range(27):
        weights = natural[tap * CI : tap * CI + CI]
        starts = [view_start(tap, frame) for frame in range(FR)]
        total = total + jnp.dot(window(views, starts), weights, preferred_element_type=WIDE)
    hidden[...] = total


def add_taps(views, scaled, core):
    total = jnp.zeros((PIX, CO), WIDE)
    for slot in range(SLOTS):
        starts = [core_start(core, slot, frame) for frame in range(FR)]
        weights = scaled[slot]
        if slot == SLOTS - 1:
            weights = jnp.where(core == 0, weights.astype(WIDE), 0.0).astype(LOW)
        total = total + jnp.dot(window(views, starts), weights, preferred_element_type=WIDE)
    return total


def half_hidden_kernel(at, views, scaled, hidden):
    hidden[...] = add_taps(views, scaled, at[4])


def finish_kernel(
    at, plan, rate, col_moment, views, natural, master, mine, peer, old, own_part,
    update_far, master_far, row_far, col_far, output_far,
    factor, row_table, update_rows, new_master, new_row, new_col, next_output, stored, rest_stored,
):
    core = at[4]
    sums = []
    for piece in (mine, peer):
        messages = [
            piece[MESSAGE, sender * BLK : sender * BLK + 16].astype(WIDE) for sender in range(8)
        ]
        sums.append([message[:8] + message[8:] for message in messages])
    total = sum(sums[0][1:] + sums[1], sums[0][0])
    store_factors(total, rate[0], col_moment, new_col, factor)

    def store(source, target, index):
        copy = pltpu.make_async_copy(source, target, rest_stored.at[index])
        copy.start()
        return [copy]

    copies = store(new_col, col_far, 0)

    for line in range(7):
        for local in range(line * 4, line * 4 + 4):
            side, slot, first, kernel = (plan[local * 8 + item] for item in range(4))
            rows = slice(local * BLK, local * BLK + BLK)
            there = pl.ds(pl.multiple_of(first, BLK), BLK)
            value = jnp.where(
                side == 0, mine[slot, there, :].astype(WIDE), peer[slot, there, :].astype(WIDE)
            )
            update = value * factor[pl.ds(kernel, 1), :]
            update_rows[rows, :] = update
            new_master[rows, :] = master[rows, :] - learn_rate * update
        there = pl.ds(line * 4 * BLK, 4 * BLK)
        pairs = ((update_rows, update_far), (new_master, master_far))
        copies += fetch(
            [(source.at[there, :], target.at[there, :]) for source, target in pairs],
            stored.at[line],
        )

    change = own_part[...] + add_taps(views, peer, 1 - core)
    hidden = old[...] - (learn_rate * factor[0:1]) * change
    small = jnp.where(core == 1, mine[SLOTS - 1].astype(WIDE), peer[SLOTS - 1].astype(WIDE))
    weights = natural[27 * CI :].astype(WIDE) - small * (learn_rate * factor[1:2])
    next_output[...] = jnp.dot(
        jax.nn.silu(hidden).astype(LOW), weights.astype(LOW), preferred_element_type=WIDE
    ).astype(LOW)
    copies += store(next_output, output_far, 1)

    for side, messages in enumerate(sums):
        for sender in range(8):
            for line in range(4):
                to = (side * 8 + sender) * 4 + line
                row_table[to : to + 1] = messages[sender][
                    6 + line // 2 : 7 + line // 2, line % 2 * 128 : line % 2 * 128 + 128
                ]
    lane = lax.broadcasted_iota(jnp.int32, (1, 128), 1)
    for line in range(7):
        values = jnp.zeros((1, 128), WIDE)
        for part in range(4):
            from_row, turn = (plan[(line * 4 + part) * 8 + item] for item in (4, 5))
            here = (lane >= part * BLK) & (lane < part * BLK + BLK)
            turned = pltpu.roll(row_table[pl.ds(from_row, 1), :], turn, 1)
            values = jnp.where(here, turned, values)
        new_row[line : line + 1] = values
    copies += store(new_row, row_far, 2)
    for copy in copies:
        copy.wait()


def shards(
    step_count,
    block_order,
    saved_tiles,
    pre_act,
    grad_output,
    pointwise_live,
    master_rows,
    row_moment,
    col_moment,
    next_tiles,
):
    decay_rate = 1.0 - step_count.astype(WIDE) ** (-decay_power)

    tile_peer = swap(saved_tiles, MASK_CORE)
    pre_peer = swap(pre_act, MASK_CORE)
    grad_peer = swap(grad_output, MASK_CORE)
    rows_far = [far_away(array) for array in (pre_act, grad_output, pointwise_live)]
    brought, grad_near, pointwise_near = call(
        own_kernel,
        [((BROUGHT, CI), LOW), ((PIX, CO), LOW), ((CO, CO), LOW)],
        [VMEM] + [HBM] * 3,
        scratch=[pltpu.VMEM((PIX, CO), LOW), pltpu.SemaphoreType.DMA((3,))],
        moved=4 << 20,
    )(saved_tiles[0], *rows_far)

    keep, *sends = call(
        term_kernel,
        [((SLOTS, 128, CO), LOW)] + [((count, 128, CO), LOW) for _, count in PARTS],
        [VMEM] * 6,
        scratch=[pltpu.VMEM((BROUGHT, CI), LOW), pltpu.VMEM((2, 2 * PIX, CO), LOW)],
        flops=2 * 14 * 1024 * 256 * 256,
        moved=6 << 20,
        room=12,
    )(brought, tile_peer[0], pre_peer, grad_peer, grad_near, pointwise_near)

    packed = call(
        pack_kernel,
        [((SLOTS + 1, 16, CO), LOW)],
        [HBM] * 3,
        scratch=[
            pltpu.VMEM((SLOTS * 16, CO), WIDE),
            pltpu.VMEM((16, 128), WIDE),
            pltpu.SemaphoreType.DMA((2,)),
        ],
    )(keep, far_away(master_rows), far_away(row_moment.reshape(7, 128)))[0]
    packed_far = swap(packed, MASK_FAR)
    views = call(shift_kernel, [((3 * SHIFTED, CI), LOW)], [VMEM], moved=3 << 20)(next_tiles[0])[0]

    for step in range(1, 4):
        gots = [swap_part(send, part, step - 1) for part, send in enumerate(sends)]
        size = 256 >> (step + 1)
        outs = [((SLOTS, size, CO), LOW)] + [((count, size, CO), LOW) for _, count in PARTS]
        if step == 1:
            extra = [packed, packed_far]
            outs = outs + [((2, SLOTS + 1, 16, CO), LOW)]
        elif step == 2:
            extra = []
        else:
            extra = [pair, pair_near]
            outs = [((SLOTS, BLK, CO), LOW), ((4, SLOTS * 16, CO), LOW), ((4, 16, CO), LOW)]
        keep, *sends = call(
            functools.partial(fold_kernel, step),
            outs,
            [VMEM] * (len(extra) + 3),
            moved=1 << 20,
        )(*extra, keep, *gots)
        if step == 1:
            pair = sends.pop()
            pair_near = swap(pair, MASK_NEAR)
    line, moments = sends
    line_one, line_two = swap_mixed(line, (MASK_Y, MASK_X)), swap_mixed(line, (MASK_X, MASK_Y))
    own_moment, plan = call(
        moments_kernel,
        [((BLK, 128), WIDE), ((NB,), jnp.int32)],
        [SMEM] + [VMEM] * 2,
        out_specs=[VMEM, SMEM],
        pin=False,
        scratch=[
            pltpu.VMEM((64, 128), WIDE),
            pltpu.VMEM((128, 128), WIDE),
            pltpu.SMEM((NB,), jnp.int32),
        ],
    )(block_order, moments, swap(moments, MASK_CORE))
    *scaled, lines = call(
        moment_kernel,
        [((count, BLK, CO), LOW) for _, count in GATHERED] + [((3, 4, SLOTS * 16, CO), LOW)],
        [SMEM] + [VMEM] * 6,
        moved=2 << 20,
    )(decay_rate, keep, swap(keep, MASK_FAR), own_moment, line, line_one, line_two)
    line_far = swap_mixed(line_one, (MASK_X, MASK_Y))
    joined, natural = scaled, None
    for step in range(2, -1, -1):
        pieces = []
        for part, value in enumerate(joined):
            pieces += [value, swap_part(value, part, step)]
        size = 256 >> step
        outs = [((count, size, CO), LOW) for _, count in GATHERED]
        if step == 0:
            outs = [((SLOTS + 1, size, CO), LOW)]
        if step == 1:
            outs = outs + [((2, SLOTS * 16, CO), LOW)] * 2
        joined = call(
            functools.partial(widen_kernel, step),
            outs,
            [VMEM if step == 1 else HBM] + [VMEM] * len(pieces),
        )((natural, line_far, views)[step], *pieces)
        if step == 1:
            parts = [lines, *joined[2:]]
            joined = joined[:2]
            natural = call(
                order_kernel, [((NB * BLK, CO), LOW)], [SMEM] + [VMEM] * 6, moved=8 << 20
            )(block_order, *parts, *[swap(part, MASK_CORE) for part in parts])[0]
    mine = joined[0]
    peer = swap(mine, MASK_CORE)
    old = call(
        old_hidden_kernel,
        [((PIX, CO), WIDE)],
        [VMEM] * 2,
        flops=2 * 27 * 512 * 256 * 256,
        moved=6 << 20,
    )(views, natural)[0]
    half = call(
        half_hidden_kernel,
        [((PIX, CO), WIDE)],
        [VMEM] * 2,
        flops=2 * 14 * 512 * 256 * 256,
        moved=4 << 20,
    )(views, mine)[0]

    outs = [
        ((NB // 8 * BLK, CO), WIDE),
        ((NB // 8 * BLK, CO), WIDE),
        ((7, 128), WIDE),
        ((2, CO), WIDE),
        ((PIX, CO), LOW),
    ]
    update_rows, new_master, new_row, new_col, next_output = call(
        finish_kernel,
        outs,
        [SMEM] * 2 + [VMEM] * 8,
        out_specs=[HBM] * 5,
        scratch=[
            pltpu.VMEM((2, CO), WIDE),
            pltpu.VMEM((64, 128), WIDE),
            pltpu.VMEM((NB // 8 * BLK, CO), WIDE),
            pltpu.VMEM((NB // 8 * BLK, CO), WIDE),
            pltpu.VMEM((7, 128), WIDE),
            pltpu.VMEM((2, CO), WIDE),
            pltpu.VMEM((PIX, CO), LOW),
            pltpu.SemaphoreType.DMA((7, 2)),
            pltpu.SemaphoreType.DMA((3,)),
        ],
        pin=False,
        flops=2 * 16 * 512 * 256 * 256,
        moved=16 << 20,
        room=16,
    )(plan, decay_rate, col_moment, views, natural, master_rows, mine, peer, old, half)
    return (update_rows, new_master, new_row.reshape(-1), new_col, next_output)


def solution(mesh):
    in_specs = (
        P(),
        P(),
        P(("group", "shard"), None, None, None, None),
        P(("group", "shard"), None),
        P(("group", "shard"), None),
        P(),
        P("shard", None),
        P("shard"),
        P(),
        P(("group", "shard"), None, None, None, None),
    )
    out_specs = (P("shard", None), P("shard", None), P("shard"), P(), P(("group", "shard"), None))
    body = shards if (mesh.shape["group"], mesh.shape["shard"]) == (4, 8) else general_shards
    return jax.shard_map(body, mesh=mesh, in_specs=in_specs, out_specs=out_specs, check_vma=False)
```

```python
import functools
import jax
import jax.numpy as jnp
from jax import lax
from jax.experimental import pallas as pl
from jax.experimental.pallas import tpu as pltpu
from jax.sharding import PartitionSpec as P

CI = 256
CO = 256
BLK = 32
FR = 2
HW = 16
NB3 = 216
NB = 224


learn_rate = 0.002
decay_power = 0.8


def silu_slope(values):
    sigma = jax.nn.sigmoid(values)
    return sigma * (1.0 + values * (1.0 - sigma))


def tap_views(frames):
    views = []
    for frame_off in range(3):
        for row_off in range(3):
            for col_off in range(3):
                window = frames[
                    frame_off : frame_off + FR, row_off : row_off + HW, col_off : col_off + HW, :
                ]
                views.append(window.reshape(FR * HW * HW, CI))
    return views


def contract_rows(left, right):
    return lax.dot_general(
        left, right, (((0,), (0,)), ((), ())), preferred_element_type=jnp.float32
    )


def kernel_sums(values, is_small):
    large_part = jnp.sum(jnp.where(is_small[:, None], 0.0, values), axis=0)
    small_part = jnp.sum(jnp.where(is_small[:, None], values, 0.0), axis=0)
    return jnp.stack([large_part, small_part])


def general_shards(
    step_count,
    block_order,
    saved_tiles,
    pre_act,
    grad_output,
    pointwise_live,
    master_rows,
    row_moment,
    col_moment,
    next_tiles,
):
    pre_float = pre_act.astype(jnp.float32)
    activation = jax.nn.silu(pre_float).astype(jnp.bfloat16)
    grad_act = lax.dot_general(
        grad_output, pointwise_live, (((1,), (1,)), ((), ())), preferred_element_type=jnp.float32
    )
    grad_pre = (grad_act * silu_slope(pre_float)).astype(jnp.bfloat16)
    pieces = [contract_rows(view, grad_pre) for view in tap_views(saved_tiles[0])]
    pieces.append(contract_rows(activation, grad_output))
    own_term = jnp.concatenate(pieces, axis=0).astype(jnp.bfloat16)
    total_rows = NB * BLK
    stored = jnp.take(own_term.reshape(NB, BLK, CO), block_order, axis=0).reshape(total_rows, CO)
    own_rows = master_rows.shape[0]
    partial_value = lax.psum_scatter(stored, "shard", scatter_dimension=0, tiled=True).astype(
        jnp.float32
    )
    gradient = lax.psum(partial_value, "group")
    owner = lax.axis_index("shard")
    own_count = own_rows // BLK
    own_blocks = lax.dynamic_slice_in_dim(block_order, owner * own_count, own_count)
    is_small = jnp.repeat(own_blocks >= NB3, BLK, total_repeat_length=own_rows)
    decay_rate = 1.0 - step_count.astype(jnp.float32)[0] ** (-decay_power)
    counts = jnp.array([27 * CI, CO], jnp.float32)
    squares = gradient * gradient
    new_row = decay_rate * row_moment + (1.0 - decay_rate) * jnp.mean(squares, axis=1)
    col_part = kernel_sums(squares, is_small)
    row_part = kernel_sums(new_row[:, None], is_small)[:, 0]
    weighted = kernel_sums(squares / new_row[:, None], is_small)
    col_total, weight_total, row_total = lax.psum((col_part, weighted, row_part), "shard")
    new_col = decay_rate * col_moment + (1.0 - decay_rate) * col_total / counts[:, None]
    row_mean = row_total / counts
    col_rows = jnp.where(is_small[:, None], new_col[1], new_col[0])
    mean_rows = jnp.where(is_small, row_mean[1], row_mean[0])
    scaled = gradient / jnp.sqrt(new_row[:, None] * col_rows / mean_rows[:, None])
    square_total = row_mean * jnp.sum(weight_total / new_col, axis=1)
    clip_factor = jnp.maximum(1.0, jnp.sqrt(square_total / (counts * CO)))
    update_rows = scaled / jnp.where(is_small, clip_factor[1], clip_factor[0])[:, None]
    new_master = master_rows - learn_rate * update_rows
    weights_low = new_master.astype(jnp.bfloat16)
    gathered = lax.all_gather(weights_low, "shard", axis=0, tiled=True)
    inverse = jnp.zeros((NB,), jnp.int32).at[block_order].set(jnp.arange(NB, dtype=jnp.int32))
    natural = jnp.take(gathered.reshape(NB, BLK, CO), inverse, axis=0).reshape(total_rows, CO)
    spatial = natural[: 27 * CI].reshape(27, CI, CO)
    pointwise = natural[27 * CI :]
    hidden_sum = jnp.zeros((FR * HW * HW, CO), jnp.float32)
    for index_tap, view in enumerate(tap_views(next_tiles[0])):
        hidden_sum = hidden_sum + jnp.dot(
            view, spatial[index_tap], preferred_element_type=jnp.float32
        )
    hidden_act = jax.nn.silu(hidden_sum).astype(jnp.bfloat16)
    next_output = jnp.dot(hidden_act, pointwise, preferred_element_type=jnp.float32).astype(
        jnp.bfloat16
    )
    return (update_rows, new_master, new_row, new_col, next_output)


AXES = ("group", "shard")
SLOTS = 14
PIX = FR * HW * HW
SHIFTED = (FR + 2) * (HW + 2) * HW
SLOPES = 3 * SHIFTED
ACTS = SLOPES + PIX
BROUGHT = ACTS + PIX
LOW = jnp.bfloat16
WIDE = jnp.float32
VMEM = pl.BlockSpec(memory_space=pltpu.VMEM)
SMEM = pl.BlockSpec(memory_space=pltpu.SMEM)
HBM = pl.BlockSpec(memory_space=pl.ANY)
MASK_CORE, MASK_NEAR, MASK_FAR, MASK_X, MASK_Y = 1, 2, 4, 8, 16
PARTS = ((0, 10), (10, 4))
ORDERS = (((0, 1, 2), (1, 0, 2)), ((2, 0, 1), (2, 1, 0)))
MESSAGE = SLOTS
GATHERED = ((0, 10), (10, 5))
MASKS = (MASK_X, MASK_Y, MASK_NEAR)


def swap(value, mask):
    return lax.ppermute(value, AXES, [(at, at ^ mask) for at in range(32)])


def swap_mixed(value, masks):
    return lax.ppermute(value, AXES, [(at, at ^ masks[at & 1]) for at in range(32)])


def swap_part(value, part, step):
    return swap_mixed(value, [MASKS[ORDERS[part][core][step]] for core in range(2)])


def place_of(at, part, step):
    zero, one = (ORDERS[part][core][step] for core in range(2))
    return at[zero] if zero == one else jnp.where(at[4] == 0, at[zero], at[one])


def position():
    group, shard = lax.axis_index("group"), lax.axis_index("shard")
    return group % 2, group // 2, shard // 2 % 2, shard // 4, shard % 2


def call(kernel, outs, in_specs, out_specs=None, scratch=(), flops=0, moved=0, room=8, pin=True):
    return pl.pallas_call(
        lambda *refs: kernel(position(), *refs),
        out_shape=[(pltpu.VMEM if pin else jax.ShapeDtypeStruct)(*out) for out in outs],
        in_specs=in_specs,
        out_specs=out_specs or [VMEM] * len(outs),
        scratch_shapes=list(scratch),
        compiler_params=pltpu.CompilerParams(vmem_limit_bytes=room << 20),
        cost_estimate=pl.CostEstimate(flops=flops, bytes_accessed=moved, transcendentals=0),
    )


def far_away(array):
    return pltpu.with_memory_space_constraint(array, pltpu.HBM)


def store_shifted(tile, out):
    for col_off in range(3):
        out[col_off * SHIFTED : (col_off + 1) * SHIFTED] = tile[
            :, :, col_off : col_off + HW, :
        ].reshape(SHIFTED, CI)


def shift_kernel(at, tile, out):
    store_shifted(tile, out)


def store_factors_of(pre, grad, pointwise, out):
    values = pre[...].astype(WIDE)
    sigma = jax.nn.sigmoid(values)
    grad_act = lax.dot_general(
        grad[...], pointwise[...], (((1,), (1,)), ((), ())), preferred_element_type=WIDE
    )
    out[SLOPES:ACTS] = (grad_act * (sigma * (1.0 + values * (1.0 - sigma)))).astype(LOW)
    out[ACTS:] = (values * sigma).astype(LOW)


def view_start(tap, frame):
    frame_off, row_off, col_off = tap // 9, tap // 3 % 3, tap % 3
    return col_off * SHIFTED + ((frame + frame_off) * (HW + 2) + row_off) * HW


def core_start(core, slot, frame):
    return pl.multiple_of(
        jnp.where(core == 0, view_start(slot, frame), view_start(min(SLOTS + slot, 26), frame)), HW
    )


def fetch(pairs, arrived):
    copies = [
        pltpu.make_async_copy(source, target, arrived.at[index])
        for index, (source, target) in enumerate(pairs)
    ]
    for copy in copies:
        copy.start()
    return copies


def own_kernel(
    at, tile, pre_far, grad_far, pointwise_far, brought, grad, pointwise, pre, arrived
):
    copies = fetch(((pre_far, pre), (grad_far, grad), (pointwise_far, pointwise)), arrived)
    store_shifted(tile, brought)
    for copy in copies:
        copy.wait()
    store_factors_of(pre, grad, pointwise, brought)


def pack_kernel(at, after, master_far, row_moment_far, packed, master, row_moment, arrived):
    quarter = pl.multiple_of((at[1] * 2 + at[0]) * (SLOTS * 16), SLOTS * 16)
    row_moment[...] = jnp.zeros((16, 128), WIDE)
    copies = fetch(
        (
            (master_far.at[pl.ds(quarter, SLOTS * 16), :], master),
            (row_moment_far, row_moment.at[pl.ds(0, 7), :]),
        ),
        arrived,
    )
    for copy in copies:
        copy.wait()
    packed[:SLOTS] = master[...].astype(LOW).reshape(SLOTS, 16, CO)
    high = row_moment[...].astype(LOW).astype(WIDE)
    packed[SLOTS] = jnp.concatenate([high, row_moment[...] - high], axis=1).astype(LOW)


def term_kernel(
    at, own, tile_peer, pre_peer, grad_peer, grad, pointwise, keep, send_one, send_two, peer, rights
):
    core = at[4]
    store_shifted(tile_peer, peer)
    store_factors_of(pre_peer, grad_peer, pointwise, peer)
    rights[0, :PIX] = own[SLOPES:ACTS]
    rights[0, PIX:] = peer[SLOPES:ACTS]
    rights[1, :PIX] = grad[...]
    rights[1, PIX:] = grad_peer[...]
    for slot in range(SLOTS):
        pieces = []
        for ref in (own, peer):
            for frame in range(FR):
                start = core_start(core, slot, frame)
                if slot == SLOTS - 1:
                    start = jnp.where(core == 0, start, ACTS + frame * HW * HW)
                pieces.append(ref[pl.ds(pl.multiple_of(start, HW), HW * HW), :])
        right = rights[core] if slot == SLOTS - 1 else rights[0]
        total = contract_rows(jnp.concatenate(pieces, axis=0), right)
        for part, ((first, count), send) in enumerate(zip(PARTS, (send_one, send_two))):
            if first <= slot < first + count:
                low, high, at_low = total[:128], total[128:], place_of(at, part, 0) == 0
                keep[slot] = jnp.where(at_low, low, high).astype(LOW)
                send[slot - first] = jnp.where(at_low, high, low).astype(LOW)


def fold_kernel(step, at, *refs):
    size = 256 >> (step + 1)
    extra = 0 if step == 2 else 2
    own, got = refs[:extra] or (None, None)
    refs = refs[extra:]
    keep, gots, stay, sends = refs[0], refs[1:3], refs[3], refs[4:]
    for part, (first, count) in enumerate(PARTS):
        here = slice(first, first + count)
        if step == 3:
            stay[here] = keep[here] + gots[part][...]
            continue
        mine = place_of(at, part, step)
        for which, out in ((mine, 0), (1 - mine, 1)):
            rows = pl.ds(pl.multiple_of(which * size, size), size)
            value = keep[here, rows] + gots[part][:, rows]
            if out == 0:
                stay[here] = value
            else:
                sends[part][...] = value
    if step == 1:
        pair = sends[2]
        pair[at[3]] = own[...]
        pair[1 - at[3]] = got[...]
    if step == 3:
        line, moments = sends
        for which, piece in ((at[2], own), (1 - at[2], got)):
            for far in range(2):
                line[far * 2 + which] = piece[far, :SLOTS].reshape(SLOTS * 16, CO)
                moments[far * 2 + which] = piece[far, SLOTS]


def moment_kernel(
    at, rate, own, got, moments, line, line_one, line_two, scaled_one, scaled_two, lines,
):
    for index, piece in enumerate((line, line_one, line_two)):
        lines[index] = piece[...]
    count = SLOTS * BLK
    total = (own[...].astype(WIDE) + got[...].astype(WIDE)).reshape(count, CO)
    squares = total * total
    decay = rate[0]
    mean = jnp.sum(squares, axis=1, keepdims=True) * (1.0 / CO)
    row_moment = jnp.concatenate([moments[:, slot : slot + 1] for slot in range(SLOTS)], axis=0)
    new_row = decay * row_moment + (1.0 - decay) * mean
    value = (total * lax.rsqrt(new_row)).astype(LOW).reshape(SLOTS, BLK, CO)
    split = PARTS[0][1]
    scaled_one[...] = value[:split]
    scaled_two[: SLOTS - split] = value[split:]
    weighted = squares / new_row
    cut = count - BLK
    last_small = at[4] == 1
    rows = []
    for values in (squares, weighted, jnp.broadcast_to(new_row, (count, CO))):
        large = jnp.sum(values[:cut], axis=0, keepdims=True)
        last = jnp.sum(values[cut:], axis=0, keepdims=True)
        rows.append(large + jnp.where(last_small, 0.0, last))
        rows.append(jnp.where(last_small, last, 0.0))
    spread = jnp.broadcast_to(new_row, (count, 128))
    spread = jnp.concatenate([spread, jnp.zeros((512 - count, 128), WIDE)], axis=0)
    rows += [jnp.transpose(spread[:CO])[:1], jnp.transpose(spread[CO:])[:1]]
    message = jnp.concatenate(rows, axis=0)
    high = message.astype(LOW).astype(WIDE)
    message = jnp.concatenate([high, message - high, jnp.zeros((16, CO), WIDE)], axis=0)
    scaled_two[SLOTS - split] = message.astype(LOW)


def store_factors(total, decay, col_moment, new_col, factor):
    for kernel in range(2):
        count = 27.0 * CI if kernel == 0 else float(CO)
        col = decay * col_moment[kernel : kernel + 1] + (1.0 - decay) * (
            total[kernel : kernel + 1] / count
        )
        row_mean = total[4 + kernel : 5 + kernel] / count
        square = row_mean * jnp.sum(
            total[2 + kernel : 3 + kernel] / col, axis=1, keepdims=True
        )
        clip = jnp.maximum(1.0, jnp.sqrt(square / (count * CO)))
        new_col[kernel : kernel + 1] = col
        factor[kernel : kernel + 1] = 1.0 / (jnp.sqrt(col / row_mean) * clip)


def moments_kernel(at, block_order, mine, peer, out, plan, table, rows, inverse):
    core = at[4]
    owner = at[3] * 4 + at[2] * 2 + core

    def place_block(local, carry):
        block = block_order[owner * (NB // 8) + local]
        half = (block >= 8 * SLOTS).astype(jnp.int32)
        slot, place = (block - half * (8 * SLOTS)) // 8, lax.rem(block, 8)
        high, middle, low = place // 4, lax.rem(place // 2, 2), lax.rem(place, 2)
        other = low * 4 + high * 2 + middle
        sender = jnp.where(slot < PARTS[1][0], other, place)
        side = half ^ core
        plan[local * 8] = side
        plan[local * 8 + 1] = slot
        plan[local * 8 + 2] = place * BLK
        plan[local * 8 + 3] = (block >= NB3).astype(jnp.int32)
        plan[local * 8 + 4] = (side * 8 + sender) * 4 + slot // 4
        plan[local * 8 + 5] = lax.rem(128 + (lax.rem(local, 4) - lax.rem(slot, 4)) * BLK, 128)
        return carry

    lax.fori_loop(0, NB // 8, place_block, 0, unroll=4)
    for side, ref in enumerate((mine, peer)):
        for line in range(4):
            values = ref[line].astype(WIDE)
            values = values[:, :128] + values[:, 128:]
            table[pl.ds(pl.multiple_of((line * 2 + (core ^ side)) * 8, 8), 8), :] = values[:8]

    def invert(stored, carry):
        inverse[block_order[stored]] = stored
        return carry

    lax.fori_loop(0, NB, invert, 0, unroll=8)
    rows[...] = jnp.zeros((128, 128), WIDE)
    for part, (first, count) in enumerate(PARTS):
        place = place_of(at, part, 0) * 4 + place_of(at, part, 1) * 2 + place_of(at, part, 2)
        for slot in range(first, first + count):
            stored = inverse[(core * SLOTS + slot) * 8 + place]
            owner, local = stored // (NB // 8), lax.rem(stored, NB // 8)
            row = table[pl.ds(owner * 8 + local // 4, 1), :]
            turn = lax.rem(128 - lax.rem(local, 4) * BLK, 128)
            rows[slot : slot + 1] = pltpu.roll(row, turn, 1)
    out[...] = jnp.transpose(rows[...])[:BLK]


def order_kernel(at, block_order, mine, mine_low, mine_high, peer, peer_low, peer_high, out):
    count = NB // 8
    quarters = count // 4
    for flip_core, (pieces, low, high) in enumerate(
        ((mine, mine_low, mine_high), (peer, peer_low, peer_high))
    ):
        core = at[4] ^ flip_core
        for index in range(4):
            flip_x = jnp.where(core == 0, index // 2, index % 2)
            quarter = (at[1] ^ (index // 2) ^ (index % 2) ^ flip_x) * 2 + (at[0] ^ flip_x)
            for local in range(quarters):
                for line in range(4):
                    block = block_order[(line * 2 + core) * count + quarter * quarters + local]
                    to = pl.ds(pl.multiple_of(block * BLK, BLK), BLK)
                    rows = slice(local * BLK, local * BLK + BLK)
                    if index < 3:
                        out[to, :] = pieces[index, line, rows]
                    else:
                        out[to, :] = (low, high)[line // 2][line % 2, rows]


def widen_kernel(step, at, after, *refs):
    size = 256 >> (step + 1)
    ins, outs = refs[:4], refs[4:]
    if step == 1:
        outs[2][...], outs[3][...] = after[:2], after[2:]
    for part, (first, count) in enumerate(GATHERED):
        mine = place_of(at, part, step)
        for index, which in enumerate((mine, 1 - mine)):
            rows = pl.ds(pl.multiple_of(which * size, size), size)
            value = ins[2 * part + index][...]
            if step == 0:
                outs[0][first : first + count, rows] = value
            else:
                outs[part][:, rows] = value


def window(views, starts):
    return jnp.concatenate([views[pl.ds(start, HW * HW), :] for start in starts], axis=0)


def old_hidden_kernel(at, views, natural, hidden):
    total = jnp.zeros((PIX, CO), WIDE)
    for tap in range(27):
        weights = natural[tap * CI : tap * CI + CI]
        starts = [view_start(tap, frame) for frame in range(FR)]
        total = total + jnp.dot(window(views, starts), weights, preferred_element_type=WIDE)
    hidden[...] = total


def add_taps(views, scaled, core):
    total = jnp.zeros((PIX, CO), WIDE)
    for slot in range(SLOTS):
        starts = [core_start(core, slot, frame) for frame in range(FR)]
        weights = scaled[slot]
        if slot == SLOTS - 1:
            weights = jnp.where(core == 0, weights.astype(WIDE), 0.0).astype(LOW)
        total = total + jnp.dot(window(views, starts), weights, preferred_element_type=WIDE)
    return total


def half_hidden_kernel(at, views, scaled, hidden):
    hidden[...] = add_taps(views, scaled, at[4])


def finish_kernel(
    at, plan, rate, col_moment, views, natural, master, mine, peer, old, own_part,
    update_far, master_far, row_far, col_far, output_far,
    factor, row_table, update_rows, new_master, new_row, new_col, next_output, stored, rest_stored,
):
    core = at[4]
    sums = []
    for piece in (mine, peer):
        messages = [
            piece[MESSAGE, sender * BLK : sender * BLK + 16].astype(WIDE) for sender in range(8)
        ]
        sums.append([message[:8] + message[8:] for message in messages])
    total = sum(sums[0][1:] + sums[1], sums[0][0])
    store_factors(total, rate[0], col_moment, new_col, factor)

    def store(source, target, index):
        copy = pltpu.make_async_copy(source, target, rest_stored.at[index])
        copy.start()
        return [copy]

    copies = store(new_col, col_far, 0)

    for line in range(7):
        for local in range(line * 4, line * 4 + 4):
            side, slot, first, kernel = (plan[local * 8 + item] for item in range(4))
            rows = slice(local * BLK, local * BLK + BLK)
            there = pl.ds(pl.multiple_of(first, BLK), BLK)
            value = jnp.where(
                side == 0, mine[slot, there, :].astype(WIDE), peer[slot, there, :].astype(WIDE)
            )
            update = value * factor[pl.ds(kernel, 1), :]
            update_rows[rows, :] = update
            new_master[rows, :] = master[rows, :] - learn_rate * update
        there = pl.ds(line * 4 * BLK, 4 * BLK)
        pairs = ((update_rows, update_far), (new_master, master_far))
        copies += fetch(
            [(source.at[there, :], target.at[there, :]) for source, target in pairs],
            stored.at[line],
        )

    for side, messages in enumerate(sums):
        for sender in range(8):
            for line in range(4):
                to = (side * 8 + sender) * 4 + line
                row_table[to : to + 1] = messages[sender][
                    6 + line // 2 : 7 + line // 2, line % 2 * 128 : line % 2 * 128 + 128
                ]
    lane = lax.broadcasted_iota(jnp.int32, (1, 128), 1)
    for line in range(7):
        values = jnp.zeros((1, 128), WIDE)
        for part in range(4):
            from_row, turn = (plan[(line * 4 + part) * 8 + item] for item in (4, 5))
            here = (lane >= part * BLK) & (lane < part * BLK + BLK)
            turned = pltpu.roll(row_table[pl.ds(from_row, 1), :], turn, 1)
            values = jnp.where(here, turned, values)
        new_row[line : line + 1] = values
    copies += store(new_row, row_far, 2)

    change = own_part[...] + add_taps(views, peer, 1 - core)
    hidden = old[...] - (learn_rate * factor[0:1]) * change
    small = jnp.where(core == 1, mine[SLOTS - 1].astype(WIDE), peer[SLOTS - 1].astype(WIDE))
    weights = natural[27 * CI :].astype(WIDE) - small * (learn_rate * factor[1:2])
    next_output[...] = jnp.dot(
        jax.nn.silu(hidden).astype(LOW), weights.astype(LOW), preferred_element_type=WIDE
    ).astype(LOW)
    copies += store(next_output, output_far, 1)
    for copy in copies:
        copy.wait()


def shards(
    step_count,
    block_order,
    saved_tiles,
    pre_act,
    grad_output,
    pointwise_live,
    master_rows,
    row_moment,
    col_moment,
    next_tiles,
):
    decay_rate = 1.0 - step_count.astype(WIDE) ** (-decay_power)

    tile_peer = swap(saved_tiles, MASK_CORE)
    pre_peer = swap(pre_act, MASK_CORE)
    grad_peer = swap(grad_output, MASK_CORE)
    rows_far = [far_away(array) for array in (pre_act, grad_output, pointwise_live)]
    brought, grad_near, pointwise_near = call(
        own_kernel,
        [((BROUGHT, CI), LOW), ((PIX, CO), LOW), ((CO, CO), LOW)],
        [VMEM] + [HBM] * 3,
        scratch=[pltpu.VMEM((PIX, CO), LOW), pltpu.SemaphoreType.DMA((3,))],
        moved=4 << 20,
    )(saved_tiles[0], *rows_far)

    keep, *sends = call(
        term_kernel,
        [((SLOTS, 128, CO), LOW)] + [((count, 128, CO), LOW) for _, count in PARTS],
        [VMEM] * 6,
        scratch=[pltpu.VMEM((BROUGHT, CI), LOW), pltpu.VMEM((2, 2 * PIX, CO), LOW)],
        flops=2 * 14 * 1024 * 256 * 256,
        moved=6 << 20,
        room=12,
    )(brought, tile_peer[0], pre_peer, grad_peer, grad_near, pointwise_near)

    packed = call(
        pack_kernel,
        [((SLOTS + 1, 16, CO), LOW)],
        [HBM] * 3,
        scratch=[
            pltpu.VMEM((SLOTS * 16, CO), WIDE),
            pltpu.VMEM((16, 128), WIDE),
            pltpu.SemaphoreType.DMA((2,)),
        ],
    )(keep, far_away(master_rows), far_away(row_moment.reshape(7, 128)))[0]
    packed_far = swap(packed, MASK_FAR)
    views = call(shift_kernel, [((3 * SHIFTED, CI), LOW)], [VMEM], moved=3 << 20)(next_tiles[0])[0]

    for step in range(1, 4):
        gots = [swap_part(send, part, step - 1) for part, send in enumerate(sends)]
        size = 256 >> (step + 1)
        outs = [((SLOTS, size, CO), LOW)] + [((count, size, CO), LOW) for _, count in PARTS]
        if step == 1:
            extra = [packed, packed_far]
            outs = outs + [((2, SLOTS + 1, 16, CO), LOW)]
        elif step == 2:
            extra = []
        else:
            extra = [pair, pair_near]
            outs = [((SLOTS, BLK, CO), LOW), ((4, SLOTS * 16, CO), LOW), ((4, 16, CO), LOW)]
        keep, *sends = call(
            functools.partial(fold_kernel, step),
            outs,
            [VMEM] * (len(extra) + 3),
            moved=1 << 20,
        )(*extra, keep, *gots)
        if step == 1:
            pair = sends.pop()
            pair_near = swap(pair, MASK_NEAR)
    line, moments = sends
    line_one, line_two = swap_mixed(line, (MASK_Y, MASK_X)), swap_mixed(line, (MASK_X, MASK_Y))
    own_moment, plan = call(
        moments_kernel,
        [((BLK, 128), WIDE), ((NB,), jnp.int32)],
        [SMEM] + [VMEM] * 2,
        out_specs=[VMEM, SMEM],
        pin=False,
        scratch=[
            pltpu.VMEM((64, 128), WIDE),
            pltpu.VMEM((128, 128), WIDE),
            pltpu.SMEM((NB,), jnp.int32),
        ],
    )(block_order, moments, swap(moments, MASK_CORE))
    *scaled, lines = call(
        moment_kernel,
        [((count, BLK, CO), LOW) for _, count in GATHERED] + [((3, 4, SLOTS * 16, CO), LOW)],
        [SMEM] + [VMEM] * 6,
        moved=2 << 20,
    )(decay_rate, keep, swap(keep, MASK_FAR), own_moment, line, line_one, line_two)
    line_far = swap_mixed(line_one, (MASK_X, MASK_Y))
    joined, natural = scaled, None
    for step in range(2, -1, -1):
        pieces = []
        for part, value in enumerate(joined):
            pieces += [value, swap_part(value, part, step)]
        size = 256 >> step
        outs = [((count, size, CO), LOW) for _, count in GATHERED]
        if step == 0:
            outs = [((SLOTS + 1, size, CO), LOW)]
        if step == 1:
            outs = outs + [((2, SLOTS * 16, CO), LOW)] * 2
        joined = call(
            functools.partial(widen_kernel, step),
            outs,
            [VMEM if step == 1 else HBM] + [VMEM] * len(pieces),
        )((natural, line_far, views)[step], *pieces)
        if step == 1:
            parts = [lines, *joined[2:]]
            joined = joined[:2]
            natural = call(
                order_kernel, [((NB * BLK, CO), LOW)], [SMEM] + [VMEM] * 6, moved=8 << 20
            )(block_order, *parts, *[swap(part, MASK_CORE) for part in parts])[0]
    mine = joined[0]
    peer = swap(mine, MASK_CORE)
    old = call(
        old_hidden_kernel,
        [((PIX, CO), WIDE)],
        [VMEM] * 2,
        flops=2 * 27 * 512 * 256 * 256,
        moved=6 << 20,
    )(views, natural)[0]
    half = call(
        half_hidden_kernel,
        [((PIX, CO), WIDE)],
        [VMEM] * 2,
        flops=2 * 14 * 512 * 256 * 256,
        moved=4 << 20,
    )(views, mine)[0]

    outs = [
        ((NB // 8 * BLK, CO), WIDE),
        ((NB // 8 * BLK, CO), WIDE),
        ((7, 128), WIDE),
        ((2, CO), WIDE),
        ((PIX, CO), LOW),
    ]
    update_rows, new_master, new_row, new_col, next_output = call(
        finish_kernel,
        outs,
        [SMEM] * 2 + [VMEM] * 8,
        out_specs=[HBM] * 5,
        scratch=[
            pltpu.VMEM((2, CO), WIDE),
            pltpu.VMEM((64, 128), WIDE),
            pltpu.VMEM((NB // 8 * BLK, CO), WIDE),
            pltpu.VMEM((NB // 8 * BLK, CO), WIDE),
            pltpu.VMEM((7, 128), WIDE),
            pltpu.VMEM((2, CO), WIDE),
            pltpu.VMEM((PIX, CO), LOW),
            pltpu.SemaphoreType.DMA((7, 2)),
            pltpu.SemaphoreType.DMA((3,)),
        ],
        pin=False,
        flops=2 * 16 * 512 * 256 * 256,
        moved=16 << 20,
        room=16,
    )(plan, decay_rate, col_moment, views, natural, master_rows, mine, peer, old, half)
    return (update_rows, new_master, new_row.reshape(-1), new_col, next_output)


def solution(mesh):
    in_specs = (
        P(),
        P(),
        P(("group", "shard"), None, None, None, None),
        P(("group", "shard"), None),
        P(("group", "shard"), None),
        P(),
        P("shard", None),
        P("shard"),
        P(),
        P(("group", "shard"), None, None, None, None),
    )
    out_specs = (P("shard", None), P("shard", None), P("shard"), P(), P(("group", "shard"), None))
    body = shards if (mesh.shape["group"], mesh.shape["shard"]) == (4, 8) else general_shards
    return jax.shard_map(body, mesh=mesh, in_specs=in_specs, out_specs=out_specs, check_vma=False)
```
